128 devices in a mesh: dp: 8 (over x, core), ctx: 16 (over z, y).
Axes of the slice: x: 4, y: 4, z: 4, core: 2. Of those that a mesh axis runs over, the one named last changes fastest.
Arguments:
- tokens: bfloat16 [32768, 512], P(('dp', 'ctx')), may hold values from -6 to 6
- cotangent: bfloat16 [32768, 512], P(('dp', 'ctx')), may hold values from -6 to 6
- lengths: int32 [8, 2], P('dp'), may hold values from 1 to 4095, as said below
- w_qkv: float32 [512, 1536], P(None, 'ctx'), may hold values from -0.25 to 0.25
- w_proj: float32 [512, 512], P(None, 'ctx'), may hold values from -6 to 6
- w_up: float32 [512, 2048], P(None, 'ctx'), may hold values from -0.25 to 0.25
- w_down: float32 [2048, 512], P('ctx'), may hold values from -0.125 to 0.125
- w_small: float32 [12, 512], P(None, 'ctx'), may hold values from -1.2 to 1.6
- mean_qkv: float32 [512, 1536], P(None, 'ctx'), may hold values from -128 to 128
- mean_proj: float32 [512, 512], P(None, 'ctx'), may hold values from -6 to 6
- mean_up: float32 [512, 2048], P(None, 'ctx'), may hold values from -32 to 32
- mean_down: float32 [2048, 512], P('ctx'), may hold values from -64 to 64
- mean_small: float32 [12, 512], P(None, 'ctx'), may hold values from -128 to 128
- square_qkv: float32 [512, 1536], P(None, 'ctx'), may hold values from 851.968 to 13762.56
- square_proj: float32 [512, 512], P(None, 'ctx'), may hold values from 8.51968 to 137.6256
- square_up: float32 [512, 2048], P(None, 'ctx'), may hold values from 78.6432 to 1245.184
- square_down: float32 [2048, 512], P('ctx'), may hold values from 311.296 to 4915.2
- square_small: float32 [12, 512], P(None, 'ctx'), may hold values from 851.968 to 13762.56
Outputs:
- out: bfloat16 [32768, 512], P(('dp', 'ctx'))
- grad_in: bfloat16 [32768, 512], P(('dp', 'ctx'))
- new_qkv: float32 [512, 1536], P(None, 'ctx')
- new_proj: float32 [512, 512], P(None, 'ctx')
- new_up: float32 [512, 2048], P(None, 'ctx')
- new_down: float32 [2048, 512], P('ctx')
- new_small: float32 [12, 512], P(None, 'ctx')
- new_mean_qkv: float32 [512, 1536], P(None, 'ctx')
- new_mean_proj: float32 [512, 512], P(None, 'ctx')
- new_mean_up: float32 [512, 2048], P(None, 'ctx')
- new_mean_down: float32 [2048, 512], P('ctx')
- new_mean_small: float32 [12, 512], P(None, 'ctx')
- new_square_qkv: float32 [512, 1536], P(None, 'ctx')
- new_square_proj: float32 [512, 512], P(None, 'ctx')
- new_square_up: float32 [512, 2048], P(None, 'ctx')
- new_square_down: float32 [2048, 512], P('ctx')
- new_square_small: float32 [12, 512], P(None, 'ctx')
The draws below stay inside these ranges and needn't reach their ends.
Inputs may be any that keep to these rules, and one draw needn't show every extreme that they name: `lengths`: in each group's row one length is at least 3841 and the other is under 256; the two sum to at most 4096; the longer may stand first or second.
All inputs are finite; a program needn't handle non-finite values.
Results may differ from the reference program's by a relative error of at most 0.03.
Values may be sent and summed in bfloat16 or wider, within the bound.
No kernel may reach another device: no remote copies, remote signals or barrier semaphores. Data moves between devices by JAX's collectives and lax.ppermute only.
A program may use at most 128 MiB of HBM per device.

```python
import math
import jax
import jax.numpy as jnp
from jax import lax

D = 512
HEADS = 8
HEAD_DIM = 64
FF = 2048
STEP = 10
GROUP_TOK = 4096
DEV_ROWS = 256
GROUPS = 8
ROWS_ALL = 32768
SMALL_ROWS = 12


def draw_lengths(key, part):
    key = jax.random.fold_in(key, 3)
    short_key, long_key, order_key, pick_key = jax.random.split(key, 4)
    short_len = jax.random.randint(short_key, (GROUPS,), 1, DEV_ROWS)
    long_len = jax.random.randint(long_key, (GROUPS,), GROUP_TOK - DEV_ROWS + 1, GROUP_TOK - short_len + 1)
    chosen = jax.random.randint(pick_key, (), 0, GROUPS)
    marked = jnp.arange(GROUPS) == chosen
    short_len = jnp.where(marked, 1, short_len)
    long_len = jnp.where(marked, GROUP_TOK - 1, long_len)
    order = jax.random.randint(order_key, (GROUPS,), 0, 2)
    first_len = jnp.where(order == 1, long_len, short_len)
    second_len = jnp.where(order == 1, short_len, long_len)
    return jnp.stack([first_len, second_len], axis=1).astype(jnp.int32)


def draw_w_small(key, part):
    key = jax.random.fold_in(key, 5)
    noise = jnp.clip(jax.random.normal(key, (SMALL_ROWS, D), jnp.float32), -4.0, 4.0)
    row_index = jnp.arange(SMALL_ROWS)[:, None]
    is_gain = (row_index == 0) | (row_index == 5)
    return jnp.where(is_gain, 1.0 + 0.15 * noise, 0.3 * noise).astype(jnp.float32)


def block_levels(stream_key, extent, cuts, smallest, top_value):
    def one(axis_at, parts):
        steps = jax.random.uniform(jax.random.fold_in(jax.random.fold_in(stream_key, 6), axis_at), (parts,), jnp.float32, smallest / len(cuts), top_value / len(cuts))
        return jnp.repeat(jnp.exp(steps), extent[axis_at] // parts).reshape((-1,) + (1,) * (len(extent) - axis_at - 1))

    gain = one(*cuts[0])
    for cut in cuts[1:]:
        gain = gain * one(*cut)
    return gain


def scatter_about(rng, shape, width, most, pieces=(), kind=jnp.bfloat16):
    factor_of = block_levels(rng, shape, pieces, -0.22, 0.18) if pieces else 1.0
    array = jax.random.normal(rng, shape, jnp.float32) * width * factor_of
    return jnp.minimum(jnp.maximum(array, -most), most).astype(kind)


def setup_inputs(seed: int = 0) -> dict:
    key_of = jax.random.split(jax.random.key(seed), 19)
    return {
        "tokens": scatter_about(key_of[0], (ROWS_ALL, D), 1.0, 6.0, ((0, 128),)),
        "cotangent": scatter_about(key_of[1], (ROWS_ALL, D), 1.0, 6.0, ((0, 128),)),
        "lengths": draw_lengths(jax.random.fold_in(key_of[18], 71), 0),
        "w_qkv": scatter_about(key_of[3], (D, 3 * D), D ** -0.5, 0.25, ((1, 16),), jnp.float32),
        "w_proj": scatter_about(key_of[4], (D, D), (max(4 * D // GROUP_TOK, 1)) ** -0.5, 6.0, ((1, 16),), jnp.float32),
        "w_up": scatter_about(key_of[5], (D, FF), D ** -0.5, 0.25, ((1, 16),), jnp.float32),
        "w_down": scatter_about(key_of[6], (FF, D), FF ** -0.5, 0.125, ((0, 16),), jnp.float32),
        "w_small": draw_w_small(jax.random.fold_in(key_of[18], 71), 0),
        "mean_qkv": scatter_about(key_of[8], (D, 3 * D), (0.11 * (GROUPS * GROUP_TOK) ** 0.5), 128.0, ((1, 16),), jnp.float32),
        "mean_proj": scatter_about(key_of[9], (D, D), (0.011 * (GROUPS * GROUP_TOK) ** 0.5), 6.0, ((1, 16),), jnp.float32),
        "mean_up": scatter_about(key_of[10], (D, FF), (0.033 * (GROUPS * GROUP_TOK) ** 0.5), 32.0, ((1, 16),), jnp.float32),
        "mean_down": scatter_about(key_of[11], (FF, D), (0.066 * (GROUPS * GROUP_TOK) ** 0.5), 64.0, ((0, 16),), jnp.float32),
        "mean_small": scatter_about(key_of[12], (SMALL_ROWS, D), (0.11 * (GROUPS * GROUP_TOK) ** 0.5), 128.0, ((1, 16),), jnp.float32),
        "square_qkv": jnp.clip(jnp.exp(math.log(13762.56) - 2.7821581 * jax.random.uniform(key_of[13], (D, 3 * D), jnp.float32) ** block_levels(key_of[13], (D, 3 * D), ((1, 16),), -0.2, 0.2)), 851.968, 13762.56),
        "square_proj": jnp.clip(jnp.exp(math.log(137.6256) - 2.7821581 * jax.random.uniform(key_of[14], (D, D), jnp.float32) ** block_levels(key_of[14], (D, D), ((1, 16),), -0.2, 0.2)), 8.51968, 137.6256),
        "square_up": jnp.clip(jnp.exp(math.log(1245.184) - 2.7621173 * jax.random.uniform(key_of[15], (D, FF), jnp.float32) ** block_levels(key_of[15], (D, FF), ((1, 16),), -0.2, 0.2)), 78.6432, 1245.184),
        "square_down": jnp.clip(jnp.exp(math.log(4915.2) - 2.7593436 * jax.random.uniform(key_of[16], (FF, D), jnp.float32) ** block_levels(key_of[16], (FF, D), ((0, 16),), -0.2, 0.2)), 311.296, 4915.2),
        "square_small": jnp.clip(jnp.exp(math.log(13762.56) - 2.7821581 * jax.random.uniform(key_of[17], (SMALL_ROWS, D), jnp.float32) ** block_levels(key_of[17], (SMALL_ROWS, D), ((1, 16),), -0.2, 0.2)), 851.968, 13762.56),
    }


@jax.custom_vjp
def low(v):
    return lax.optimization_barrier(v.astype(jnp.bfloat16)).astype(jnp.float32)

@jax.custom_vjp
def low_back(v):
    return v

def low_keep(v):
    return (low(v), None)

def low_pass(kept, grad):
    return (grad,)

def back_keep(v):
    return (v, None)

def back_low(kept, grad):
    return (low(grad),)
low.defvjp(low_keep, low_pass)
low_back.defvjp(back_keep, back_low)
epsilon = 1e-05
beta_first = 0.9
beta_second = 0.95
adam_epsilon = 1e-08
weight_decay = 0.1
step_rates = (0.04, 1.0, 0.04, 0.02, 2.0)
decay_flags = (1.0, 1.0, 1.0, 1.0, 0.0)
highest = lax.Precision.HIGHEST

def layer_norm(values, gain_row, bias_row):
    center = values - lax.optimization_barrier(jnp.mean(values, axis=-1, keepdims=True))
    spread = lax.optimization_barrier(jnp.mean(center * center, axis=-1, keepdims=True))
    return center * lax.rsqrt(spread + epsilon) * gain_row + bias_row

def matmul(left_side, right_side):
    return jnp.dot(left_side, right_side, precision=highest, preferred_element_type=jnp.float32)

def doc_ids(positions, lens_row):
    return (positions >= lens_row[0]).astype(jnp.int32) + (positions >= lens_row[0] + lens_row[1]).astype(jnp.int32)

def group_forward(inputs, w_qkv, w_proj, w_up, w_down, packed, lens_row):
    model_width = inputs.shape[1]
    group_rows = inputs.shape[0]
    packed = low(packed)
    gain_one = packed[0]
    bias_one = packed[1]
    bias_query = packed[2]
    bias_value = packed[3]
    bias_proj = packed[4]
    gain_two = packed[5]
    bias_two = packed[6]
    bias_down = packed[7]
    bias_up = packed[8:].reshape(-1)
    normed = low(layer_norm(inputs, gain_one, bias_one))
    mixed_qkv = matmul(normed, low(w_qkv))
    queries = low_back(low(mixed_qkv[:, :model_width] + bias_query))
    key_rows = low_back(low(mixed_qkv[:, model_width:2 * model_width]))
    value_rows = low_back(low(mixed_qkv[:, 2 * model_width:] + bias_value))
    rows_all = jnp.arange(group_rows, dtype=jnp.int32)
    docs_all = doc_ids(rows_all, lens_row)
    block_rows = 512 if group_rows % 512 == 0 else group_rows
    key_heads = key_rows.reshape(group_rows, HEADS, HEAD_DIM)
    value_heads = value_rows.reshape(group_rows, HEADS, HEAD_DIM)

    def attend(first_row):
        query_block = lax.dynamic_slice_in_dim(queries, first_row, block_rows, 0).reshape(block_rows, HEADS, HEAD_DIM)
        query_pos = first_row + jnp.arange(block_rows, dtype=jnp.int32)
        raw_scores = jnp.einsum('qhd,khd->hqk', query_block, key_heads, precision=highest)
        scores = low_back(raw_scores) * HEAD_DIM ** (-0.5)
        allowed = (doc_ids(query_pos, lens_row)[:, None] == docs_all[None, :]) & (rows_all[None, :] <= query_pos[:, None])
        scores = jnp.where(allowed[None], scores, -jnp.inf)
        attn_probs = low(jax.nn.softmax(scores, axis=-1))
        mixed_rows = jnp.einsum('hqk,khd->qhd', attn_probs, value_heads, precision=highest)
        return mixed_rows.reshape(block_rows, model_width)
    starts = jnp.arange(group_rows // block_rows, dtype=jnp.int32) * block_rows
    attended = lax.map(jax.checkpoint(attend), starts).reshape(group_rows, model_width)
    attended = low_back(low(attended))
    residual = inputs + low_back(matmul(attended, low(w_proj))) + bias_proj
    normed_two = low(layer_norm(residual, gain_two, bias_two))
    hidden = low_back(matmul(normed_two, low(w_up))) + bias_up
    activated = low(jax.nn.gelu(hidden, approximate=True))
    branch = low_back(matmul(activated, low(w_down))) + bias_down
    return residual + branch

def adam_update(weight, grad_sum, mean_old, square_old, step_rate, decay_on):
    mean_new = beta_first * mean_old + (1.0 - beta_first) * grad_sum
    square_new = beta_second * square_old + (1.0 - beta_second) * grad_sum * grad_sum
    mean_hat = mean_new / (1.0 - beta_first ** STEP)
    square_hat = square_new / (1.0 - beta_second ** STEP)
    weight_new = weight - step_rate * (mean_hat / (jnp.sqrt(square_hat) + adam_epsilon) + decay_on * weight_decay * weight)
    return (weight_new, mean_new, square_new)

def reference(tokens, cotangent, lengths, w_qkv, w_proj, w_up, w_down, w_small, mean_qkv, mean_proj, mean_up, mean_down, mean_small, square_qkv, square_proj, square_up, square_down, square_small):
    weights = (w_qkv, w_proj, w_up, w_down, w_small)
    model_width = tokens.shape[1]
    inputs = tokens.astype(jnp.float32).reshape(GROUPS, GROUP_TOK, model_width)
    back_rows = cotangent.astype(jnp.float32).reshape(GROUPS, GROUP_TOK, model_width)

    def one_group(totals, group_item):
        group_in, group_back, lens_row = group_item
        live_rows = (jnp.arange(GROUP_TOK, dtype=jnp.int32) < lens_row[0] + lens_row[1]).astype(jnp.float32)
        output, pull_back = jax.vjp(lambda values, *params: group_forward(values, *params, lens_row), group_in, *weights)
        grad_list = pull_back(group_back * live_rows[:, None])
        totals = tuple((running + grad_part for running, grad_part in zip(totals, grad_list[1:])))
        return (totals, (output.astype(jnp.bfloat16), grad_list[0].astype(jnp.bfloat16)))
    zero_grads = tuple((jnp.zeros(weight.shape, jnp.float32) for weight in weights))
    totals, (outputs, grad_rows) = lax.scan(one_group, zero_grads, (inputs, back_rows, lengths))
    means = (mean_qkv, mean_proj, mean_up, mean_down, mean_small)
    squares = (square_qkv, square_proj, square_up, square_down, square_small)
    results = [adam_update(weights[which], totals[which], means[which], squares[which], step_rates[which], decay_flags[which]) for which in range(5)]
    return (outputs.reshape(-1, model_width), grad_rows.reshape(-1, model_width), results[0][0], results[1][0], results[2][0], results[3][0], results[4][0], results[0][1], results[1][1], results[2][1], results[3][1], results[4][1], results[0][2], results[1][2], results[2][2], results[3][2], results[4][2])
```

```python
import functools
import jax
import jax.numpy as jnp
from jax import lax
from jax.experimental import pallas as pl
from jax.experimental.pallas import tpu as pltpu
from jax.sharding import Mesh, PartitionSpec as P

HEADS = 8
HEAD_DIM = 64
STEP = 10
WIDTH = 512
HIDDEN = 2048
ROWS = 256
CHUNK = 512
TILE = 512

epsilon = 1e-05
negative_big = -1e30
beta_first = 0.9
beta_second = 0.95
adam_epsilon = 1e-08
weight_decay = 0.1
gelu_scale = 0.7978845608028654
gelu_cubic = 0.044715
log2_e = 1.4426950408889634

NN = (((1,), (0,)), ((), ()))
NT = (((1,), (1,)), ((), ()))
TN = (((0,), (0,)), ((), ()))
CTX = ("z", "y")


def dot(left, right, dims):
    return lax.dot_general(left, right, dims, preferred_element_type=jnp.float32)


def bfloat(values):
    return values.astype(jnp.bfloat16)


def f32(values):
    return values.astype(jnp.float32)


def normed(values):
    center = values - jnp.mean(values, axis=-1, keepdims=True)
    spread = jnp.mean(center * center, axis=-1, keepdims=True)
    scale = lax.rsqrt(spread + epsilon)
    return center * scale, scale


def norm_back(unit, scale, gain, grad):
    scaled = grad * gain
    first = jnp.mean(scaled, axis=-1, keepdims=True)
    second = jnp.mean(scaled * unit, axis=-1, keepdims=True)
    grad_values = (scaled - first - unit * second) * scale
    grad_gain = jnp.sum(grad * unit, axis=0, keepdims=True)
    grad_bias = jnp.sum(grad, axis=0, keepdims=True)
    return grad_values, grad_gain, grad_bias


def low_lanes(shape):
    return lax.broadcasted_iota(jnp.int32, shape, 1) < HEAD_DIM


def pair_pack(top, bottom):
    low = low_lanes(top.shape)
    first = jnp.where(low, top, pltpu.roll(bottom, HEAD_DIM, 1))
    second = jnp.where(low, pltpu.roll(top, HEAD_DIM, 1), bottom)
    return first, second


def qkv_kernel(tokens, wide, send, weights, small):
    for owner in range(16):
        for piece in range(3):
            first = owner * 96 + piece * 32
            part, offset = divmod(first, 512)
            if part == 0:
                target = first
            else:
                head, inside = divmod(offset, HEAD_DIM)
                target = 512 + head * 128 + (part - 1) * HEAD_DIM + inside
            half, row = divmod(piece * 32, 64)
            weights[target : target + 32, :] = wide[half, owner, row : row + 32, :]
    lane = lax.broadcasted_iota(jnp.int32, (16, 128), 1)
    for block in range(4):
        total = jnp.zeros((16, 128), jnp.float32)
        for inside in range(4):
            piece = f32(wide[1, block * 4 + inside, 32:48, 0:128])
            moved = pltpu.roll(piece, inside * 32, 1) if inside else piece
            keep = (lane >= inside * 32) & (lane < inside * 32 + 32)
            total = jnp.where(keep, moved, total)
        small[:, block * 128 : block * 128 + 128] = total
    unit, _ = normed(f32(tokens[...]))
    hidden = bfloat(unit * small[0:1, :] + small[1:2, :])
    for pair in range(4):
        columns = slice(pair * 128, pair * 128 + 128)
        query = dot(hidden, weights[columns, :], NT) + small[2:3, columns]
        query = f32(bfloat(query)) * HEAD_DIM**-0.5
        first, second = pair_pack(query[0:128], query[128:256])
        for offset, block in ((0, first), (1, second)):
            head = pair * 2 + offset
            send[2 * head, 256:384, :] = bfloat(block)
            send[2 * head + 1, 256:384, :] = bfloat(block)
    for head in range(HEADS):
        rows = slice(512 + head * 128, 512 + head * 128 + 128)
        bias = small[3:4, (head // 2) * 128 : (head // 2) * 128 + 128]
        if head % 2 == 0:
            bias = pltpu.roll(jnp.broadcast_to(bias, (8, 128)), HEAD_DIM, 1)[0:1]
        bias = jnp.where(low_lanes((1, 128)), 0.0, bias)
        both = bfloat(dot(hidden, weights[rows, :], NT) + bias)
        send[2 * head, 0:256, :] = both
        send[2 * head + 1, 0:256, :] = both


def block_of(step, half):
    return 2 * step + ((step & 1) ^ half)


def doc_start(position, first_end, second_end):
    return jnp.where(
        position >= second_end, second_end, jnp.where(position >= first_end, first_end, 0)
    )


def packed_t(block):
    turned = block.T
    return jnp.concatenate([turned[0:HEAD_DIM], turned[HEAD_DIM:128]], axis=1)


def chunk_loops(step, block, first_end, second_end, body, state):
    first_row = block * ROWS
    low = doc_start(first_row, first_end, second_end) // CHUNK
    last_start = doc_start(first_row + ROWS - 1, first_end, second_end)
    edge = jnp.minimum(step, (last_start + CHUNK - 1) // CHUNK)
    edge = jnp.maximum(edge, low)
    masked_count = edge - low + 1

    def masked_body(index, state):
        chunk = jnp.where(index == 0, step, low + index - 1)
        return body(chunk, True, state)

    state = lax.fori_loop(0, masked_count, masked_body, state)
    return lax.fori_loop(edge, step, lambda chunk, state: body(chunk, False, state), state)


def allowed_mask(chunk, block, first_end, second_end):
    key = lax.broadcasted_iota(jnp.int32, (CHUNK, ROWS), 0) + chunk * CHUNK
    position = lax.broadcasted_iota(jnp.int32, (1, ROWS), 1) + block * ROWS
    start = doc_start(position, first_end, second_end)
    return (key <= position) & (key >= start)


def attend_kernel(scalars, pieces, send, turned_out, out_t, stats, ones_t):
    half, first_end, second_end = scalars[1], scalars[3], scalars[4]

    def turn(source, _):
        columns = pl.ds(pl.multiple_of(source * ROWS, ROWS), ROWS)
        turned = f32(pieces[source, 0:256, :]).T
        turned_out[:, columns] = bfloat(turned)
        row = lax.broadcasted_iota(jnp.int32, (128, ROWS), 0)
        ones_t[:, columns] = bfloat(jnp.where(row < HEAD_DIM, 1.0, turned))
        send[source] = jnp.zeros((128, 128), jnp.bfloat16)
        return 0

    lax.fori_loop(0, 16, turn, 0)

    def one_block(step, _):
        block = block_of(step, half)
        query_t = packed_t(f32(pieces[block, 256:384, :]))
        query_t = bfloat(jnp.concatenate([query_t, jnp.zeros_like(query_t)], axis=0))

        def body(chunk, masked, state):
            run_max, total = state
            keys = pieces[pl.ds(chunk * 2, 2), 0:256, :].reshape(CHUNK, 128)
            scores = dot(keys, query_t, NN)
            if masked:
                scores = jnp.where(
                    allowed_mask(chunk, block, first_end, second_end), scores, negative_big
                )
            new_max = jnp.maximum(run_max, jnp.max(scores, axis=0, keepdims=True))
            weights = bfloat(jnp.exp2((scores - new_max) * log2_e))
            scale = jnp.exp2((run_max - new_max) * log2_e)
            columns = pl.ds(pl.multiple_of(chunk * CHUNK, CHUNK), CHUNK)
            total = total * scale + dot(ones_t[:, columns], weights, NN)
            return new_max, total

        state = (
            jnp.full((1, ROWS), negative_big, jnp.float32),
            jnp.zeros((128, ROWS), jnp.float32),
        )
        run_max, total = chunk_loops(step, block, first_end, second_end, body, state)
        row_sum = total[0:1]
        result = total[HEAD_DIM:128] / row_sum
        out_t[step] = result
        stats[step] = jnp.broadcast_to(run_max + jnp.log(row_sum), (8, ROWS))
        packed = jnp.concatenate([result[:, 0:128], result[:, 128:256]], axis=0).T
        send[block] = bfloat(packed)
        return 0

    lax.fori_loop(0, 8, one_block, 0)


def attend_back_kernel(scalars, pieces, turned, out_t, stats, grads, send, total):
    half, first_end, second_end = scalars[1], scalars[3], scalars[4]

    def clear(source, _):
        rows = pl.ds(pl.multiple_of(source * ROWS, ROWS), ROWS)
        total[rows, :] = jnp.zeros((ROWS, 128), jnp.float32)
        send[source, 256:384, :] = jnp.zeros((128, 128), jnp.bfloat16)
        return 0

    lax.fori_loop(0, 16, clear, 0)

    def one_block(step, _):
        block = block_of(step, half)
        low = low_lanes((128, 128))
        query = f32(pieces[block, 256:384, :])
        query_t = packed_t(query)
        query_t = bfloat(jnp.concatenate([query_t, jnp.zeros_like(query_t)], axis=0))
        query = bfloat(
            jnp.concatenate(
                [jnp.where(low, query, 0.0), jnp.where(low, pltpu.roll(query, HEAD_DIM, 1), 0.0)],
                axis=0,
            )
        )
        grad = f32(grads[block])
        grad_t = packed_t(grad)
        dots = jnp.sum(grad_t * out_t[step], axis=0, keepdims=True)
        grad_t = bfloat(jnp.concatenate([jnp.zeros_like(grad_t), grad_t], axis=0))
        grad = bfloat(
            jnp.concatenate(
                [jnp.where(low, 0.0, pltpu.roll(grad, HEAD_DIM, 1)), jnp.where(low, 0.0, grad)],
                axis=0,
            )
        )
        stat = stats[step][0:1]

        def body(chunk, masked, grad_query_t):
            keys = pieces[pl.ds(chunk * 2, 2), 0:256, :].reshape(CHUNK, 128)
            scores = dot(keys, query_t, NN)
            weights = jnp.exp2((scores - stat) * log2_e)
            if masked:
                weights = jnp.where(
                    allowed_mask(chunk, block, first_end, second_end), weights, 0.0
                )
            grad_weights = dot(keys, grad_t, NN)
            grad_scores = bfloat(weights * (grad_weights - dots))
            rows = pl.ds(pl.multiple_of(chunk * CHUNK, CHUNK), CHUNK)
            total[rows, :] += dot(grad_scores, query, NN) + dot(bfloat(weights), grad, NN)
            return grad_query_t + dot(turned[:, rows], grad_scores, NN)

        grad_query_t = chunk_loops(
            step, block, first_end, second_end, body, jnp.zeros((128, ROWS), jnp.float32)
        )
        grad_query_t = grad_query_t[0:HEAD_DIM] * HEAD_DIM**-0.5
        packed = jnp.concatenate([grad_query_t[:, 0:128], grad_query_t[:, 128:256]], axis=0).T
        send[block, 256:384, :] = bfloat(packed)
        return 0

    lax.fori_loop(0, 8, one_block, 0)

    def emit(source, _):
        rows = pl.ds(pl.multiple_of(source * ROWS, ROWS), ROWS)
        send[source, 0:256, :] = bfloat(total[rows, :])
        return 0

    lax.fori_loop(0, 16, emit, 0)


def middle_kernel(
    scalars, attended_in, tokens, cotangent, w_proj, w_up, w_down, small,
    out, send, grad_resid_out, grads, grad_small,
):
    first_row, mine, second_end = scalars[0] * ROWS, scalars[2], scalars[4]
    blocks = []
    for pair in range(4):
        top, bottom = pair_pack(
            f32(attended_in[4 * pair + mine]), f32(attended_in[4 * pair + 2 + mine])
        )
        blocks.append(jnp.concatenate([top, bottom], axis=0))
    attended = bfloat(jnp.concatenate(blocks, axis=1))
    residual = f32(tokens[...]) + dot(attended, w_proj[...], NT) + small[4:5, :]
    unit, scale = normed(residual)
    hidden_in = bfloat(unit * small[5:6, :] + small[6:7, :])
    position = lax.broadcasted_iota(jnp.int32, (ROWS, 1), 0) + first_row
    grad_out = jnp.where(position < second_end, f32(cotangent[...]), 0.0)
    grad_out_b = bfloat(grad_out)

    def one_tile(tile, state):
        branch, grad_hidden_in = state
        rows = pl.ds(pl.multiple_of(tile * TILE, TILE), TILE)
        up_rows = w_up[rows, :]
        down_rows = w_down[rows, :]
        hidden = dot(hidden_in, up_rows, NT) + small[pl.ds(8 + tile, 1), :]
        square = hidden * hidden
        bend = jnp.tanh(gelu_scale * hidden * (1.0 + gelu_cubic * square))
        half_open = 0.5 * (1.0 + bend)
        activated = bfloat(hidden * half_open)
        slope = half_open + 0.5 * hidden * (1.0 - bend * bend) * gelu_scale * (
            1.0 + 3.0 * gelu_cubic * square
        )
        branch = branch + dot(activated, down_rows, NN)
        grad_hidden = dot(grad_out_b, down_rows, NT) * slope
        grad_hidden_b = bfloat(grad_hidden)
        grad_hidden_in = grad_hidden_in + dot(grad_hidden_b, up_rows, NN)
        grad_small[pl.ds(8 + tile, 1), :] = jnp.sum(grad_hidden, axis=0, keepdims=True)
        grad_up = bfloat(dot(grad_hidden_b, hidden_in, TN))
        grad_down = bfloat(dot(activated, grad_out_b, TN))
        for part in range(4):
            owner = tile * 4 + part
            grads[owner, 32:160, :] = grad_up[part * 128 : part * 128 + 128]
            grads[owner, 160:288, :] = grad_down[part * 128 : part * 128 + 128]
        return branch, grad_hidden_in

    zeros = jnp.zeros((ROWS, WIDTH), jnp.float32)
    branch, grad_hidden_in = lax.fori_loop(0, HIDDEN // TILE, one_tile, (zeros, zeros))
    out[...] = bfloat(residual + branch + small[7:8, :])
    grad_norm, grad_gain, grad_bias = norm_back(unit, scale, small[5:6, :], grad_hidden_in)
    grad_resid = grad_out + grad_norm
    grad_resid_out[...] = grad_resid
    grad_resid_b = bfloat(grad_resid)
    grad_proj = bfloat(dot(grad_resid_b, attended, TN))
    for owner in range(16):
        grads[owner, 0:32, :] = grad_proj[owner * 32 : owner * 32 + 32]
    grad_small[0:4, :] = jnp.zeros((4, WIDTH), jnp.float32)
    grad_small[12:16, :] = jnp.zeros((4, WIDTH), jnp.float32)
    grad_small[4:5, :] = jnp.sum(grad_resid, axis=0, keepdims=True)
    grad_small[5:6, :] = grad_gain
    grad_small[6:7, :] = grad_bias
    grad_small[7:8, :] = jnp.sum(grad_out, axis=0, keepdims=True)
    grad_attended = f32(bfloat(dot(grad_resid_b, w_proj[...], NN)))
    for pair in range(4):
        columns = slice(pair * 128, pair * 128 + 128)
        first, second = pair_pack(grad_attended[0:128, columns], grad_attended[128:256, columns])
        for offset, block in ((0, first), (1, second)):
            send[4 * pair + 2 * offset] = bfloat(block)
            send[4 * pair + 2 * offset + 1] = bfloat(block)


def last_kernel(scalars, pieces, tokens, weights, small, grad_resid, part_small, grad_in, grads):
    mine = scalars[2]
    unit, scale = normed(f32(tokens[...]))
    hidden = bfloat(unit * small[0:1, :] + small[1:2, :])
    grad_hidden = jnp.zeros((ROWS, WIDTH), jnp.float32)
    sums_query = []
    sums_value = []

    def store(weight_grad, first_rows):
        for index, first in enumerate(first_rows):
            owner, row = divmod(first, 96)
            grads[row // 64, owner, row % 64 : row % 64 + 32, :] = weight_grad[
                index * 32 : index * 32 + 32
            ]

    for pair in range(4):
        top, bottom = pair_pack(
            f32(pieces[4 * pair + mine, 256:384, :]), f32(pieces[4 * pair + 2 + mine, 256:384, :])
        )
        grad_query = jnp.concatenate([top, bottom], axis=0)
        sums_query.append(jnp.sum(grad_query, axis=0, keepdims=True))
        grad_query = bfloat(grad_query)
        rows = slice(pair * 128, pair * 128 + 128)
        grad_hidden = grad_hidden + dot(grad_query, weights[rows, :], NN)
        store(
            bfloat(dot(grad_query, hidden, TN)), [pair * 128 + inside * 32 for inside in range(4)]
        )
    for head in range(HEADS):
        both = bfloat(f32(pieces[2 * head, 0:256, :]) + f32(pieces[2 * head + 1, 0:256, :]))
        sums_value.append(jnp.sum(f32(both), axis=0, keepdims=True))
        rows = slice(512 + head * 128, 512 + head * 128 + 128)
        grad_hidden = grad_hidden + dot(both, weights[rows, :], NN)
        first = 512 + head * HEAD_DIM
        store(
            bfloat(dot(both, hidden, TN)), [first, first + 32, first + 512, first + 512 + 32]
        )
    grad_norm, grad_gain, grad_bias = norm_back(unit, scale, small[0:1, :], grad_hidden)
    grad_in[...] = bfloat(grad_resid[...] + grad_norm)
    row = lax.broadcasted_iota(jnp.int32, (16, 128), 0)
    lane = lax.broadcasted_iota(jnp.int32, (16, 128), 1)
    for block in range(4):
        columns = slice(block * 128, block * 128 + 128)
        first = pltpu.roll(jnp.broadcast_to(sums_value[2 * block], (16, 128)), HEAD_DIM, 1)
        second = jnp.broadcast_to(sums_value[2 * block + 1], (16, 128))
        value_row = jnp.where(lane < HEAD_DIM, first, second)
        total = part_small[:, columns]
        total = jnp.where(row == 0, grad_gain[:, columns], total)
        total = jnp.where(row == 1, grad_bias[:, columns], total)
        total = jnp.where(row == 2, sums_query[block], total)
        total = jnp.where(row == 3, value_row, total)
        for inside in range(4):
            owner = block * 4 + inside
            moved = pltpu.roll(total, 128 - inside * 32, 1) if inside else total
            grads[1, owner, 32:48, 0:128] = bfloat(moved)
            grads[1, owner, 32:48, 128:512] = jnp.zeros((16, 384), jnp.bfloat16)
            grads[1, owner, 48:64, :] = jnp.zeros((16, 512), jnp.bfloat16)


def call(kernel, shapes, scratch=(), scalar=False, count=0, flops=0, moved=0):
    vmem = pl.BlockSpec(memory_space=pltpu.VMEM)
    specs = [vmem] * count
    if scalar:
        specs[0] = pl.BlockSpec(memory_space=pltpu.SMEM)
    return pl.pallas_call(
        kernel,
        out_shape=[jax.ShapeDtypeStruct(shape, kind) for shape, kind in shapes],
        in_specs=specs,
        out_specs=[vmem] * len(shapes),
        scratch_shapes=list(scratch),
        compiler_params=pltpu.CompilerParams(vmem_limit_bytes=52 * 1024 * 1024),
        cost_estimate=pl.CostEstimate(flops=flops, bytes_accessed=moved, transcendentals=0),
    )


def adam_update(weight, grad_sum, mean_old, square_old, step_rate, decay_on):
    mean_new = beta_first * mean_old + (1.0 - beta_first) * grad_sum
    square_new = beta_second * square_old + (1.0 - beta_second) * grad_sum * grad_sum
    mean_hat = mean_new / (1.0 - beta_first**STEP)
    square_hat = square_new / (1.0 - beta_second**STEP)
    weight_new = weight - step_rate * (
        mean_hat / (jnp.sqrt(square_hat) + adam_epsilon) + decay_on * weight_decay * weight
    )
    return (weight_new, mean_new, square_new)


def exchange(values):
    return lax.all_to_all(values, CTX, 0, 0, tiled=True)


def swap_cores(values):
    return lax.ppermute(values, "c", [(0, 1), (1, 0)])


def on_device(
    tokens, cotangent, lengths,
    w_qkv, w_proj, w_up, w_down, w_small,
    mean_qkv, mean_proj, mean_up, mean_down, mean_small,
    square_qkv, square_proj, square_up, square_down, square_small,
):
    core = lax.axis_index("c")
    place = lax.axis_index("z") * 4 + lax.axis_index("y")
    mine = (place ^ (place >> 1)) & 1
    lens_row = lengths[0]
    scalars = jnp.stack(
        [place, place & 1, mine, lens_row[0], lens_row[0] + lens_row[1], 0, 0, 0]
    ).astype(jnp.int32)

    later_own = bfloat(jnp.concatenate([w_proj.T, w_up.T, w_down], axis=0))
    later = lax.all_gather(later_own, CTX, axis=0, tiled=False)
    full_proj = later[:, 0:32].reshape(WIDTH, WIDTH)
    full_up = later[:, 32:160].reshape(HIDDEN, WIDTH)
    full_down = later[:, 160:288].reshape(HIDDEN, WIDTH)

    small_rows = jnp.pad(bfloat(w_small), ((0, 20), (0, WIDTH - 32)))
    first_own = jnp.concatenate([bfloat(w_qkv.T), small_rows], axis=0)
    first_half = lax.dynamic_slice_in_dim(first_own, core * 64, 64, 0)
    first_half = exchange(jnp.broadcast_to(first_half[None], (16, 64, WIDTH)))
    wide = lax.all_gather(first_half, "c", axis=0, tiled=False)

    kind = jnp.bfloat16
    send, weights, small = call(
        qkv_kernel,
        [((16, 384, 128), kind), ((1536, WIDTH), kind), ((16, WIDTH), jnp.float32)],
        count=2, flops=2 * 256 * 512 * 1536, moved=6 << 20,
    )(tokens, wide)
    pieces = exchange(send)
    send, turned, out_t, stats = call(
        attend_kernel,
        [
            ((16, 128, 128), kind),
            ((128, 4096), kind),
            ((8, HEAD_DIM, ROWS), jnp.float32),
            ((8, 8, ROWS), jnp.float32),
        ],
        [pltpu.VMEM((128, 4096), kind)],
        scalar=True, count=2, flops=36 * 512 * 256 * 2 * 256 * 2, moved=4 << 20,
    )(scalars, pieces)
    attended = exchange(send)
    out, send, grad_resid, grads_early, part_small = call(
        middle_kernel,
        [
            ((ROWS, WIDTH), kind),
            ((16, 128, 128), kind),
            ((ROWS, WIDTH), jnp.float32),
            ((16, 288, WIDTH), kind),
            ((16, WIDTH), jnp.float32),
        ],
        scalar=True, count=8, flops=2 * 256 * 512 * (3 * 512 + 6 * 2048), moved=12 << 20,
    )(scalars, attended, tokens, cotangent, full_proj, full_up, full_down, small)
    early = lax.psum_scatter(
        grads_early.reshape(16 * 288, WIDTH), CTX, scatter_dimension=0, tiled=True
    )
    grads = exchange(send)
    (send,) = call(
        attend_back_kernel,
        [((16, 384, 128), kind)],
        [pltpu.VMEM((4096, 128), jnp.float32)],
        scalar=True, count=6, flops=36 * 512 * 256 * 2 * 256 * 5, moved=5 << 20,
    )(scalars, pieces, turned, out_t, stats, grads)
    pieces = exchange(send)
    grad_in, grads_late = call(
        last_kernel,
        [((ROWS, WIDTH), kind), ((2, 16, 64, WIDTH), kind)],
        scalar=True, count=7, flops=4 * 256 * 512 * 1536, moved=8 << 20,
    )(scalars, pieces, tokens, weights, small, grad_resid, part_small)

    other = swap_cores(lax.dynamic_index_in_dim(grads_late, 1 - core, 0, keepdims=False))
    own = lax.dynamic_index_in_dim(grads_late, core, 0, keepdims=False)
    late = exchange(bfloat(f32(own) + f32(other)))
    late = bfloat(jnp.sum(f32(late), axis=0))
    early_other = swap_cores(lax.dynamic_slice_in_dim(early, (1 - core) * 144, 144, 0))
    early_own = lax.dynamic_slice_in_dim(early, core * 144, 144, 0)
    joined = jnp.concatenate([bfloat(f32(early_own) + f32(early_other)), late], axis=0)
    joined = lax.all_to_all(
        jnp.broadcast_to(joined[None], (4, 208, WIDTH)), "x", 0, 0, tiled=True
    )
    joined = bfloat(jnp.sum(f32(joined), axis=0))
    joined = f32(lax.all_gather(joined, "c", axis=0, tiled=False))
    early = joined[:, 0:144].reshape(288, WIDTH)
    late = joined[:, 144:208].reshape(128, WIDTH)
    own_qkv = late[0:96].T
    own_small = late[96:108, 0:32]
    own_proj = early[0:32].T
    own_up = early[32:160].T
    own_down = early[160:288]

    new_qkv, new_mean_qkv, new_square_qkv = adam_update(
        w_qkv, own_qkv, mean_qkv, square_qkv, 0.04, 1.0
    )
    new_proj, new_mean_proj, new_square_proj = adam_update(
        w_proj, own_proj, mean_proj, square_proj, 1.0, 1.0
    )
    new_up, new_mean_up, new_square_up = adam_update(w_up, own_up, mean_up, square_up, 0.04, 1.0)
    new_down, new_mean_down, new_square_down = adam_update(
        w_down, own_down, mean_down, square_down, 0.02, 1.0
    )
    new_small, new_mean_small, new_square_small = adam_update(
        w_small, own_small, mean_small, square_small, 2.0, 0.0
    )
    return (
        out, grad_in,
        new_qkv, new_proj, new_up, new_down, new_small,
        new_mean_qkv, new_mean_proj, new_mean_up, new_mean_down, new_mean_small,
        new_square_qkv, new_square_proj, new_square_up, new_square_down, new_square_small,
    )


def solution(mesh):
    fine = Mesh(mesh.devices.reshape(4, 2, 4, 4), ("x", "c", "z", "y"))
    rows = P(("x", "c", "z", "y"), None)
    columns = P(None, CTX)
    shards = (columns, columns, columns, P(CTX, None), columns)
    return jax.shard_map(
        on_device,
        mesh=fine,
        in_specs=(rows, rows, P(("x", "c"), None)) + shards * 3,
        out_specs=(rows, rows) + shards * 3,
        check_vma=False,
    )
```

```python
import functools
import jax
import jax.numpy as jnp
from jax import lax
from jax.experimental import pallas as pl
from jax.experimental.pallas import tpu as pltpu
from jax.sharding import Mesh, PartitionSpec as P

HEADS = 8
HEAD_DIM = 64
STEP = 10
WIDTH = 512
HIDDEN = 2048
ROWS = 256
HALF = 128
CHUNK = 512
TILE = 512

epsilon = 1e-05
negative_big = -1e30
beta_first = 0.9
beta_second = 0.95
adam_epsilon = 1e-08
weight_decay = 0.1
gelu_scale = 0.7978845608028654
gelu_cubic = 0.044715
log2_e = 1.4426950408889634

NN = (((1,), (0,)), ((), ()))
NT = (((1,), (1,)), ((), ()))
TN = (((0,), (0,)), ((), ()))
CTX = ("z", "y")


def dot(left, right, dims):
    return lax.dot_general(left, right, dims, preferred_element_type=jnp.float32)


def bfloat(values):
    return values.astype(jnp.bfloat16)


def f32(values):
    return values.astype(jnp.float32)


def normed(values):
    center = values - jnp.mean(values, axis=-1, keepdims=True)
    spread = jnp.mean(center * center, axis=-1, keepdims=True)
    scale = lax.rsqrt(spread + epsilon)
    return center * scale, scale


def norm_back(unit, scale, gain, grad):
    scaled = grad * gain
    first = jnp.mean(scaled, axis=-1, keepdims=True)
    second = jnp.mean(scaled * unit, axis=-1, keepdims=True)
    grad_values = (scaled - first - unit * second) * scale
    grad_gain = jnp.sum(grad * unit, axis=0, keepdims=True)
    grad_bias = jnp.sum(grad, axis=0, keepdims=True)
    return grad_values, grad_gain, grad_bias


def low_lanes(shape):
    return lax.broadcasted_iota(jnp.int32, shape, 1) < HEAD_DIM


def fetch(pairs, done):
    copies = [
        pltpu.make_async_copy(source, target, done.at[index])
        for index, (source, target) in enumerate(pairs)
    ]
    for copy in copies:
        copy.start()
    return copies


def mixed_rows(core, own, other):
    keep = own[pl.ds(pl.multiple_of(core * HALF, HALF), HALF), :]
    first = jnp.where(core == 0, keep, other)
    second = jnp.where(core == 0, other, keep)
    return jnp.concatenate([first, second], axis=0)


def pair_pack(top, bottom):
    low = low_lanes(top.shape)
    first = jnp.where(low, top, pltpu.roll(bottom, HEAD_DIM, 1))
    second = jnp.where(low, pltpu.roll(top, HEAD_DIM, 1), bottom)
    return first, second


def gather_kernel(
    scalars, tokens_in, cotangent_in, qkv_in, proj_in, up_in, down_in, small_in, send, rows_out,
    rows, qkv, proj, up, down, small, block, small_block, done,
):
    core = scalars[0]
    lanes = pl.ds(pl.multiple_of(scalars[1] * 128, 128), 128)
    away = pl.ds(pl.multiple_of((1 - core) * HALF, HALF), HALF)
    pairs = (
        (qkv_in, qkv), (up_in, up), (down_in, down), (proj_in, proj), (small_in, small),
        (tokens_in.at[away], rows.at[0]), (cotangent_in.at[away], rows.at[1]),
    )
    for copy in fetch(pairs, done):
        copy.wait()
    first_core = core == 0
    rows_out[...] = rows[...]
    small_block[...] = jnp.zeros((16, 128), jnp.float32)
    small_block[0:12, 0:32] = small[...]
    for part in range(4):
        columns = slice(part * 128, part * 128 + 128)
        tail = small_block[...] if part == 0 else jnp.zeros((16, 128), jnp.float32)
        second = jnp.concatenate([qkv[64:96, columns], tail, jnp.zeros((16, 128), jnp.float32)])
        half = jnp.where(first_core, qkv[0:64, columns], second)
        block[part * 64 : part * 64 + 64, :] = bfloat(half)
    half = jnp.where(first_core, up[lanes, :].T, down[:, lanes])
    block[256:384, :] = bfloat(half)
    half = jnp.where(first_core, proj[0:16, lanes], proj[16:32, lanes])
    block[384:400, :] = bfloat(half)
    for owner in range(16):
        send[owner] = block[...]


def qkv_kernel(
    scalars, tokens_in, rows_in, wide_own, wide_other, send, weights_out, small_out,
    tokens, rows_other, weights, small, done, stored,
):
    copies = fetch(((tokens_in, tokens), (rows_in, rows_other)), done)
    first_core = scalars[0] == 0

    def wide(half, owner, part, first, count):
        rows = slice(part * 64 + first, part * 64 + first + count)
        own, other = wide_own[owner, rows, :], wide_other[owner, rows, :]
        return jnp.where(first_core, own, other) if half == 0 else jnp.where(first_core, other, own)

    for owner in range(16):
        for piece in range(3):
            first = owner * 96 + piece * 32
            part, offset = divmod(first, 512)
            if part == 0:
                target = first
            else:
                head, inside = divmod(offset, HEAD_DIM)
                target = 512 + head * 128 + (part - 1) * HEAD_DIM + inside
            half, row = divmod(piece * 32, 64)
            for lanes in range(4):
                weights[target : target + 32, lanes * 128 : lanes * 128 + 128] = wide(
                    half, owner, lanes, row, 32
                )
    lane = lax.broadcasted_iota(jnp.int32, (16, 128), 1)
    for block in range(4):
        total = jnp.zeros((16, 128), jnp.float32)
        for inside in range(4):
            piece = f32(wide(1, block * 4 + inside, 0, 32, 16))
            moved = pltpu.roll(piece, inside * 32, 1) if inside else piece
            keep = (lane >= inside * 32) & (lane < inside * 32 + 32)
            total = jnp.where(keep, moved, total)
        small[:, block * 128 : block * 128 + 128] = total
    stores = fetch(((weights, weights_out), (small, small_out)), stored)
    for copy in copies:
        copy.wait()
    unit, _ = normed(f32(mixed_rows(scalars[0], tokens, rows_other[0])))
    hidden = bfloat(unit * small[0:1, :] + small[1:2, :])
    for pair in range(4):
        columns = slice(pair * 128, pair * 128 + 128)
        query = dot(hidden, weights[columns, :], NT) + small[2:3, columns]
        query = f32(bfloat(query)) * HEAD_DIM**-0.5
        for group in range(2):
            rows = group * HALF
            blocks = pair_pack(query[rows : rows + 64], query[rows + 64 : rows + 128])
            for offset, block in enumerate(blocks):
                send[group * 8 + pair * 2 + offset, HALF : HALF + 64, :] = bfloat(block)
    for head in range(HEADS):
        rows = slice(512 + head * 128, 512 + head * 128 + 128)
        bias = small[3:4, (head // 2) * 128 : (head // 2) * 128 + 128]
        if head % 2 == 0:
            bias = pltpu.roll(jnp.broadcast_to(bias, (8, 128)), HEAD_DIM, 1)[0:1]
        bias = jnp.where(low_lanes((1, 128)), 0.0, bias)
        both = bfloat(dot(hidden, weights[rows, :], NT) + bias)
        send[head, 0:HALF, :] = both[0:HALF]
        send[8 + head, 0:HALF, :] = both[HALF:ROWS]
    for copy in stores:
        copy.wait()


def query_positions(step, core):
    lane = lax.broadcasted_iota(jnp.int32, (1, ROWS), 1)
    block = 2 * step + ((lane & 64) >> 6)
    return block * ROWS + core * HALF + (lane & 63) + ((lane & 128) >> 1)


def doc_start(position, first_end, second_end):
    return jnp.where(
        position >= second_end, second_end, jnp.where(position >= first_end, first_end, 0)
    )


def packed_t(block):
    turned = block.T
    return jnp.concatenate([turned[0:HEAD_DIM], turned[HEAD_DIM:128]], axis=1)


def chunk_loops(step, first_end, second_end, body, state):
    low = doc_start(step * CHUNK, first_end, second_end) // CHUNK
    last_start = doc_start(step * CHUNK + 2 * CHUNK - 1, first_end, second_end)
    edge = jnp.minimum(step, (last_start + CHUNK - 1) // CHUNK)
    edge = jnp.maximum(edge, low)

    def masked_body(index, state):
        chunk = jnp.where(index == 0, step, low + index - 1)
        return body(chunk, True, state)

    state = lax.fori_loop(0, edge - low + 1, masked_body, state)
    return lax.fori_loop(edge, step, lambda chunk, state: body(chunk, False, state), state)


def allowed_mask(chunk, position, first_end, second_end):
    key = lax.broadcasted_iota(jnp.int32, (CHUNK, ROWS), 0) + chunk * CHUNK
    start = doc_start(position, first_end, second_end)
    return (key <= position) & (key >= start)


def packed_block(pieces, step):
    return jnp.concatenate(
        [f32(pieces[2 * step, HALF : HALF + 64, :]), f32(pieces[2 * step + 1, HALF : HALF + 64, :])],
        axis=0,
    )


def doc_ends(scalars, lens_own, lens_other, group):
    own = scalars[0] == group
    first = jnp.where(own, lens_own[0, 0], lens_other[0, 0])
    return first, first + jnp.where(own, lens_own[0, 1], lens_other[0, 1])


def attend_kernel(
    scalars, lens_own, lens_other, pieces, others,
    send, keys_hbm, turned_hbm, out_hbm, stats_hbm,
    keys_out, turned_out, out_t, stats, ones_t, done,
):
    core = scalars[0]
    first_end, second_end = doc_ends(scalars, lens_own, lens_other, scalars[2] // HEADS)

    def turn(source, _):
        columns = pl.ds(pl.multiple_of(source * ROWS, ROWS), ROWS)
        own, other = pieces[source, 0:HALF, :], others[source, 0:HALF, :]
        first, second = jnp.where(core == 0, own, other), jnp.where(core == 0, other, own)
        keys = jnp.concatenate([first, second], axis=0)
        keys_out[columns, :] = keys
        turned = f32(keys).T
        turned_out[:, columns] = bfloat(turned)
        row = lax.broadcasted_iota(jnp.int32, (128, ROWS), 0)
        ones_t[:, columns] = bfloat(jnp.where(row < HEAD_DIM, 1.0, turned))
        return 0

    lax.fori_loop(0, 16, turn, 0)
    stores = fetch(((keys_out, keys_hbm), (turned_out, turned_hbm)), done)

    def load_query(step):
        query_t = packed_t(packed_block(pieces, step))
        return bfloat(jnp.concatenate([query_t, jnp.zeros_like(query_t)], axis=0))

    def one_pair(pair, _):
        step = 2 * pair
        positions = tuple(query_positions(step + index, core) for index in range(2))
        queries = tuple(load_query(step + index) for index in range(2))

        def advance(chunk, masked, which, state):
            new_state = []
            columns = pl.ds(pl.multiple_of(chunk * CHUNK, CHUNK), CHUNK)
            keys = keys_out[columns, :]
            values = ones_t[:, columns]
            scores = [dot(keys, queries[index], NN) for index in which]
            for index, score, (run_max, total) in zip(which, scores, state):
                if masked:
                    allowed = allowed_mask(chunk, positions[index], first_end, second_end)
                    score = jnp.where(allowed, score, negative_big)
                new_max = jnp.maximum(run_max, jnp.max(score, axis=0, keepdims=True))
                weights = bfloat(jnp.exp2((score - new_max) * log2_e))
                scale = jnp.exp2((run_max - new_max) * log2_e)
                new_state.append((new_max, total * scale + dot(values, weights, NN)))
            return tuple(new_state)

        start = (
            jnp.full((1, ROWS), negative_big, jnp.float32),
            jnp.zeros((128, ROWS), jnp.float32),
        )
        state = chunk_loops(
            step, first_end, second_end,
            lambda chunk, masked, state: advance(chunk, masked, (0, 1), state),
            (start, start),
        )
        state = (state[0],) + advance(step + 1, True, (1,), state[1:])
        for index, (run_max, total) in enumerate(state):
            row_sum = total[0:1]
            result = total[HEAD_DIM:128] / row_sum
            out_t[step + index] = result
            stats[step + index] = jnp.broadcast_to(run_max + jnp.log(row_sum), (8, ROWS))
            packed = jnp.concatenate([result[:, 0:128], result[:, 128:256]], axis=0).T
            send[2 * (step + index)] = bfloat(packed[0:64])
            send[2 * (step + index) + 1] = bfloat(packed[64:128])
        return 0

    lax.fori_loop(0, 4, one_pair, 0)
    stores += fetch(((out_t, out_hbm), (stats, stats_hbm)), done.at[pl.ds(2, 2)])
    for copy in stores:
        copy.wait()


def attend_back_kernel(
    scalars, lens_own, lens_other, pieces, keys_hbm, turned_hbm, out_hbm, stats_hbm, grads,
    send, send_core, key_rows, turned, out_t, stats, total, done,
):
    copies = fetch(
        ((keys_hbm, key_rows), (turned_hbm, turned), (out_hbm, out_t), (stats_hbm, stats)), done
    )
    core = scalars[0]
    first_end, second_end = doc_ends(scalars, lens_own, lens_other, scalars[2] // HEADS)

    def clear(source, _):
        rows = pl.ds(pl.multiple_of(source * ROWS, ROWS), ROWS)
        total[rows, :] = jnp.zeros((ROWS, 128), jnp.float32)
        return 0

    lax.fori_loop(0, 16, clear, 0)
    for copy in copies:
        copy.wait()

    low = low_lanes((128, 128))

    def load_block(step):
        query = packed_block(pieces, step)
        query_t = packed_t(query)
        query_t = bfloat(jnp.concatenate([query_t, jnp.zeros_like(query_t)], axis=0))
        query = bfloat(
            jnp.concatenate(
                [jnp.where(low, query, 0.0), jnp.where(low, pltpu.roll(query, HEAD_DIM, 1), 0.0)],
                axis=0,
            )
        )
        grad = jnp.concatenate([f32(grads[2 * step]), f32(grads[2 * step + 1])], axis=0)
        grad_t = packed_t(grad)
        dots = jnp.sum(grad_t * out_t[step], axis=0, keepdims=True)
        grad_t = bfloat(jnp.concatenate([jnp.zeros_like(grad_t), grad_t], axis=0))
        grad = bfloat(
            jnp.concatenate(
                [jnp.where(low, 0.0, pltpu.roll(grad, HEAD_DIM, 1)), jnp.where(low, 0.0, grad)],
                axis=0,
            )
        )
        return query_t, grad_t, query, grad, dots, stats[step][0:1]

    def one_pair(pair, _):
        step = 2 * pair
        positions = tuple(query_positions(step + index, core) for index in range(2))
        loaded = tuple(load_block(step + index) for index in range(2))

        def advance(chunk, masked, which, state):
            rows = pl.ds(pl.multiple_of(chunk * CHUNK, CHUNK), CHUNK)
            keys = key_rows[rows, :]
            keys_t = turned[:, rows]
            scores = [dot(keys, loaded[index][0], NN) for index in which]
            grad_weights = [dot(keys, loaded[index][1], NN) for index in which]
            left, right, new_state = [], [], []
            for place, index in enumerate(which):
                _, _, query, grad, dots, stat = loaded[index]
                weights = jnp.exp2((scores[place] - stat) * log2_e)
                if masked:
                    allowed = allowed_mask(chunk, positions[index], first_end, second_end)
                    weights = jnp.where(allowed, weights, 0.0)
                grad_scores = bfloat(weights * (grad_weights[place] - dots))
                left += [grad_scores, bfloat(weights)]
                right += [query, grad]
                new_state.append(state[place] + dot(keys_t, grad_scores, NN))
            total[rows, :] += dot(jnp.concatenate(left, axis=1), jnp.concatenate(right, axis=0), NN)
            return tuple(new_state)

        start = jnp.zeros((128, ROWS), jnp.float32)
        state = chunk_loops(
            step, first_end, second_end,
            lambda chunk, masked, state: advance(chunk, masked, (0, 1), state),
            (start, start),
        )
        state = (state[0],) + advance(step + 1, True, (1,), state[1:])
        for index, grad_query_t in enumerate(state):
            turn = grad_query_t[0:HEAD_DIM] * HEAD_DIM**-0.5
            packed = jnp.concatenate([turn[:, 0:128], turn[:, 128:256]], axis=0).T
            send[2 * (step + index), HALF : HALF + 64, :] = bfloat(packed[0:64])
            send[2 * (step + index) + 1, HALF : HALF + 64, :] = bfloat(packed[64:128])
        return 0

    lax.fori_loop(0, 4, one_pair, 0)

    def emit(source, _):
        mine = pl.ds(pl.multiple_of(source * ROWS + core * HALF, HALF), HALF)
        away = pl.ds(pl.multiple_of(source * ROWS + (1 - core) * HALF, HALF), HALF)
        send[source, 0:HALF, :] = bfloat(total[mine, :])
        send_core[source] = bfloat(total[away, :])
        return 0

    lax.fori_loop(0, 16, emit, 0)


def middle_kernel(
    scalars, lens_own, lens_other, attended_in, tokens_in, cotangent_in, rows_in, later_in,
    later_other, small_in,
    out_own, out_away, send, grad_resid_hbm, small_hbm, grads_out,
    w_proj, grads, tokens, cotangent, rows_other, later_own, small, grad_resid_out, grad_small,
    done, fetched,
):
    pairs = (
        (later_in, later_own), (tokens_in, tokens), (rows_in, rows_other), (small_in, small),
        (cotangent_in, cotangent),
    )
    copies = fetch(pairs, fetched)
    core = scalars[0]
    first_core = core == 0
    slots = (core, 1 - core)
    for copy in copies:
        copy.wait()
    for owner in range(16):
        for lanes in range(4):
            columns = slice(lanes * 128, lanes * 128 + 128)
            own = later_own[lanes, owner, 128:144, :]
            other = later_other[lanes, owner, 128:144, :]
            first = owner * 32
            w_proj[first : first + 16, columns] = jnp.where(first_core, own, other)
            w_proj[first + 16 : first + 32, columns] = jnp.where(first_core, other, own)
    blocks = []
    for pair in range(4):
        parts = []
        for group in range(2):
            head = group * 8 + pair * 2
            parts += pair_pack(f32(attended_in[head]), f32(attended_in[head + 1]))
        blocks.append(jnp.concatenate(parts, axis=0))
    attended = bfloat(jnp.concatenate(blocks, axis=1))
    residual = f32(mixed_rows(core, tokens, rows_other[0])) + dot(attended, w_proj[...], NT) + small[4:5, :]
    unit, scale = normed(residual)
    hidden_in = bfloat(unit * small[5:6, :] + small[6:7, :])
    row = lax.broadcasted_iota(jnp.int32, (ROWS, 1), 0)
    position = (row & (HALF - 1)) + scalars[2] * ROWS + core * HALF
    _, first_live = doc_ends(scalars, lens_own, lens_other, 0)
    _, second_live = doc_ends(scalars, lens_own, lens_other, 1)
    live = position < jnp.where(row < HALF, first_live, second_live)
    grad_out = jnp.where(live, f32(mixed_rows(core, cotangent, rows_other[1])), 0.0)
    grad_out_b = bfloat(grad_out)

    def one_tile(tile, state):
        branch, grad_hidden_in = state
        owners = pl.ds(tile * 4, 4)
        own, other = (
            jnp.concatenate(
                [part[lanes, owners, 0:128, :].reshape(TILE, 128) for lanes in range(4)], axis=1
            )
            for part in (later_own, later_other)
        )
        up_rows = jnp.where(first_core, own, other)
        down_rows = jnp.where(first_core, other, own)
        hidden = dot(hidden_in, up_rows, NT) + small[pl.ds(8 + tile, 1), :]
        square = hidden * hidden
        bend = jnp.tanh(gelu_scale * hidden * (1.0 + gelu_cubic * square))
        half_open = 0.5 * (1.0 + bend)
        activated = bfloat(hidden * half_open)
        slope = half_open + 0.5 * hidden * (1.0 - bend * bend) * gelu_scale * (
            1.0 + 3.0 * gelu_cubic * square
        )
        branch = branch + dot(activated, down_rows, NN)
        grad_hidden = dot(grad_out_b, down_rows, NT) * slope
        grad_hidden_b = bfloat(grad_hidden)
        grad_hidden_in = grad_hidden_in + dot(grad_hidden_b, up_rows, NN)
        grad_small[pl.ds(8 + tile, 1), :] = jnp.sum(grad_hidden, axis=0, keepdims=True)
        grad_up = bfloat(dot(grad_hidden_b, hidden_in, TN))
        grad_down = bfloat(dot(activated, grad_out_b, TN))
        for lanes in range(4):
            columns = slice(lanes * 128, lanes * 128 + 128)
            grads[lanes, slots[0], owners, 0:128, :] = grad_up[:, columns].reshape(4, 128, 128)
            grads[lanes, slots[1], owners, 0:128, :] = grad_down[:, columns].reshape(4, 128, 128)
        here = grads.at[:, :, owners, 0:128, :]
        pltpu.make_async_copy(here, grads_out.at[:, :, owners, 0:128, :], done.at[tile]).start()
        return branch, grad_hidden_in

    zeros = jnp.zeros((ROWS, WIDTH), jnp.float32)
    branch, grad_hidden_in = lax.fori_loop(0, HIDDEN // TILE, one_tile, (zeros, zeros))
    out = bfloat(residual + branch + small[7:8, :])
    out_own[...] = jnp.where(first_core, out[0:HALF], out[HALF:ROWS])
    out_away[...] = jnp.where(first_core, out[HALF:ROWS], out[0:HALF])
    grad_norm, grad_gain, grad_bias = norm_back(unit, scale, small[5:6, :], grad_hidden_in)
    grad_resid = grad_out + grad_norm
    grad_resid_out[...] = grad_resid
    grad_resid_b = bfloat(grad_resid)
    grad_proj = bfloat(dot(grad_resid_b, attended, TN)).reshape(16, 32, WIDTH)
    for lanes in range(4):
        columns = slice(lanes * 128, lanes * 128 + 128)
        grads[lanes, slots[0], :, 128:144, :] = grad_proj[:, 0:16, columns]
        grads[lanes, slots[1], :, 128:144, :] = grad_proj[:, 16:32, columns]
    tail = pltpu.make_async_copy(
        grads.at[:, :, :, 128:144, :], grads_out.at[:, :, :, 128:144, :], done.at[4]
    )
    tail.start()
    grad_small[0:4, :] = jnp.zeros((4, WIDTH), jnp.float32)
    grad_small[12:16, :] = jnp.zeros((4, WIDTH), jnp.float32)
    grad_small[4:5, :] = jnp.sum(grad_resid, axis=0, keepdims=True)
    grad_small[5:6, :] = grad_gain
    grad_small[6:7, :] = grad_bias
    grad_small[7:8, :] = jnp.sum(grad_out, axis=0, keepdims=True)
    stores = fetch(
        ((grad_resid_out, grad_resid_hbm), (grad_small, small_hbm)), done.at[pl.ds(5, 2)]
    )
    grad_attended = f32(bfloat(dot(grad_resid_b, w_proj[...], NN)))
    for pair in range(4):
        columns = slice(pair * 128, pair * 128 + 128)
        for group in range(2):
            first = group * HALF
            halves = grad_attended[first : first + 64, columns], grad_attended[
                first + 64 : first + 128, columns
            ]
            for offset, block in enumerate(pair_pack(*halves)):
                send[group * 8 + pair * 2 + offset] = bfloat(block)
    for tile in range(HIDDEN // TILE):
        owners = pl.ds(tile * 4, 4)
        pltpu.make_async_copy(
            grads.at[:, :, owners, 0:128, :], grads_out.at[:, :, owners, 0:128, :], done.at[tile]
        ).wait()
    tail.wait()
    for copy in stores:
        copy.wait()


def last_kernel(
    scalars, pieces, tokens_in, rows_in, weights_in, small_in, grad_resid_in, part_in,
    grad_in_own, grad_in_away, grads_own, grads_away,
    tokens, rows_other, weights, small, grad_resid, part_small, grads, done,
):
    pairs = (
        (weights_in, weights), (tokens_in, tokens), (rows_in, rows_other), (small_in, small),
        (grad_resid_in, grad_resid), (part_in, part_small),
    )
    copies = fetch(pairs, done)
    core = scalars[0]
    slots = (core, 1 - core)
    for copy in copies:
        copy.wait()
    unit, scale = normed(f32(mixed_rows(core, tokens, rows_other[0])))
    hidden = bfloat(unit * small[0:1, :] + small[1:2, :])
    grad_hidden = jnp.zeros((ROWS, WIDTH), jnp.float32)
    sums_query = []
    sums_value = []

    def store(weight_grad, first_rows):
        for index, first in enumerate(first_rows):
            owner, row = divmod(first, 96)
            for lanes in range(4):
                place = slice(lanes * 64 + row % 64, lanes * 64 + row % 64 + 32)
                grads[slots[row // 64], owner, place, :] = weight_grad[
                    index * 32 : index * 32 + 32, lanes * 128 : lanes * 128 + 128
                ]

    for pair in range(4):
        parts = []
        for group in range(2):
            head = group * 8 + pair * 2
            blocks = (f32(pieces[head + offset, HALF : HALF + 64, :]) for offset in range(2))
            parts += pair_pack(*blocks)
        grad_query = jnp.concatenate(parts, axis=0)
        sums_query.append(jnp.sum(grad_query, axis=0, keepdims=True))
        grad_query = bfloat(grad_query)
        rows = slice(pair * 128, pair * 128 + 128)
        grad_hidden = grad_hidden + dot(grad_query, weights[rows, :], NN)
        store(
            bfloat(dot(grad_query, hidden, TN)), [pair * 128 + inside * 32 for inside in range(4)]
        )
    for head in range(HEADS):
        both = jnp.concatenate([pieces[head, 0:HALF, :], pieces[8 + head, 0:HALF, :]], axis=0)
        sums_value.append(jnp.sum(f32(both), axis=0, keepdims=True))
        rows = slice(512 + head * 128, 512 + head * 128 + 128)
        grad_hidden = grad_hidden + dot(both, weights[rows, :], NN)
        first = 512 + head * HEAD_DIM
        store(
            bfloat(dot(both, hidden, TN)), [first, first + 32, first + 512, first + 512 + 32]
        )
    grad_norm, grad_gain, grad_bias = norm_back(unit, scale, small[0:1, :], grad_hidden)
    grad_in = bfloat(grad_resid[...] + grad_norm)
    grad_in_own[...] = jnp.where(core == 0, grad_in[0:HALF], grad_in[HALF:ROWS])
    grad_in_away[...] = jnp.where(core == 0, grad_in[HALF:ROWS], grad_in[0:HALF])
    row = lax.broadcasted_iota(jnp.int32, (16, 128), 0)
    lane = lax.broadcasted_iota(jnp.int32, (16, 128), 1)
    for block in range(4):
        columns = slice(block * 128, block * 128 + 128)
        first = pltpu.roll(jnp.broadcast_to(sums_value[2 * block], (16, 128)), HEAD_DIM, 1)
        second = jnp.broadcast_to(sums_value[2 * block + 1], (16, 128))
        value_row = jnp.where(lane < HEAD_DIM, first, second)
        total = part_small[:, columns]
        total = jnp.where(row == 0, grad_gain[:, columns], total)
        total = jnp.where(row == 1, grad_bias[:, columns], total)
        total = jnp.where(row == 2, sums_query[block], total)
        total = jnp.where(row == 3, value_row, total)
        for inside in range(4):
            owner = block * 4 + inside
            moved = pltpu.roll(total, 128 - inside * 32, 1) if inside else total
            grads[slots[1], owner, 32:48, :] = bfloat(moved)
            grads[slots[1], owner, 48:64, :] = jnp.zeros((16, 128), jnp.bfloat16)
            for lanes in range(1, 4):
                place = slice(lanes * 64 + 32, lanes * 64 + 64)
                grads[slots[1], owner, place, :] = jnp.zeros((32, 128), jnp.bfloat16)
    for owner in range(16):
        grads_own[owner] = grads[0, owner]
        grads_away[owner] = grads[1, owner]


def adam_update(weight, grad_sum, mean_old, square_old, step_rate, decay_on):
    mean_new = beta_first * mean_old + (1.0 - beta_first) * grad_sum
    square_new = beta_second * square_old + (1.0 - beta_second) * grad_sum * grad_sum
    mean_hat = mean_new / (1.0 - beta_first**STEP)
    square_hat = square_new / (1.0 - beta_second**STEP)
    weight_new = weight - step_rate * (
        mean_hat / (jnp.sqrt(square_hat) + adam_epsilon) + decay_on * weight_decay * weight
    )
    return (weight_new, mean_new, square_new)


rates = ((0.04, 1.0), (1.0, 1.0), (0.04, 1.0), (0.02, 1.0), (2.0, 0.0))


def adam_kernel(scalars, grads_own, grads_other, *refs):
    core = scalars[0]
    for index in range(2):
        own, other = refs[15 + 2 * index], refs[16 + 2 * index]
        whole = refs[19 + index]
        whole[pl.ds(pl.multiple_of(core * HALF, HALF), HALF), :] = own[...]
        whole[pl.ds(pl.multiple_of((1 - core) * HALF, HALF), HALF), :] = other[...]
    first_core = scalars[0] == 0
    olds, news = refs[:15], refs[21:36]

    def picked(half, rows, part=None):
        own, other = (
            jnp.concatenate([f32(ref[lanes, rows, :]) for lanes in range(4)], axis=1)
            if part is None
            else sum(f32(ref[group, part * 64 + rows.start : part * 64 + rows.stop, :]) for group in range(4))
            for ref in (grads_own, grads_other)
        )
        return jnp.where(first_core, own, other) if half == 0 else jnp.where(first_core, other, own)

    def late(half, rows):
        return jnp.concatenate([picked(half, rows, part) for part in range(4)], axis=1)

    grad_qkv = jnp.concatenate([late(0, slice(0, 64)), late(1, slice(0, 32))], axis=0)
    grad_small = picked(1, slice(32, 48), 0)[0:12, 0:32]
    grad_up = picked(0, slice(256, 384)).T
    grad_down = picked(1, slice(256, 384))
    grad_proj = jnp.concatenate([picked(0, slice(384, 400)), picked(1, slice(384, 400))], axis=0)
    for index, grad in enumerate((grad_qkv, grad_proj, grad_up, grad_down, grad_small)):
        results = adam_update(
            olds[index][...], grad, olds[5 + index][...], olds[10 + index][...], *rates[index]
        )
        for group, result in enumerate(results):
            news[group * 5 + index][...] = result


def call(
    kernel, shapes, scratch=(), scalars=1, hbm_in=(), hbm_out=(), flops=0, moved=0, vmem_mib=20
):
    vmem = pl.BlockSpec(memory_space=pltpu.VMEM)
    hbm = pl.BlockSpec(memory_space=pltpu.HBM)
    smem = pl.BlockSpec(memory_space=pltpu.SMEM)

    def run(*args):
        specs = [
            smem if index < scalars else hbm if index in hbm_in else vmem
            for index in range(len(args))
        ]
        args = [
            pltpu.with_memory_space_constraint(arg, pltpu.HBM) if index in hbm_in else arg
            for index, arg in enumerate(args)
        ]
        return pl.pallas_call(
            kernel,
            out_shape=[
                pltpu.HBM(shape, kind) if index in hbm_out else jax.ShapeDtypeStruct(shape, kind)
                for index, (shape, kind) in enumerate(shapes)
            ],
            in_specs=specs,
            out_specs=[hbm if index in hbm_out else vmem for index in range(len(shapes))],
            scratch_shapes=list(scratch),
            compiler_params=pltpu.CompilerParams(vmem_limit_bytes=vmem_mib * 1024 * 1024),
            cost_estimate=pl.CostEstimate(flops=flops, bytes_accessed=moved, transcendentals=0),
        )(*args)

    return run


def exchange(values):
    return lax.all_to_all(values, CTX, 0, 0, tiled=True)


def swap_cores(values):
    return lax.ppermute(values, "c", [(0, 1), (1, 0)])


def on_device(
    tokens, cotangent, lengths,
    w_qkv, w_proj, w_up, w_down, w_small,
    mean_qkv, mean_proj, mean_up, mean_down, mean_small,
    square_qkv, square_proj, square_up, square_down, square_small,
):
    kind = jnp.bfloat16
    core = lax.axis_index("c")
    place = lax.axis_index("z") * 4 + lax.axis_index("y")
    scalars = jnp.stack([core, lax.axis_index("x"), place]).astype(jnp.int32)
    lens_other = swap_cores(lengths)
    turned_olds = (
        w_qkv.T, w_proj.T, w_up, w_down, w_small,
        mean_qkv.T, mean_proj.T, mean_up, mean_down, mean_small,
        square_qkv.T, square_proj.T, square_up, square_down, square_small,
    )
    single = jnp.float32
    rows_kind = pltpu.VMEM((ROWS, WIDTH), kind)
    pair_kind = pltpu.VMEM((2, HALF, WIDTH), kind)
    small_kind = pltpu.VMEM((16, WIDTH), single)

    send, rows_away = call(
        gather_kernel,
        [((16, 400, 128), kind), ((2, HALF, WIDTH), kind)],
        [
            pair_kind,
            pltpu.VMEM((96, WIDTH), single),
            pltpu.VMEM((32, WIDTH), single),
            pltpu.VMEM((WIDTH, 128), single),
            pltpu.VMEM((128, WIDTH), single),
            pltpu.VMEM((12, 32), single),
            pltpu.VMEM((400, 128), kind),
            pltpu.VMEM((16, 128), single),
            pltpu.SemaphoreType.DMA((7,)),
        ],
        hbm_in=range(1, 8), moved=3 << 20,
    )(scalars, tokens, cotangent, *turned_olds[0:5])
    rows_other = swap_cores(rows_away)
    first_own = exchange(send)
    first_other = swap_cores(first_own[:, 0:256])
    later_own = lax.all_gather(first_own[:, 256:400], "x", axis=0, tiled=False)
    first_other, lens_other = lax.optimization_barrier((first_other, lens_other))

    send, weights, small = call(
        qkv_kernel,
        [((16, 192, 128), kind), ((1536, WIDTH), kind), ((16, WIDTH), single)],
        [
            rows_kind, pair_kind, pltpu.VMEM((1536, WIDTH), kind), small_kind,
            pltpu.SemaphoreType.DMA((2,)), pltpu.SemaphoreType.DMA((2,)),
        ],
        hbm_in=(1, 2), hbm_out=(1, 2), flops=2 * 256 * 512 * 1536, moved=6 << 20,
    )(scalars, tokens, rows_other, first_own, first_other)
    pieces = exchange(send)
    kept = [
        ((4096, 128), kind), ((128, 4096), kind),
        ((8, HEAD_DIM, ROWS), single), ((8, 8, ROWS), single),
    ]
    kept_scratch = [pltpu.VMEM(*item) for item in kept]
    send, *kept_values = call(
        attend_kernel,
        [((16, 64, 128), kind)] + kept,
        kept_scratch + [pltpu.VMEM((128, 4096), kind), pltpu.SemaphoreType.DMA((4,))],
        scalars=3, hbm_out=(1, 2, 3, 4), flops=36 * 512 * 256 * 2 * 256 * 2, moved=4 << 20,
    )(scalars, lengths, lens_other, pieces, swap_cores(pieces))
    send, later_own = lax.optimization_barrier((send, later_own))
    later_other = swap_cores(later_own)
    attended = exchange(send)
    out_own, out_away, send, grad_resid, part_small, early = call(
        middle_kernel,
        [
            ((HALF, WIDTH), kind),
            ((HALF, WIDTH), kind),
            ((16, 64, 128), kind),
            ((ROWS, WIDTH), single),
            ((16, WIDTH), single),
            ((4, 2, 16, 144, 128), kind),
        ],
        [
            pltpu.VMEM((WIDTH, WIDTH), kind),
            pltpu.VMEM((4, 2, 16, 144, 128), kind),
            rows_kind, rows_kind, pair_kind,
            pltpu.VMEM((4, 16, 144, 128), kind),
            small_kind,
            pltpu.VMEM((ROWS, WIDTH), single),
            small_kind,
            pltpu.SemaphoreType.DMA((7,)),
            pltpu.SemaphoreType.DMA((5,)),
        ],
        scalars=3, hbm_in=(4, 5, 6, 7, 9), hbm_out=(3, 4, 5),
        flops=2 * 256 * 512 * (3 * 512 + 6 * 2048), moved=12 << 20, vmem_mib=32,
    )(
        scalars, lengths, lens_other, attended, tokens, cotangent, rows_other,
        later_own, later_other, small,
    )
    early = lax.psum_scatter(
        early.reshape(4 * 2 * 16 * 144, 128), "x", scatter_dimension=0, tiled=True
    ).reshape(2, 16, 144, 128)
    grads = exchange(send)
    send, send_core = call(
        attend_back_kernel,
        [((16, 192, 128), kind), ((16, HALF, 128), kind)],
        kept_scratch + [pltpu.VMEM((4096, 128), single), pltpu.SemaphoreType.DMA((4,))],
        scalars=3, hbm_in=(4, 5, 6, 7), flops=36 * 512 * 256 * 2 * 256 * 5, moved=5 << 20,
    )(scalars, lengths, lens_other, pieces, *kept_values, grads)
    whole = f32(send[:, 0:HALF]) + f32(swap_cores(send_core))
    pieces = exchange(jnp.concatenate([bfloat(whole), send[:, HALF:]], axis=1))
    grad_in_own, grad_in_away, late_own, late_away = call(
        last_kernel,
        [((HALF, WIDTH), kind), ((HALF, WIDTH), kind)] + [((16, 256, 128), kind)] * 2,
        [
            rows_kind, pair_kind, pltpu.VMEM((1536, WIDTH), kind), small_kind,
            pltpu.VMEM((ROWS, WIDTH), single), small_kind,
            pltpu.VMEM((2, 16, 256, 128), kind), pltpu.SemaphoreType.DMA((6,)),
        ],
        hbm_in=(2, 3, 4, 5, 6, 7), flops=4 * 256 * 512 * 1536, moved=8 << 20,
    )(scalars, pieces, tokens, rows_other, weights, small, grad_resid, part_small)

    late = f32(late_own) + f32(swap_cores(late_away))
    early = f32(early[0]) + f32(swap_cores(early[1]))
    sums = exchange(jnp.concatenate([bfloat(late), bfloat(early)], axis=1))
    sums = bfloat(jnp.sum(f32(sums), axis=0))
    grads_own = lax.all_to_all(
        jnp.broadcast_to(sums[None], (4, 400, 128)), "x", 0, 0, tiled=True
    )
    out, grad_in, *news = call(
        adam_kernel,
        [((ROWS, WIDTH), kind)] * 2 + [(old.shape, single) for old in turned_olds],
        moved=8 << 20,
    )(
        scalars, grads_own, swap_cores(grads_own), *turned_olds,
        out_own, swap_cores(out_away), grad_in_own, swap_cores(grad_in_away),
    )
    news = [new.T if index % 5 < 2 else new for index, new in enumerate(news)]
    return (out, grad_in, *news)


def solution(mesh):
    fine = Mesh(mesh.devices.reshape(4, 2, 4, 4), ("x", "c", "z", "y"))
    rows = P(("x", "c", "z", "y"), None)
    columns = P(None, CTX)
    shards = (columns, columns, columns, P(CTX, None), columns)
    return jax.shard_map(
        on_device,
        mesh=fine,
        in_specs=(rows, rows, P(("x", "c"), None)) + shards * 3,
        out_specs=(rows, rows) + shards * 3,
        check_vma=False,
    )
```

```python
import functools
import jax
import jax.numpy as jnp
from jax import lax
from jax.experimental import pallas as pl
from jax.experimental.pallas import tpu as pltpu
from jax.sharding import Mesh, PartitionSpec as P

HEADS = 8
HEAD_DIM = 64
STEP = 10
WIDTH = 512
HIDDEN = 2048
ROWS = 256
HALF = 128
CHUNK = 512
TILE = 512
WIDE = 1024
EARLY = 208
BLOCK = 352

epsilon = 1e-05
negative_big = -1e30
beta_first = 0.9
beta_second = 0.95
adam_epsilon = 1e-08
weight_decay = 0.1
gelu_scale = 0.7978845608028654
gelu_cubic = 0.044715
log2_e = 1.4426950408889634

NN = (((1,), (0,)), ((), ()))
NT = (((1,), (1,)), ((), ()))
TN = (((0,), (0,)), ((), ()))
CTX = ("z", "y")


def dot(left, right, dims):
    return lax.dot_general(left, right, dims, preferred_element_type=jnp.float32)


def bfloat(values):
    return values.astype(jnp.bfloat16)


def f32(values):
    return values.astype(jnp.float32)


def normed(values):
    center = values - jnp.mean(values, axis=-1, keepdims=True)
    spread = jnp.mean(center * center, axis=-1, keepdims=True)
    scale = lax.rsqrt(spread + epsilon)
    return center * scale, scale


def norm_back(unit, scale, gain, grad):
    scaled = grad * gain
    first = jnp.mean(scaled, axis=-1, keepdims=True)
    second = jnp.mean(scaled * unit, axis=-1, keepdims=True)
    grad_values = (scaled - first - unit * second) * scale
    grad_gain = jnp.sum(grad * unit, axis=0, keepdims=True)
    grad_bias = jnp.sum(grad, axis=0, keepdims=True)
    return grad_values, grad_gain, grad_bias


def low_lanes(shape):
    return lax.broadcasted_iota(jnp.int32, shape, 1) < HEAD_DIM


def fetch(pairs, done):
    copies = [
        pltpu.make_async_copy(source, target, done.at[index])
        for index, (source, target) in enumerate(pairs)
    ]
    for copy in copies:
        copy.start()
    return copies


def mixed_rows(core, own, other):
    keep = own[pl.ds(pl.multiple_of(core * HALF, HALF), HALF), :]
    first = jnp.where(core == 0, keep, other)
    second = jnp.where(core == 0, other, keep)
    return jnp.concatenate([first, second], axis=0)


def pair_pack(top, bottom):
    low = low_lanes(top.shape)
    first = jnp.where(low, top, pltpu.roll(bottom, HEAD_DIM, 1))
    second = jnp.where(low, pltpu.roll(top, HEAD_DIM, 1), bottom)
    return first, second


def gather_kernel(
    scalars, tokens_in, cotangent_in, qkv_in, proj_in, up_in, down_in, small_in, send, rows_out,
    rows, qkv, proj, up, down, small, block, small_block, done,
):
    core = scalars[0]
    lanes = pl.ds(pl.multiple_of(scalars[1] * 128, 128), 128)
    away = pl.ds(pl.multiple_of((1 - core) * HALF, HALF), HALF)
    pairs = (
        (qkv_in, qkv), (up_in, up), (down_in, down), (proj_in, proj), (small_in, small),
        (tokens_in.at[away], rows.at[0]), (cotangent_in.at[away], rows.at[1]),
    )
    for copy in fetch(pairs, done):
        copy.wait()
    first_core = core == 0
    rows_out[...] = rows[...]
    small_block[...] = jnp.zeros((16, 128), jnp.float32)
    small_block[0:12, 0:32] = small[...]
    for part in range(4):
        columns = slice(part * 128, part * 128 + 128)
        half = jnp.where(first_core, qkv[0:48, columns], qkv[48:96, columns])
        block[part * 48 : part * 48 + 48, :] = bfloat(half)
    block[192:208, :] = bfloat(small_block[...])
    half = jnp.where(first_core, up[lanes, :].T, down[:, lanes])
    block[208:336, :] = bfloat(half)
    half = jnp.where(first_core, proj[0:16, lanes], proj[16:32, lanes])
    block[336:352, :] = bfloat(half)
    for owner in range(16):
        send[owner] = block[...]


def qkv_kernel(
    scalars, tokens_in, rows_other, wide_own, wide_other, send, weights_out, small_out,
    tokens, weights, small, done, stored,
):
    copies = fetch(((tokens_in, tokens),), done)
    first_core = scalars[0] == 0

    def wide(half, owner, part, first):
        rows = slice(part * 48 + first, part * 48 + first + 16)
        own, other = wide_own[owner, rows, :], wide_other[owner, rows, :]
        return jnp.where(first_core, own, other) if half == 0 else jnp.where(first_core, other, own)

    for owner in range(16):
        for piece in range(6):
            first = owner * 96 + piece * 16
            part, offset = divmod(first, 512)
            if part == 0:
                target = first
            else:
                head, inside = divmod(offset, HEAD_DIM)
                target = 512 + head * 128 + (part - 1) * HEAD_DIM + inside
            half, row = divmod(piece * 16, 48)
            for lanes in range(4):
                weights[target : target + 16, lanes * 128 : lanes * 128 + 128] = wide(
                    half, owner, lanes, row
                )
    lane = lax.broadcasted_iota(jnp.int32, (16, 128), 1)
    for block in range(4):
        total = jnp.zeros((16, 128), jnp.float32)
        for inside in range(4):
            piece = f32(wide_own[block * 4 + inside, 192:208, :])
            moved = pltpu.roll(piece, inside * 32, 1) if inside else piece
            keep = (lane >= inside * 32) & (lane < inside * 32 + 32)
            total = jnp.where(keep, moved, total)
        small[:, block * 128 : block * 128 + 128] = total
    stores = fetch(((weights, weights_out), (small, small_out)), stored)
    for copy in copies:
        copy.wait()
    unit, _ = normed(f32(mixed_rows(scalars[0], tokens, rows_other[0])))
    hidden = bfloat(unit * small[0:1, :] + small[1:2, :])
    for pair in range(4):
        columns = slice(pair * 128, pair * 128 + 128)
        query = dot(hidden, weights[columns, :], NT) + small[2:3, columns]
        query = f32(bfloat(query)) * HEAD_DIM**-0.5
        for group in range(2):
            rows = group * HALF
            blocks = pair_pack(query[rows : rows + 64], query[rows + 64 : rows + 128])
            for offset, block in enumerate(blocks):
                send[group * 8 + pair * 2 + offset, HALF : HALF + 64, :] = bfloat(block)
    for head in range(HEADS):
        rows = slice(512 + head * 128, 512 + head * 128 + 128)
        bias = small[3:4, (head // 2) * 128 : (head // 2) * 128 + 128]
        if head % 2 == 0:
            bias = pltpu.roll(jnp.broadcast_to(bias, (8, 128)), HEAD_DIM, 1)[0:1]
        bias = jnp.where(low_lanes((1, 128)), 0.0, bias)
        both = bfloat(dot(hidden, weights[rows, :], NT) + bias)
        send[head, 0:HALF, :] = both[0:HALF]
        send[8 + head, 0:HALF, :] = both[HALF:ROWS]
    for copy in stores:
        copy.wait()


def query_rows(core):
    lane = lax.broadcasted_iota(jnp.int32, (1, ROWS), 1)
    return ((lane & 64) << 2) + core * HALF + (lane & 63) + ((lane & 128) >> 1)


def doc_of(position, first_end, second_end):
    return (position >= first_end).astype(jnp.int32) + (position >= second_end).astype(jnp.int32)


def doc_start(position, first_end, second_end):
    return jnp.where(
        position >= second_end, second_end, jnp.where(position >= first_end, first_end, 0)
    )


def packed_t(block):
    turned = block.T
    return jnp.concatenate([turned[0:HEAD_DIM], turned[HEAD_DIM:128]], axis=1)


def causal_bias(bias, core):
    key = lax.broadcasted_iota(jnp.int32, (CHUNK, ROWS), 0)
    bias[...] = jnp.where(key <= query_rows(core), 0.0, negative_big)


def keyed_rows(rows, first, first_end, second_end):
    lane = lax.broadcasted_iota(jnp.int32, (ROWS, 128), 1)
    row = lax.broadcasted_iota(jnp.int32, (ROWS, 128), 0) + first
    mark = lane - HEAD_DIM == doc_of(row, first_end, second_end)
    return bfloat(jnp.where(lane < HEAD_DIM, rows, jnp.where(mark, 1.0, 0.0)))


def keyed_queries(query_t, step, core, first_end, second_end):
    position = query_rows(core) + step * CHUNK
    line = lax.broadcasted_iota(jnp.int32, (HEAD_DIM, ROWS), 0)
    other = (line < 3) & (line != doc_of(position, first_end, second_end))
    penalty = jnp.where(other, negative_big, 0.0)
    return bfloat(jnp.concatenate([query_t, penalty], axis=0))


def packed_block(pieces, step):
    return jnp.concatenate(
        [f32(pieces[2 * step, HALF : HALF + 64, :]), f32(pieces[2 * step + 1, HALF : HALF + 64, :])],
        axis=0,
    )


def doc_ends(scalars, lens_own, lens_other, group):
    own = scalars[0] == group
    first = jnp.where(own, lens_own[0, 0], lens_other[0, 0])
    return first, first + jnp.where(own, lens_own[0, 1], lens_other[0, 1])


def attend_kernel(
    scalars, lens_own, lens_other, pieces, others,
    send, keyed_hbm, keys_hbm, turned_hbm, out_hbm, stats_hbm,
    keyed, keys_out, turned_out, out_t, stats, ones_t, bias, done,
):
    core = scalars[0]
    first_end, second_end = doc_ends(scalars, lens_own, lens_other, scalars[2] // HEADS)
    causal_bias(bias, core)

    def turn(source, _):
        columns = pl.ds(pl.multiple_of(source * ROWS, ROWS), ROWS)
        own, other = pieces[source, 0:HALF, :], others[source, 0:HALF, :]
        first, second = jnp.where(core == 0, own, other), jnp.where(core == 0, other, own)
        keys = jnp.concatenate([first, second], axis=0)
        keys_out[columns, :] = keys
        keys = f32(keys)
        keyed[columns, :] = keyed_rows(keys, source * ROWS, first_end, second_end)
        turned = keys.T
        turned_out[:, columns] = bfloat(turned)
        row = lax.broadcasted_iota(jnp.int32, (128, ROWS), 0)
        ones_t[:, columns] = bfloat(jnp.where(row < HEAD_DIM, 1.0, turned))
        return 0

    lax.fori_loop(0, 16, turn, 0, unroll=4)
    stores = fetch(((keyed, keyed_hbm), (keys_out, keys_hbm), (turned_out, turned_hbm)), done)

    def one_pair(pair, _):
        step = 2 * pair
        queries = tuple(
            keyed_queries(
                packed_t(packed_block(pieces, step + index)), step + index, core, first_end, second_end
            )
            for index in range(2)
        )

        def advance(scores, values, state):
            run_max, total = state
            new_max = jnp.maximum(run_max, jnp.max(scores, axis=0, keepdims=True))
            weights = bfloat(jnp.exp2((scores - new_max) * log2_e))
            scale = jnp.exp2((run_max - new_max) * log2_e)
            return new_max, total * scale + dot(values, weights, NN)

        def body(wide, state):
            rows = pl.ds(pl.multiple_of(wide * WIDE, WIDE), WIDE)
            keys, values = keyed[rows, :], ones_t[:, rows]
            scores = [dot(keys, query, NN) for query in queries]
            return tuple(advance(scores[index], values, state[index]) for index in range(2))

        start = (
            jnp.full((1, ROWS), negative_big, jnp.float32),
            jnp.zeros((128, ROWS), jnp.float32),
        )
        low = doc_start(step * CHUNK, first_end, second_end) // WIDE
        first, second = lax.fori_loop(low, pair, body, (start, start))
        rows = pl.ds(pl.multiple_of(pair * WIDE, WIDE), WIDE)
        keys, values = keyed[rows, :], ones_t[:, rows]
        scores = dot(keys, queries[1], NN)
        scores = jnp.concatenate([scores[0:CHUNK], scores[CHUNK:WIDE] + bias[...]], axis=0)
        first = advance(dot(keys[0:CHUNK], queries[0], NN) + bias[...], values[:, 0:CHUNK], first)
        second = advance(scores, values, second)
        for index, (run_max, total) in enumerate((first, second)):
            row_sum = total[0:1]
            result = total[HEAD_DIM:128] / row_sum
            out_t[step + index] = result
            stats[step + index] = jnp.broadcast_to(run_max + jnp.log(row_sum), (8, ROWS))
            packed = jnp.concatenate([result[:, 0:128], result[:, 128:256]], axis=0).T
            send[2 * (step + index)] = bfloat(packed[0:64])
            send[2 * (step + index) + 1] = bfloat(packed[64:128])
        return 0

    lax.fori_loop(0, 4, one_pair, 0)
    stores += fetch(((out_t, out_hbm), (stats, stats_hbm)), done.at[pl.ds(3, 2)])
    for copy in stores:
        copy.wait()


def attend_back_kernel(
    scalars, lens_own, lens_other, pieces, keyed_hbm, keys_hbm, turned_hbm, out_hbm, stats_hbm, grads,
    send, send_core, keyed, key_rows, turned, out_t, stats, total, bias, done, done_small,
):
    small_copies = fetch(((out_hbm, out_t), (stats_hbm, stats)), done_small)

    def wide_copies(pair):
        rows = pl.ds(pl.multiple_of(pair * WIDE, WIDE), WIDE)
        places = (
            (keyed_hbm.at[rows, :], keyed.at[rows, :]),
            (keys_hbm.at[rows, :], key_rows.at[rows, :]),
            (turned_hbm.at[:, rows], turned.at[:, rows]),
        )
        return [
            pltpu.make_async_copy(source, target, done.at[pair, index])
            for index, (source, target) in enumerate(places)
        ]

    for pair in range(4):
        for copy in wide_copies(pair):
            copy.start()
    core = scalars[0]
    first_end, second_end = doc_ends(scalars, lens_own, lens_other, scalars[2] // HEADS)
    causal_bias(bias, core)

    def clear(source, _):
        rows = pl.ds(pl.multiple_of(source * ROWS, ROWS), ROWS)
        total[rows, :] = jnp.zeros((ROWS, 128), jnp.float32)
        return 0

    lax.fori_loop(0, 16, clear, 0)
    for copy in small_copies:
        copy.wait()
    low_half = low_lanes((128, 128))

    def load_block(step):
        query = packed_block(pieces, step)
        query_t = keyed_queries(packed_t(query), step, core, first_end, second_end)
        top = jnp.where(low_half, query, 0.0)
        bottom = jnp.where(low_half, pltpu.roll(query, HEAD_DIM, 1), 0.0)
        query = bfloat(jnp.concatenate([top, bottom], axis=0))
        grad = jnp.concatenate([f32(grads[2 * step]), f32(grads[2 * step + 1])], axis=0)
        grad_t = packed_t(grad)
        dots = jnp.sum(grad_t * out_t[step], axis=0, keepdims=True)
        grad_t = bfloat(jnp.concatenate([jnp.zeros_like(grad_t), grad_t], axis=0))
        top = jnp.where(low_half, 0.0, pltpu.roll(grad, HEAD_DIM, 1))
        bottom = jnp.where(low_half, 0.0, grad)
        grad = bfloat(jnp.concatenate([top, bottom], axis=0))
        return query_t, grad_t, query, grad, dots, stats[step][0:1]

    def one_pair(pair, _):
        step = 2 * pair
        for copy in wide_copies(pair):
            copy.wait()
        loaded = tuple(load_block(step + index) for index in range(2))

        def score_grads(index, scores, grad_weights):
            weights = jnp.exp2((scores - loaded[index][5]) * log2_e)
            return bfloat(weights * (grad_weights - loaded[index][4])), bfloat(weights)

        both = jnp.concatenate([loaded[0][2], loaded[0][3], loaded[1][2], loaded[1][3]], axis=0)

        def body(wide, state):
            rows = pl.ds(pl.multiple_of(wide * WIDE, WIDE), WIDE)
            marked, keys, keys_t = keyed[rows, :], key_rows[rows, :], turned[:, rows]
            scores = [dot(marked, item[0], NN) for item in loaded]
            grad_weights = [dot(keys, item[1], NN) for item in loaded]
            parts = [score_grads(index, scores[index], grad_weights[index]) for index in range(2)]
            total[rows, :] += dot(jnp.concatenate(parts[0] + parts[1], axis=1), both, NN)
            return tuple(state[index] + dot(keys_t, parts[index][0], NN) for index in range(2))

        start = jnp.zeros((128, ROWS), jnp.float32)
        low = doc_start(step * CHUNK, first_end, second_end) // WIDE
        first, second = lax.fori_loop(low, pair, body, (start, start))
        rows = pl.ds(pl.multiple_of(pair * WIDE, WIDE), CHUNK)
        rows_next = pl.ds(pl.multiple_of(pair * WIDE + CHUNK, CHUNK), CHUNK)
        marked, keys, keys_t = keyed[rows, :], key_rows[rows, :], turned[:, rows]
        marked_next, keys_next = keyed[rows_next, :], key_rows[rows_next, :]
        parts = (
            score_grads(
                0, dot(marked, loaded[0][0], NN) + bias[...], dot(keys, loaded[0][1], NN)
            ),
            score_grads(1, dot(marked, loaded[1][0], NN), dot(keys, loaded[1][1], NN)),
            score_grads(
                1, dot(marked_next, loaded[1][0], NN) + bias[...], dot(keys_next, loaded[1][1], NN)
            ),
        )
        total[rows, :] += dot(jnp.concatenate(parts[0] + parts[1], axis=1), both, NN)
        total[rows_next, :] += dot(jnp.concatenate(parts[2], axis=1), both[2 * ROWS : 4 * ROWS], NN)
        first = first + dot(keys_t, parts[0][0], NN)
        second = second + dot(keys_t, parts[1][0], NN)
        second = second + dot(turned[:, rows_next], parts[2][0], NN)
        for index, grad_query_t in enumerate((first, second)):
            turn = grad_query_t[0:HEAD_DIM] * HEAD_DIM**-0.5
            packed = jnp.concatenate([turn[:, 0:128], turn[:, 128:256]], axis=0).T
            send[2 * (step + index), HALF : HALF + 64, :] = bfloat(packed[0:64])
            send[2 * (step + index) + 1, HALF : HALF + 64, :] = bfloat(packed[64:128])
        return 0

    lax.fori_loop(0, 4, one_pair, 0)

    def emit(source, _):
        mine = pl.ds(pl.multiple_of(source * ROWS + core * HALF, HALF), HALF)
        away = pl.ds(pl.multiple_of(source * ROWS + (1 - core) * HALF, HALF), HALF)
        send[source, 0:HALF, :] = bfloat(total[mine, :])
        send_core[source] = bfloat(total[away, :])
        return 0

    lax.fori_loop(0, 16, emit, 0)


def middle_kernel(
    scalars, lens_own, lens_other, attended_in, tokens_in, cotangent_in, rows_in, later_in,
    later_other, small_in,
    out_own_hbm, out_away_hbm, send, grad_resid_hbm, small_hbm, grads_out,
    w_proj, grads, out_own, out_away, tokens, cotangent, rows_other, later_own, small, grad_resid_out, grad_small,
    done, fetched,
):
    pairs = (
        (later_in.at[:, :, 128:144, :], later_own.at[:, :, 128:144, :]),
        (tokens_in, tokens), (rows_in, rows_other), (small_in, small), (cotangent_in, cotangent),
        (later_in.at[:, :, 0:128, :], later_own.at[:, :, 0:128, :]),
    )
    copies = fetch(pairs, fetched)
    core = scalars[0]
    first_core = core == 0
    slots = (core, 1 - core)
    for copy in copies[0:5]:
        copy.wait()
    for owner in range(16):
        for lanes in range(4):
            columns = slice(lanes * 128, lanes * 128 + 128)
            own = later_own[lanes, owner, 128:144, :]
            other = later_other[lanes, owner, 128:144, :]
            first = owner * 32
            w_proj[first : first + 16, columns] = jnp.where(first_core, own, other)
            w_proj[first + 16 : first + 32, columns] = jnp.where(first_core, other, own)
    blocks = []
    for pair in range(4):
        parts = []
        for group in range(2):
            head = group * 8 + pair * 2
            parts += pair_pack(f32(attended_in[head]), f32(attended_in[head + 1]))
        blocks.append(jnp.concatenate(parts, axis=0))
    attended = bfloat(jnp.concatenate(blocks, axis=1))
    residual = f32(mixed_rows(core, tokens, rows_other[0])) + dot(attended, w_proj[...], NT) + small[4:5, :]
    unit, scale = normed(residual)
    hidden_in = bfloat(unit * small[5:6, :] + small[6:7, :])
    row = lax.broadcasted_iota(jnp.int32, (ROWS, 1), 0)
    position = (row & (HALF - 1)) + scalars[2] * ROWS + core * HALF
    _, first_live = doc_ends(scalars, lens_own, lens_other, 0)
    _, second_live = doc_ends(scalars, lens_own, lens_other, 1)
    live = position < jnp.where(row < HALF, first_live, second_live)
    grad_out = jnp.where(live, f32(mixed_rows(core, cotangent, rows_other[1])), 0.0)
    grad_out_b = bfloat(grad_out)

    copies[5].wait()

    def one_tile(tile, state):
        branch, grad_hidden_in = state
        owners = pl.ds(tile * 4, 4)
        own, other = (
            jnp.concatenate(
                [part[lanes, owners, 0:128, :].reshape(TILE, 128) for lanes in range(4)], axis=1
            )
            for part in (later_own, later_other)
        )
        up_rows = jnp.where(first_core, own, other)
        down_rows = jnp.where(first_core, other, own)
        hidden = dot(hidden_in, up_rows, NT) + small[pl.ds(8 + tile, 1), :]
        square = hidden * hidden
        bend = jnp.tanh(gelu_scale * hidden * (1.0 + gelu_cubic * square))
        half_open = 0.5 * (1.0 + bend)
        activated = bfloat(hidden * half_open)
        slope = half_open + 0.5 * hidden * (1.0 - bend * bend) * gelu_scale * (
            1.0 + 3.0 * gelu_cubic * square
        )
        branch = branch + dot(activated, down_rows, NN)
        grad_hidden = dot(grad_out_b, down_rows, NT) * slope
        grad_hidden_b = bfloat(grad_hidden)
        grad_hidden_in = grad_hidden_in + dot(grad_hidden_b, up_rows, NN)
        grad_small[pl.ds(8 + tile, 1), :] = jnp.sum(grad_hidden, axis=0, keepdims=True)
        grad_up = bfloat(dot(grad_hidden_b, hidden_in, TN))
        grad_down = bfloat(dot(activated, grad_out_b, TN))
        for lanes in range(4):
            columns = slice(lanes * 128, lanes * 128 + 128)
            grads[lanes, slots[0], owners, 0:128, :] = grad_up[:, columns].reshape(4, 128, 128)
            grads[lanes, slots[1], owners, 0:128, :] = grad_down[:, columns].reshape(4, 128, 128)
        here = grads.at[:, :, owners, 0:128, :]
        pltpu.make_async_copy(here, grads_out.at[:, :, owners, 0:128, :], done.at[tile]).start()
        return branch, grad_hidden_in

    zeros = jnp.zeros((ROWS, WIDTH), jnp.float32)
    branch, grad_hidden_in = lax.fori_loop(0, HIDDEN // TILE, one_tile, (zeros, zeros))
    out = bfloat(residual + branch + small[7:8, :])
    out_own[...] = jnp.where(first_core, out[0:HALF], out[HALF:ROWS])
    out_away[...] = jnp.where(first_core, out[HALF:ROWS], out[0:HALF])
    grad_norm, grad_gain, grad_bias = norm_back(unit, scale, small[5:6, :], grad_hidden_in)
    grad_resid = grad_out + grad_norm
    grad_resid_out[...] = grad_resid
    grad_resid_b = bfloat(grad_resid)
    grad_proj = bfloat(dot(grad_resid_b, attended, TN)).reshape(16, 32, WIDTH)
    for lanes in range(4):
        columns = slice(lanes * 128, lanes * 128 + 128)
        grads[lanes, slots[0], :, 128:144, :] = grad_proj[:, 0:16, columns]
        grads[lanes, slots[1], :, 128:144, :] = grad_proj[:, 16:32, columns]
    tail = pltpu.make_async_copy(
        grads.at[:, :, :, 128:144, :], grads_out.at[:, :, :, 128:144, :], done.at[4]
    )
    tail.start()
    grad_small[0:4, :] = jnp.zeros((4, WIDTH), jnp.float32)
    grad_small[12:16, :] = jnp.zeros((4, WIDTH), jnp.float32)
    grad_small[4:5, :] = jnp.sum(grad_resid, axis=0, keepdims=True)
    grad_small[5:6, :] = grad_gain
    grad_small[6:7, :] = grad_bias
    grad_small[7:8, :] = jnp.sum(grad_out, axis=0, keepdims=True)
    pairs = (
        (grad_resid_out, grad_resid_hbm), (grad_small, small_hbm),
        (out_own, out_own_hbm), (out_away, out_away_hbm),
    )
    stores = fetch(pairs, done.at[pl.ds(5, 4)])
    grad_attended = f32(bfloat(dot(grad_resid_b, w_proj[...], NN)))
    for pair in range(4):
        columns = slice(pair * 128, pair * 128 + 128)
        for group in range(2):
            first = group * HALF
            halves = grad_attended[first : first + 64, columns], grad_attended[
                first + 64 : first + 128, columns
            ]
            for offset, block in enumerate(pair_pack(*halves)):
                send[group * 8 + pair * 2 + offset] = bfloat(block)
    for tile in range(HIDDEN // TILE):
        owners = pl.ds(tile * 4, 4)
        pltpu.make_async_copy(
            grads.at[:, :, owners, 0:128, :], grads_out.at[:, :, owners, 0:128, :], done.at[tile]
        ).wait()
    tail.wait()
    for copy in stores:
        copy.wait()


def last_kernel(
    scalars, pieces, tokens_in, rows_in, weights_in, small_in, grad_resid_in, part_in,
    grad_in_own_hbm, grad_in_away_hbm, grads_own, grads_away,
    grad_in_own, grad_in_away, tokens, rows_other, weights, small, grad_resid, part_small, grads, done,
):
    pairs = (
        (weights_in, weights), (tokens_in, tokens), (rows_in, rows_other), (small_in, small),
        (grad_resid_in, grad_resid), (part_in, part_small),
    )
    copies = fetch(pairs, done)
    core = scalars[0]
    slots = (core, 1 - core)
    for copy in copies[1:4]:
        copy.wait()
    unit, scale = normed(f32(mixed_rows(core, tokens, rows_other[0])))
    hidden = bfloat(unit * small[0:1, :] + small[1:2, :])
    grad_hidden = jnp.zeros((ROWS, WIDTH), jnp.float32)
    parts_all = []
    sums_query = []
    sums_value = []

    def store(weight_grad, first_rows):
        for index in range(8):
            owner, row = divmod(first_rows[index // 4] + index % 4 * 16, 96)
            for lanes in range(4):
                place = slice(lanes * 48 + row % 48, lanes * 48 + row % 48 + 16)
                grads[slots[row // 48], owner, place, :] = weight_grad[
                    index * 16 : index * 16 + 16, lanes * 128 : lanes * 128 + 128
                ]

    for pair in range(4):
        parts = []
        for group in range(2):
            head = group * 8 + pair * 2
            blocks = (f32(pieces[head + offset, HALF : HALF + 64, :]) for offset in range(2))
            parts += pair_pack(*blocks)
        grad_query = jnp.concatenate(parts, axis=0)
        sums_query.append(jnp.sum(grad_query, axis=0, keepdims=True))
        grad_query = bfloat(grad_query)
        rows = slice(pair * 128, pair * 128 + 128)
        store(bfloat(dot(grad_query, hidden, TN)), (pair * 128, pair * 128 + HEAD_DIM))
        parts_all.append((grad_query, rows))
    for head in range(HEADS):
        both = jnp.concatenate([pieces[head, 0:HALF, :], pieces[8 + head, 0:HALF, :]], axis=0)
        sums_value.append(jnp.sum(f32(both), axis=0, keepdims=True))
        rows = slice(512 + head * 128, 512 + head * 128 + 128)
        first = 512 + head * HEAD_DIM
        store(bfloat(dot(both, hidden, TN)), (first, first + 512))
        parts_all.append((both, rows))
    for copy in copies[0:1] + copies[4:6]:
        copy.wait()
    for part, rows in parts_all:
        grad_hidden = grad_hidden + dot(part, weights[rows, :], NN)
    grad_norm, grad_gain, grad_bias = norm_back(unit, scale, small[0:1, :], grad_hidden)
    grad_in = bfloat(grad_resid[...] + grad_norm)
    grad_in_own[...] = jnp.where(core == 0, grad_in[0:HALF], grad_in[HALF:ROWS])
    grad_in_away[...] = jnp.where(core == 0, grad_in[HALF:ROWS], grad_in[0:HALF])
    pairs = ((grad_in_own, grad_in_own_hbm), (grad_in_away, grad_in_away_hbm))
    stores = fetch(pairs, done.at[pl.ds(6, 2)])
    row = lax.broadcasted_iota(jnp.int32, (16, 128), 0)
    lane = lax.broadcasted_iota(jnp.int32, (16, 128), 1)
    for block in range(4):
        columns = slice(block * 128, block * 128 + 128)
        first = pltpu.roll(jnp.broadcast_to(sums_value[2 * block], (16, 128)), HEAD_DIM, 1)
        second = jnp.broadcast_to(sums_value[2 * block + 1], (16, 128))
        value_row = jnp.where(lane < HEAD_DIM, first, second)
        total = part_small[:, columns]
        total = jnp.where(row == 0, grad_gain[:, columns], total)
        total = jnp.where(row == 1, grad_bias[:, columns], total)
        total = jnp.where(row == 2, sums_query[block], total)
        total = jnp.where(row == 3, value_row, total)
        for inside in range(4):
            owner = block * 4 + inside
            moved = pltpu.roll(total, 128 - inside * 32, 1) if inside else total
            grads[slots[0], owner, 192:208, :] = bfloat(moved)
            grads[slots[1], owner, 192:208, :] = jnp.zeros((16, 128), jnp.bfloat16)
    for owner in range(16):
        grads_own[owner] = grads[0, owner]
        grads_away[owner] = grads[1, owner]
    for copy in stores:
        copy.wait()


def combine_kernel(late_own, late_other, early_in, early_other, sums, early, done):
    copy = pltpu.make_async_copy(early_in.at[0], early, done)
    copy.start()
    for owner in range(16):
        sums[owner, 0:EARLY, :] = bfloat(f32(late_own[owner]) + f32(late_other[owner]))
    copy.wait()
    for owner in range(16):
        sums[owner, EARLY:BLOCK, :] = bfloat(f32(early[owner]) + f32(early_other[owner]))


def reduce_kernel(pieces, sums):
    total = bfloat(sum(f32(pieces[owner]) for owner in range(16)))
    for group in range(4):
        sums[group] = total


def adam_update(weight, grad_sum, mean_old, square_old, step_rate, decay_on):
    mean_new = beta_first * mean_old + (1.0 - beta_first) * grad_sum
    square_new = beta_second * square_old + (1.0 - beta_second) * grad_sum * grad_sum
    mean_hat = mean_new / (1.0 - beta_first**STEP)
    square_hat = square_new / (1.0 - beta_second**STEP)
    weight_new = weight - step_rate * (
        mean_hat / (jnp.sqrt(square_hat) + adam_epsilon) + decay_on * weight_decay * weight
    )
    return (weight_new, mean_new, square_new)


rates = ((0.04, 1.0), (1.0, 1.0), (0.04, 1.0), (0.02, 1.0), (2.0, 0.0))


def adam_kernel(scalars, grads_own, grads_other, *refs):
    core = scalars[0]
    for index in range(2):
        own, other = refs[15 + 2 * index], refs[16 + 2 * index]
        whole = refs[19 + index]
        whole[pl.ds(pl.multiple_of(core * HALF, HALF), HALF), :] = own[...]
        whole[pl.ds(pl.multiple_of((1 - core) * HALF, HALF), HALF), :] = other[...]
    first_core = scalars[0] == 0
    olds, news = refs[:15], refs[21:36]

    def picked(half, rows, part=None):
        own, other = (
            jnp.concatenate([f32(ref[lanes, rows, :]) for lanes in range(4)], axis=1)
            if part is None
            else sum(f32(ref[group, part * 48 + rows.start : part * 48 + rows.stop, :]) for group in range(4))
            for ref in (grads_own, grads_other)
        )
        return jnp.where(first_core, own, other) if half == 0 else jnp.where(first_core, other, own)

    def late(half, rows):
        return jnp.concatenate([picked(half, rows, part) for part in range(4)], axis=1)

    grad_qkv = jnp.concatenate([late(0, slice(0, 48)), late(1, slice(0, 48))], axis=0)
    grad_small = picked(0, slice(192, 208), 0)[0:12, 0:32]
    grad_up = picked(0, slice(208, 336)).T
    grad_down = picked(1, slice(208, 336))
    grad_proj = jnp.concatenate([picked(0, slice(336, 352)), picked(1, slice(336, 352))], axis=0)
    for index, grad in enumerate((grad_qkv, grad_proj, grad_up, grad_down, grad_small)):
        results = adam_update(
            olds[index][...], grad, olds[5 + index][...], olds[10 + index][...], *rates[index]
        )
        for group, result in enumerate(results):
            news[group * 5 + index][...] = result


def call(
    kernel, shapes, scratch=(), scalars=1, hbm_in=(), hbm_out=(), flops=0, moved=0, vmem_mib=20
):
    vmem = pl.BlockSpec(memory_space=pltpu.VMEM)
    hbm = pl.BlockSpec(memory_space=pltpu.HBM)
    smem = pl.BlockSpec(memory_space=pltpu.SMEM)

    def run(*args):
        specs = [
            smem if index < scalars else hbm if index in hbm_in else vmem
            for index in range(len(args))
        ]
        args = [
            pltpu.with_memory_space_constraint(arg, pltpu.HBM) if index in hbm_in else arg
            for index, arg in enumerate(args)
        ]
        return pl.pallas_call(
            kernel,
            out_shape=[
                pltpu.HBM(shape, kind) if index in hbm_out else jax.ShapeDtypeStruct(shape, kind)
                for index, (shape, kind) in enumerate(shapes)
            ],
            in_specs=specs,
            out_specs=[hbm if index in hbm_out else vmem for index in range(len(shapes))],
            scratch_shapes=list(scratch),
            compiler_params=pltpu.CompilerParams(vmem_limit_bytes=vmem_mib * 1024 * 1024),
            cost_estimate=pl.CostEstimate(flops=flops, bytes_accessed=moved, transcendentals=0),
        )(*args)

    return run


def exchange(values):
    return lax.all_to_all(values, CTX, 0, 0, tiled=True)


def swap_cores(values):
    return lax.ppermute(values, "c", [(0, 1), (1, 0)])


def on_device(
    tokens, cotangent, lengths,
    w_qkv, w_proj, w_up, w_down, w_small,
    mean_qkv, mean_proj, mean_up, mean_down, mean_small,
    square_qkv, square_proj, square_up, square_down, square_small,
):
    kind = jnp.bfloat16
    core = lax.axis_index("c")
    place = lax.axis_index("z") * 4 + lax.axis_index("y")
    scalars = jnp.stack([core, lax.axis_index("x"), place]).astype(jnp.int32)
    lens_other = swap_cores(lengths)
    turned_olds = (
        w_qkv.T, w_proj.T, w_up, w_down, w_small,
        mean_qkv.T, mean_proj.T, mean_up, mean_down, mean_small,
        square_qkv.T, square_proj.T, square_up, square_down, square_small,
    )
    single = jnp.float32
    rows_kind = pltpu.VMEM((ROWS, WIDTH), kind)
    pair_kind = pltpu.VMEM((2, HALF, WIDTH), kind)
    small_kind = pltpu.VMEM((16, WIDTH), single)

    send, rows_away = call(
        gather_kernel,
        [((16, BLOCK, 128), kind), ((2, HALF, WIDTH), kind)],
        [
            pair_kind,
            pltpu.VMEM((96, WIDTH), single),
            pltpu.VMEM((32, WIDTH), single),
            pltpu.VMEM((WIDTH, 128), single),
            pltpu.VMEM((128, WIDTH), single),
            pltpu.VMEM((12, 32), single),
            pltpu.VMEM((BLOCK, 128), kind),
            pltpu.VMEM((16, 128), single),
            pltpu.SemaphoreType.DMA((7,)),
        ],
        hbm_in=range(1, 8), moved=3 << 20,
    )(scalars, tokens, cotangent, *turned_olds[0:5])
    rows_other = swap_cores(rows_away)
    first_own = exchange(send)
    first_other = swap_cores(first_own[:, 0:EARLY])
    later_own = lax.all_gather(first_own[:, EARLY:BLOCK], "x", axis=0, tiled=False)
    first_other, lens_other = lax.optimization_barrier((first_other, lens_other))

    send, weights, small = call(
        qkv_kernel,
        [((16, 192, 128), kind), ((1536, WIDTH), kind), ((16, WIDTH), single)],
        [
            rows_kind, pltpu.VMEM((1536, WIDTH), kind), small_kind,
            pltpu.SemaphoreType.DMA((1,)), pltpu.SemaphoreType.DMA((2,)),
        ],
        hbm_in=(1,), hbm_out=(1, 2), flops=2 * 256 * 512 * 1536, moved=6 << 20,
    )(scalars, tokens, rows_other, first_own, first_other)
    pieces = exchange(send)
    kept = [
        ((4096, 128), kind), ((4096, 128), kind), ((128, 4096), kind),
        ((8, HEAD_DIM, ROWS), single), ((8, 8, ROWS), single),
    ]
    kept_scratch = [pltpu.VMEM(*item) for item in kept]
    send, *kept_values = call(
        attend_kernel,
        [((16, 64, 128), kind)] + kept,
        kept_scratch
        + [
            pltpu.VMEM((128, 4096), kind), pltpu.VMEM((CHUNK, ROWS), single),
            pltpu.SemaphoreType.DMA((5,)),
        ],
        scalars=3, hbm_out=(1, 2, 3, 4, 5), vmem_mib=28, flops=36 * 512 * 256 * 2 * 256 * 2, moved=4 << 20,
    )(scalars, lengths, lens_other, pieces, swap_cores(pieces))
    send, later_own = lax.optimization_barrier((send, later_own))
    later_other = swap_cores(later_own)
    attended = exchange(send)
    out_own, out_away, send, grad_resid, part_small, early = call(
        middle_kernel,
        [
            ((HALF, WIDTH), kind),
            ((HALF, WIDTH), kind),
            ((16, 64, 128), kind),
            ((ROWS, WIDTH), single),
            ((16, WIDTH), single),
            ((4, 2, 16, 144, 128), kind),
        ],
        [
            pltpu.VMEM((WIDTH, WIDTH), kind),
            pltpu.VMEM((4, 2, 16, 144, 128), kind),
            pltpu.VMEM((HALF, WIDTH), kind), pltpu.VMEM((HALF, WIDTH), kind),
            rows_kind, rows_kind, pair_kind,
            pltpu.VMEM((4, 16, 144, 128), kind),
            small_kind,
            pltpu.VMEM((ROWS, WIDTH), single),
            small_kind,
            pltpu.SemaphoreType.DMA((9,)),
            pltpu.SemaphoreType.DMA((6,)),
        ],
        scalars=3, hbm_in=(4, 5, 6, 7, 9), hbm_out=(0, 1, 3, 4, 5),
        flops=2 * 256 * 512 * (3 * 512 + 6 * 2048), moved=12 << 20, vmem_mib=32,
    )(
        scalars, lengths, lens_other, attended, tokens, cotangent, rows_other,
        later_own, later_other, small,
    )
    early = lax.psum_scatter(
        early.reshape(4 * 2 * 16 * 144, 128), "x", scatter_dimension=0, tiled=True
    ).reshape(2, 16, 144, 128)
    grads = exchange(send)
    send, send_core = call(
        attend_back_kernel,
        [((16, 192, 128), kind), ((16, HALF, 128), kind)],
        kept_scratch
        + [
            pltpu.VMEM((4096, 128), single), pltpu.VMEM((CHUNK, ROWS), single),
            pltpu.SemaphoreType.DMA((4, 3)), pltpu.SemaphoreType.DMA((2,)),
        ],
        scalars=3, hbm_in=(4, 5, 6, 7, 8), vmem_mib=32, flops=36 * 512 * 256 * 2 * 256 * 5, moved=5 << 20,
    )(scalars, lengths, lens_other, pieces, *kept_values, grads)
    whole = f32(send[:, 0:HALF]) + f32(swap_cores(send_core))
    pieces = exchange(jnp.concatenate([bfloat(whole), send[:, HALF:]], axis=1))
    grad_in_own, grad_in_away, late_own, late_away = call(
        last_kernel,
        [((HALF, WIDTH), kind), ((HALF, WIDTH), kind)] + [((16, EARLY, 128), kind)] * 2,
        [
            pltpu.VMEM((HALF, WIDTH), kind), pltpu.VMEM((HALF, WIDTH), kind),
            rows_kind, pair_kind, pltpu.VMEM((1536, WIDTH), kind), small_kind,
            pltpu.VMEM((ROWS, WIDTH), single), small_kind,
            pltpu.VMEM((2, 16, EARLY, 128), kind), pltpu.SemaphoreType.DMA((8,)),
        ],
        hbm_in=(2, 3, 4, 5, 6, 7), hbm_out=(0, 1), flops=4 * 256 * 512 * 1536, moved=8 << 20,
    )(scalars, pieces, tokens, rows_other, weights, small, grad_resid, part_small)

    late_other, out_other, grad_in_other = lax.optimization_barrier(
        (swap_cores(late_away), swap_cores(out_away), swap_cores(grad_in_away))
    )
    (sums,) = call(
        combine_kernel, [((16, BLOCK, 128), kind)],
        [pltpu.VMEM((16, 144, 128), kind), pltpu.SemaphoreType.DMA],
        scalars=0, hbm_in=(2,), moved=4 << 20,
    )(
        late_own, late_other, early, swap_cores(early[1])
    )
    (sums,) = call(reduce_kernel, [((4, BLOCK, 128), kind)], scalars=0, moved=2 << 20)(
        exchange(sums)
    )
    grads_own = lax.all_to_all(sums, "x", 0, 0, tiled=True)
    out, grad_in, *news = call(
        adam_kernel,
        [((ROWS, WIDTH), kind)] * 2 + [(old.shape, single) for old in turned_olds],
        moved=8 << 20,
    )(
        scalars, grads_own, swap_cores(grads_own), *turned_olds,
        out_own, out_other, grad_in_own, grad_in_other,
    )
    news = [new.T if index % 5 < 2 else new for index, new in enumerate(news)]
    return (out, grad_in, *news)


def solution(mesh):
    fine = Mesh(mesh.devices.reshape(4, 2, 4, 4), ("x", "c", "z", "y"))
    rows = P(("x", "c", "z", "y"), None)
    columns = P(None, CTX)
    shards = (columns, columns, columns, P(CTX, None), columns)
    return jax.shard_map(
        on_device,
        mesh=fine,
        in_specs=(rows, rows, P(("x", "c"), None)) + shards * 3,
        out_specs=(rows, rows) + shards * 3,
        check_vma=False,
    )
```

```python
import functools
import jax
import jax.numpy as jnp
from jax import lax
from jax.experimental import pallas as pl
from jax.experimental.pallas import tpu as pltpu
from jax.sharding import Mesh, PartitionSpec as P

HEADS = 8
HEAD_DIM = 64
STEP = 10
WIDTH = 512
HIDDEN = 2048
ROWS = 256
HALF = 128
CHUNK = 512
TILE = 512
WIDE = 1024
EARLY = 208
BLOCK = 352

epsilon = 1e-05
negative_big = -1e30
beta_first = 0.9
beta_second = 0.95
adam_epsilon = 1e-08
weight_decay = 0.1
gelu_scale = 0.7978845608028654
gelu_cubic = 0.044715
log2_e = 1.4426950408889634

NN = (((1,), (0,)), ((), ()))
NT = (((1,), (1,)), ((), ()))
TN = (((0,), (0,)), ((), ()))
CTX = ("z", "y")


def dot(left, right, dims):
    return lax.dot_general(left, right, dims, preferred_element_type=jnp.float32)


def bfloat(values):
    return values.astype(jnp.bfloat16)


def f32(values):
    return values.astype(jnp.float32)


def normed(values):
    center = values - jnp.mean(values, axis=-1, keepdims=True)
    spread = jnp.mean(center * center, axis=-1, keepdims=True)
    scale = lax.rsqrt(spread + epsilon)
    return center * scale, scale


def norm_back(unit, scale, gain, grad):
    scaled = grad * gain
    first = jnp.mean(scaled, axis=-1, keepdims=True)
    second = jnp.mean(scaled * unit, axis=-1, keepdims=True)
    grad_values = (scaled - first - unit * second) * scale
    grad_gain = jnp.sum(grad * unit, axis=0, keepdims=True)
    grad_bias = jnp.sum(grad, axis=0, keepdims=True)
    return grad_values, grad_gain, grad_bias


def low_lanes(shape):
    return lax.broadcasted_iota(jnp.int32, shape, 1) < HEAD_DIM


def fetch(pairs, done):
    copies = [
        pltpu.make_async_copy(source, target, done.at[index])
        for index, (source, target) in enumerate(pairs)
    ]
    for copy in copies:
        copy.start()
    return copies


def mixed_rows(core, own, other):
    keep = own[pl.ds(pl.multiple_of(core * HALF, HALF), HALF), :]
    first = jnp.where(core == 0, keep, other)
    second = jnp.where(core == 0, other, keep)
    return jnp.concatenate([first, second], axis=0)


def pair_pack(top, bottom):
    low = low_lanes(top.shape)
    first = jnp.where(low, top, pltpu.roll(bottom, HEAD_DIM, 1))
    second = jnp.where(low, pltpu.roll(top, HEAD_DIM, 1), bottom)
    return first, second


def gather_kernel(
    scalars, tokens_in, cotangent_in, qkv_in, proj_in, up_in, down_in, small_in, send, rows_out,
    rows, qkv, proj, up, down, small, block, small_block, done,
):
    core = scalars[0]
    lanes = pl.ds(pl.multiple_of(scalars[1] * 128, 128), 128)
    away = pl.ds(pl.multiple_of((1 - core) * HALF, HALF), HALF)
    pairs = (
        (qkv_in.at[pl.ds(pl.multiple_of(core * 48, 16), 48)], qkv),
        (up_in.at[lanes], up),
        (down_in.at[:, lanes], down),
        (proj_in.at[pl.ds(pl.multiple_of(core * 16, 16), 16), lanes], proj),
        (small_in, small),
        (tokens_in.at[away], rows.at[0]), (cotangent_in.at[away], rows.at[1]),
    )
    for copy in fetch(pairs, done):
        copy.wait()
    first_core = core == 0
    rows_out[...] = rows[...]
    small_block[...] = jnp.zeros((16, 128), jnp.float32)
    small_block[0:12, 0:32] = small[...]
    for part in range(4):
        columns = slice(part * 128, part * 128 + 128)
        block[part * 48 : part * 48 + 48, :] = bfloat(qkv[:, columns])
    block[192:208, :] = bfloat(small_block[...])
    half = jnp.where(first_core, up[...].T, down[...])
    block[208:336, :] = bfloat(half)
    block[336:352, :] = bfloat(proj[...])
    for owner in range(16):
        send[owner] = block[...]


def qkv_kernel(
    scalars, tokens_in, rows_other, wide_own, wide_other, send, weights, small_out,
    tokens, small, done, stored,
):
    copies = fetch(((tokens_in, tokens),), done)
    first_core = scalars[0] == 0

    def wide(half, owner, part, first):
        rows = slice(part * 48 + first, part * 48 + first + 16)
        own, other = wide_own[owner, rows, :], wide_other[owner, rows, :]
        return jnp.where(first_core, own, other) if half == 0 else jnp.where(first_core, other, own)

    for owner in range(16):
        for piece in range(6):
            first = owner * 96 + piece * 16
            part, offset = divmod(first, 512)
            if part == 0:
                target = first
            else:
                head, inside = divmod(offset, HEAD_DIM)
                target = 512 + head * 128 + (part - 1) * HEAD_DIM + inside
            half, row = divmod(piece * 16, 48)
            for lanes in range(4):
                weights[target : target + 16, lanes * 128 : lanes * 128 + 128] = wide(
                    half, owner, lanes, row
                )
    lane = lax.broadcasted_iota(jnp.int32, (16, 128), 1)
    for block in range(4):
        total = jnp.zeros((16, 128), jnp.float32)
        for inside in range(4):
            piece = f32(wide_own[block * 4 + inside, 192:208, :])
            moved = pltpu.roll(piece, inside * 32, 1) if inside else piece
            keep = (lane >= inside * 32) & (lane < inside * 32 + 32)
            total = jnp.where(keep, moved, total)
        small[:, block * 128 : block * 128 + 128] = total
    stores = fetch(((small, small_out),), stored)
    for copy in copies:
        copy.wait()
    unit, _ = normed(f32(mixed_rows(scalars[0], tokens, rows_other[0])))
    hidden = bfloat(unit * small[0:1, :] + small[1:2, :])
    for pair in range(4):
        columns = slice(pair * 128, pair * 128 + 128)
        query = dot(hidden, weights[columns, :], NT) + small[2:3, columns]
        query = f32(bfloat(query)) * HEAD_DIM**-0.5
        for group in range(2):
            rows = group * HALF
            blocks = pair_pack(query[rows : rows + 64], query[rows + 64 : rows + 128])
            for offset, block in enumerate(blocks):
                send[group * 8 + pair * 2 + offset, HALF : HALF + 64, :] = bfloat(block)
    for head in range(HEADS):
        rows = slice(512 + head * 128, 512 + head * 128 + 128)
        bias = small[3:4, (head // 2) * 128 : (head // 2) * 128 + 128]
        if head % 2 == 0:
            bias = pltpu.roll(jnp.broadcast_to(bias, (8, 128)), HEAD_DIM, 1)[0:1]
        bias = jnp.where(low_lanes((1, 128)), 0.0, bias)
        both = bfloat(dot(hidden, weights[rows, :], NT) + bias)
        send[head, 0:HALF, :] = both[0:HALF]
        send[8 + head, 0:HALF, :] = both[HALF:ROWS]
    for copy in stores:
        copy.wait()


def query_rows(core):
    lane = lax.broadcasted_iota(jnp.int32, (1, ROWS), 1)
    return ((lane & 64) << 2) + core * HALF + (lane & 63) + ((lane & 128) >> 1)


def doc_of(position, first_end, second_end):
    return (position >= first_end).astype(jnp.int32) + (position >= second_end).astype(jnp.int32)


def doc_start(position, first_end, second_end):
    return jnp.where(
        position >= second_end, second_end, jnp.where(position >= first_end, first_end, 0)
    )


def packed_t(block):
    turned = block.T
    return jnp.concatenate([turned[0:HEAD_DIM], turned[HEAD_DIM:128]], axis=1)


def causal_bias(bias, core):
    key = lax.broadcasted_iota(jnp.int32, (CHUNK, ROWS), 0)
    bias[...] = jnp.where(key <= query_rows(core), 0.0, negative_big)


def keyed_rows(rows, first, first_end, second_end):
    lane = lax.broadcasted_iota(jnp.int32, (ROWS, 128), 1)
    row = lax.broadcasted_iota(jnp.int32, (ROWS, 128), 0) + first
    mark = lane - HEAD_DIM == doc_of(row, first_end, second_end)
    return bfloat(jnp.where(lane < HEAD_DIM, rows, jnp.where(mark, 1.0, 0.0)))


def keyed_queries(query_t, step, core, first_end, second_end):
    position = query_rows(core) + step * CHUNK
    line = lax.broadcasted_iota(jnp.int32, (HEAD_DIM, ROWS), 0)
    other = (line < 3) & (line != doc_of(position, first_end, second_end))
    penalty = jnp.where(other, negative_big, 0.0)
    return bfloat(jnp.concatenate([query_t, penalty], axis=0))


def packed_block(pieces, step):
    return jnp.concatenate(
        [f32(pieces[2 * step, HALF : HALF + 64, :]), f32(pieces[2 * step + 1, HALF : HALF + 64, :])],
        axis=0,
    )


def doc_ends(scalars, lens_own, lens_other, group):
    own = scalars[0] == group
    first = jnp.where(own, lens_own[0, 0], lens_other[0, 0])
    return first, first + jnp.where(own, lens_own[0, 1], lens_other[0, 1])


def attend_kernel(
    scalars, lens_own, lens_other, pieces, others,
    send, keyed_hbm, keys_hbm, turned_hbm, out_hbm, stats_hbm,
    keyed, keys_out, turned_out, out_t, stats, ones_t, bias, done,
):
    core = scalars[0]
    first_end, second_end = doc_ends(scalars, lens_own, lens_other, scalars[2] // HEADS)
    causal_bias(bias, core)

    def turn(source, _):
        columns = pl.ds(pl.multiple_of(source * ROWS, ROWS), ROWS)
        own, other = pieces[source, 0:HALF, :], others[source, 0:HALF, :]
        first, second = jnp.where(core == 0, own, other), jnp.where(core == 0, other, own)
        keys = jnp.concatenate([first, second], axis=0)
        keys_out[columns, :] = keys
        keys = f32(keys)
        keyed[columns, :] = keyed_rows(keys, source * ROWS, first_end, second_end)
        turned = keys.T
        turned_out[:, columns] = bfloat(turned)
        row = lax.broadcasted_iota(jnp.int32, (128, ROWS), 0)
        ones_t[:, columns] = bfloat(jnp.where(row < HEAD_DIM, 1.0, turned))
        return 0

    lax.fori_loop(0, 16, turn, 0, unroll=4)
    stores = fetch(((keyed, keyed_hbm), (keys_out, keys_hbm), (turned_out, turned_hbm)), done)

    def one_pair(pair, _):
        step = 2 * pair
        queries = tuple(
            keyed_queries(
                packed_t(packed_block(pieces, step + index)), step + index, core, first_end, second_end
            )
            for index in range(2)
        )

        def advance(scores, values, state):
            run_max, total = state
            new_max = jnp.maximum(run_max, jnp.max(scores, axis=0, keepdims=True))
            weights = bfloat(jnp.exp2((scores - new_max) * log2_e))
            scale = jnp.exp2((run_max - new_max) * log2_e)
            return new_max, total * scale + dot(values, weights, NN)

        def body(wide, state):
            rows = pl.ds(pl.multiple_of(wide * WIDE, WIDE), WIDE)
            keys, values = keyed[rows, :], ones_t[:, rows]
            scores = [dot(keys, query, NN) for query in queries]
            return tuple(advance(scores[index], values, state[index]) for index in range(2))

        start = (
            jnp.full((1, ROWS), negative_big, jnp.float32),
            jnp.zeros((128, ROWS), jnp.float32),
        )
        low = doc_start(step * CHUNK, first_end, second_end) // WIDE
        first, second = lax.fori_loop(low, pair, body, (start, start))
        rows = pl.ds(pl.multiple_of(pair * WIDE, WIDE), WIDE)
        keys, values = keyed[rows, :], ones_t[:, rows]
        scores = dot(keys, queries[1], NN)
        scores = jnp.concatenate([scores[0:CHUNK], scores[CHUNK:WIDE] + bias[...]], axis=0)
        first = advance(dot(keys[0:CHUNK], queries[0], NN) + bias[...], values[:, 0:CHUNK], first)
        second = advance(scores, values, second)
        for index, (run_max, total) in enumerate((first, second)):
            row_sum = total[0:1]
            result = total[HEAD_DIM:128] / row_sum
            out_t[step + index] = result
            stats[step + index] = jnp.broadcast_to(run_max + jnp.log(row_sum), (8, ROWS))
            packed = jnp.concatenate([result[:, 0:128], result[:, 128:256]], axis=0).T
            send[2 * (step + index)] = bfloat(packed[0:64])
            send[2 * (step + index) + 1] = bfloat(packed[64:128])
        return 0

    lax.fori_loop(0, 4, one_pair, 0)
    stores += fetch(((out_t, out_hbm), (stats, stats_hbm)), done.at[pl.ds(3, 2)])
    for copy in stores:
        copy.wait()


def attend_back_kernel(
    scalars, lens_own, lens_other, pieces, keyed_hbm, keys_hbm, turned_hbm, out_hbm, stats_hbm, grads,
    send, send_core, keyed, key_rows, turned, out_t, stats, total, bias, done, done_small,
):
    small_copies = fetch(((out_hbm, out_t), (stats_hbm, stats)), done_small)

    def wide_copies(pair):
        rows = pl.ds(pl.multiple_of(pair * WIDE, WIDE), WIDE)
        places = (
            (keyed_hbm.at[rows, :], keyed.at[rows, :]),
            (keys_hbm.at[rows, :], key_rows.at[rows, :]),
            (turned_hbm.at[:, rows], turned.at[:, rows]),
        )
        return [
            pltpu.make_async_copy(source, target, done.at[pair, index])
            for index, (source, target) in enumerate(places)
        ]

    for pair in range(4):
        for copy in wide_copies(pair):
            copy.start()
    core = scalars[0]
    first_end, second_end = doc_ends(scalars, lens_own, lens_other, scalars[2] // HEADS)
    causal_bias(bias, core)

    def clear(source, _):
        rows = pl.ds(pl.multiple_of(source * ROWS, ROWS), ROWS)
        total[rows, :] = jnp.zeros((ROWS, 128), jnp.float32)
        return 0

    lax.fori_loop(0, 16, clear, 0)
    for copy in small_copies:
        copy.wait()
    low_half = low_lanes((128, 128))

    def load_block(step):
        query = packed_block(pieces, step)
        query_t = keyed_queries(packed_t(query), step, core, first_end, second_end)
        top = jnp.where(low_half, query, 0.0)
        bottom = jnp.where(low_half, pltpu.roll(query, HEAD_DIM, 1), 0.0)
        query = bfloat(jnp.concatenate([top, bottom], axis=0))
        grad = jnp.concatenate([f32(grads[2 * step]), f32(grads[2 * step + 1])], axis=0)
        grad_t = packed_t(grad)
        dots = jnp.sum(grad_t * out_t[step], axis=0, keepdims=True)
        grad_t = bfloat(jnp.concatenate([jnp.zeros_like(grad_t), grad_t], axis=0))
        top = jnp.where(low_half, 0.0, pltpu.roll(grad, HEAD_DIM, 1))
        bottom = jnp.where(low_half, 0.0, grad)
        grad = bfloat(jnp.concatenate([top, bottom], axis=0))
        return query_t, grad_t, query, grad, dots, stats[step][0:1]

    def one_pair(pair, _):
        step = 2 * pair
        for copy in wide_copies(pair):
            copy.wait()
        loaded = tuple(load_block(step + index) for index in range(2))

        def score_grads(index, scores, grad_weights):
            weights = jnp.exp2((scores - loaded[index][5]) * log2_e)
            return bfloat(weights * (grad_weights - loaded[index][4])), bfloat(weights)

        both = jnp.concatenate([loaded[0][2], loaded[0][3], loaded[1][2], loaded[1][3]], axis=0)

        def body(wide, state):
            rows = pl.ds(pl.multiple_of(wide * WIDE, WIDE), WIDE)
            marked, keys, keys_t = keyed[rows, :], key_rows[rows, :], turned[:, rows]
            scores = [dot(marked, item[0], NN) for item in loaded]
            grad_weights = [dot(keys, item[1], NN) for item in loaded]
            parts = [score_grads(index, scores[index], grad_weights[index]) for index in range(2)]
            total[rows, :] += dot(jnp.concatenate(parts[0] + parts[1], axis=1), both, NN)
            return tuple(state[index] + dot(keys_t, parts[index][0], NN) for index in range(2))

        start = jnp.zeros((128, ROWS), jnp.float32)
        low = doc_start(step * CHUNK, first_end, second_end) // WIDE
        first, second = lax.fori_loop(low, pair, body, (start, start))
        rows = pl.ds(pl.multiple_of(pair * WIDE, WIDE), CHUNK)
        rows_next = pl.ds(pl.multiple_of(pair * WIDE + CHUNK, CHUNK), CHUNK)
        marked, keys, keys_t = keyed[rows, :], key_rows[rows, :], turned[:, rows]
        marked_next, keys_next = keyed[rows_next, :], key_rows[rows_next, :]
        parts = (
            score_grads(
                0, dot(marked, loaded[0][0], NN) + bias[...], dot(keys, loaded[0][1], NN)
            ),
            score_grads(1, dot(marked, loaded[1][0], NN), dot(keys, loaded[1][1], NN)),
            score_grads(
                1, dot(marked_next, loaded[1][0], NN) + bias[...], dot(keys_next, loaded[1][1], NN)
            ),
        )
        total[rows, :] += dot(jnp.concatenate(parts[0] + parts[1], axis=1), both, NN)
        total[rows_next, :] += dot(jnp.concatenate(parts[2], axis=1), both[2 * ROWS : 4 * ROWS], NN)
        first = first + dot(keys_t, parts[0][0], NN)
        second = second + dot(keys_t, parts[1][0], NN)
        second = second + dot(turned[:, rows_next], parts[2][0], NN)
        for index, grad_query_t in enumerate((first, second)):
            turn = grad_query_t[0:HEAD_DIM] * HEAD_DIM**-0.5
            packed = jnp.concatenate([turn[:, 0:128], turn[:, 128:256]], axis=0).T
            send[2 * (step + index), HALF : HALF + 64, :] = bfloat(packed[0:64])
            send[2 * (step + index) + 1, HALF : HALF + 64, :] = bfloat(packed[64:128])
        return 0

    lax.fori_loop(0, 4, one_pair, 0)

    def emit(source, _):
        mine = pl.ds(pl.multiple_of(source * ROWS + core * HALF, HALF), HALF)
        away = pl.ds(pl.multiple_of(source * ROWS + (1 - core) * HALF, HALF), HALF)
        send[source, 0:HALF, :] = bfloat(total[mine, :])
        send_core[source] = bfloat(total[away, :])
        return 0

    lax.fori_loop(0, 16, emit, 0)


def middle_kernel(
    scalars, lens_own, lens_other, attended_in, tokens_in, cotangent_in, rows_in, later_in,
    later_other, small_in,
    out_own_hbm, out_away_hbm, send, grad_resid_out, small_hbm, grads_out,
    w_proj, grads, out_own, out_away, tokens, cotangent, rows_other, later_own, small, grad_small,
    done, fetched,
):
    pairs = (
        (later_in.at[:, :, 128:144, :], later_own.at[:, :, 128:144, :]),
        (tokens_in, tokens), (rows_in, rows_other), (small_in, small), (cotangent_in, cotangent),
        (later_in.at[:, :, 0:128, :], later_own.at[:, :, 0:128, :]),
    )
    copies = fetch(pairs, fetched)
    core = scalars[0]
    first_core = core == 0
    slots = (core, 1 - core)
    for copy in copies[0:5]:
        copy.wait()
    for owner in range(16):
        for lanes in range(4):
            columns = slice(lanes * 128, lanes * 128 + 128)
            own = later_own[lanes, owner, 128:144, :]
            other = later_other[lanes, owner, 128:144, :]
            first = owner * 32
            w_proj[first : first + 16, columns] = jnp.where(first_core, own, other)
            w_proj[first + 16 : first + 32, columns] = jnp.where(first_core, other, own)
    blocks = []
    for pair in range(4):
        parts = []
        for group in range(2):
            head = group * 8 + pair * 2
            parts += pair_pack(f32(attended_in[head]), f32(attended_in[head + 1]))
        blocks.append(jnp.concatenate(parts, axis=0))
    attended = bfloat(jnp.concatenate(blocks, axis=1))
    residual = f32(mixed_rows(core, tokens, rows_other[0])) + dot(attended, w_proj[...], NT) + small[4:5, :]
    unit, scale = normed(residual)
    hidden_in = bfloat(unit * small[5:6, :] + small[6:7, :])
    row = lax.broadcasted_iota(jnp.int32, (ROWS, 1), 0)
    position = (row & (HALF - 1)) + scalars[2] * ROWS + core * HALF
    _, first_live = doc_ends(scalars, lens_own, lens_other, 0)
    _, second_live = doc_ends(scalars, lens_own, lens_other, 1)
    live = position < jnp.where(row < HALF, first_live, second_live)
    grad_out = jnp.where(live, f32(mixed_rows(core, cotangent, rows_other[1])), 0.0)
    grad_out_b = bfloat(grad_out)

    copies[5].wait()

    def one_tile(tile, state):
        branch, grad_hidden_in = state
        owners = pl.ds(tile * 4, 4)
        own, other = (
            jnp.concatenate(
                [part[lanes, owners, 0:128, :].reshape(TILE, 128) for lanes in range(4)], axis=1
            )
            for part in (later_own, later_other)
        )
        up_rows = jnp.where(first_core, own, other)
        down_rows = jnp.where(first_core, other, own)
        hidden = dot(hidden_in, up_rows, NT) + small[pl.ds(8 + tile, 1), :]
        square = hidden * hidden
        bend = jnp.tanh(gelu_scale * hidden * (1.0 + gelu_cubic * square))
        half_open = 0.5 * (1.0 + bend)
        activated = bfloat(hidden * half_open)
        slope = half_open + 0.5 * hidden * (1.0 - bend * bend) * gelu_scale * (
            1.0 + 3.0 * gelu_cubic * square
        )
        branch = branch + dot(activated, down_rows, NN)
        grad_hidden = dot(grad_out_b, down_rows, NT) * slope
        grad_hidden_b = bfloat(grad_hidden)
        grad_hidden_in = grad_hidden_in + dot(grad_hidden_b, up_rows, NN)
        grad_small[pl.ds(8 + tile, 1), :] = jnp.sum(grad_hidden, axis=0, keepdims=True)
        grad_up = bfloat(dot(grad_hidden_b, hidden_in, TN))
        grad_down = bfloat(dot(activated, grad_out_b, TN))
        for lanes in range(4):
            columns = slice(lanes * 128, lanes * 128 + 128)
            grads[lanes, slots[0], owners, 0:128, :] = grad_up[:, columns].reshape(4, 128, 128)
            grads[lanes, slots[1], owners, 0:128, :] = grad_down[:, columns].reshape(4, 128, 128)
        here = grads.at[:, :, owners, 0:128, :]
        pltpu.make_async_copy(here, grads_out.at[:, :, owners, 0:128, :], done.at[tile]).start()
        return branch, grad_hidden_in

    zeros = jnp.zeros((ROWS, WIDTH), jnp.float32)
    branch, grad_hidden_in = lax.fori_loop(0, HIDDEN // TILE, one_tile, (zeros, zeros))
    out = bfloat(residual + branch + small[7:8, :])
    out_own[...] = jnp.where(first_core, out[0:HALF], out[HALF:ROWS])
    out_away[...] = jnp.where(first_core, out[HALF:ROWS], out[0:HALF])
    grad_norm, grad_gain, grad_bias = norm_back(unit, scale, small[5:6, :], grad_hidden_in)
    grad_resid = grad_out + grad_norm
    grad_resid_out[...] = grad_resid
    grad_resid_b = bfloat(grad_resid)
    grad_proj = bfloat(dot(grad_resid_b, attended, TN)).reshape(16, 32, WIDTH)
    for lanes in range(4):
        columns = slice(lanes * 128, lanes * 128 + 128)
        grads[lanes, slots[0], :, 128:144, :] = grad_proj[:, 0:16, columns]
        grads[lanes, slots[1], :, 128:144, :] = grad_proj[:, 16:32, columns]
    tail = pltpu.make_async_copy(
        grads.at[:, :, :, 128:144, :], grads_out.at[:, :, :, 128:144, :], done.at[4]
    )
    tail.start()
    grad_small[0:4, :] = jnp.zeros((4, WIDTH), jnp.float32)
    grad_small[12:16, :] = jnp.zeros((4, WIDTH), jnp.float32)
    grad_small[4:5, :] = jnp.sum(grad_resid, axis=0, keepdims=True)
    grad_small[5:6, :] = grad_gain
    grad_small[6:7, :] = grad_bias
    grad_small[7:8, :] = jnp.sum(grad_out, axis=0, keepdims=True)
    pairs = (
        (grad_small, small_hbm), (out_own, out_own_hbm), (out_away, out_away_hbm),
    )
    stores = fetch(pairs, done.at[pl.ds(5, 3)])
    grad_attended = f32(bfloat(dot(grad_resid_b, w_proj[...], NN)))
    for pair in range(4):
        columns = slice(pair * 128, pair * 128 + 128)
        for group in range(2):
            first = group * HALF
            halves = grad_attended[first : first + 64, columns], grad_attended[
                first + 64 : first + 128, columns
            ]
            for offset, block in enumerate(pair_pack(*halves)):
                send[group * 8 + pair * 2 + offset] = bfloat(block)
    for tile in range(HIDDEN // TILE):
        owners = pl.ds(tile * 4, 4)
        pltpu.make_async_copy(
            grads.at[:, :, owners, 0:128, :], grads_out.at[:, :, owners, 0:128, :], done.at[tile]
        ).wait()
    tail.wait()
    for copy in stores:
        copy.wait()


def last_kernel(
    scalars, pieces, tokens_in, rows_in, weights, small_in, grad_resid, part_in,
    grad_in_own_hbm, grad_in_away_hbm, grads_own, grads_away,
    grad_in_own, grad_in_away, tokens, rows_other, small, part_small, grads, done,
):
    pairs = (
        (tokens_in, tokens), (rows_in, rows_other), (small_in, small), (part_in, part_small)
    )
    copies = fetch(pairs, done)
    core = scalars[0]
    slots = (core, 1 - core)
    for copy in copies:
        copy.wait()
    unit, scale = normed(f32(mixed_rows(core, tokens, rows_other[0])))
    hidden = bfloat(unit * small[0:1, :] + small[1:2, :])
    grad_hidden = jnp.zeros((ROWS, WIDTH), jnp.float32)
    parts_all = []
    sums_query = []
    sums_value = []

    def store(weight_grad, first_rows):
        for index in range(8):
            owner, row = divmod(first_rows[index // 4] + index % 4 * 16, 96)
            for lanes in range(4):
                place = slice(lanes * 48 + row % 48, lanes * 48 + row % 48 + 16)
                grads[slots[row // 48], owner, place, :] = weight_grad[
                    index * 16 : index * 16 + 16, lanes * 128 : lanes * 128 + 128
                ]

    for pair in range(4):
        parts = []
        for group in range(2):
            head = group * 8 + pair * 2
            blocks = (f32(pieces[head + offset, HALF : HALF + 64, :]) for offset in range(2))
            parts += pair_pack(*blocks)
        grad_query = jnp.concatenate(parts, axis=0)
        sums_query.append(jnp.sum(grad_query, axis=0, keepdims=True))
        grad_query = bfloat(grad_query)
        rows = slice(pair * 128, pair * 128 + 128)
        store(bfloat(dot(grad_query, hidden, TN)), (pair * 128, pair * 128 + HEAD_DIM))
        parts_all.append((grad_query, rows))
    for head in range(HEADS):
        both = jnp.concatenate([pieces[head, 0:HALF, :], pieces[8 + head, 0:HALF, :]], axis=0)
        sums_value.append(jnp.sum(f32(both), axis=0, keepdims=True))
        rows = slice(512 + head * 128, 512 + head * 128 + 128)
        first = 512 + head * HEAD_DIM
        store(bfloat(dot(both, hidden, TN)), (first, first + 512))
        parts_all.append((both, rows))
    for part, rows in parts_all:
        grad_hidden = grad_hidden + dot(part, weights[rows, :], NN)
    grad_norm, grad_gain, grad_bias = norm_back(unit, scale, small[0:1, :], grad_hidden)
    grad_in = bfloat(grad_resid[...] + grad_norm)
    grad_in_own[...] = jnp.where(core == 0, grad_in[0:HALF], grad_in[HALF:ROWS])
    grad_in_away[...] = jnp.where(core == 0, grad_in[HALF:ROWS], grad_in[0:HALF])
    pairs = ((grad_in_own, grad_in_own_hbm), (grad_in_away, grad_in_away_hbm))
    stores = fetch(pairs, done.at[pl.ds(4, 2)])
    row = lax.broadcasted_iota(jnp.int32, (16, 128), 0)
    lane = lax.broadcasted_iota(jnp.int32, (16, 128), 1)
    for block in range(4):
        columns = slice(block * 128, block * 128 + 128)
        first = pltpu.roll(jnp.broadcast_to(sums_value[2 * block], (16, 128)), HEAD_DIM, 1)
        second = jnp.broadcast_to(sums_value[2 * block + 1], (16, 128))
        value_row = jnp.where(lane < HEAD_DIM, first, second)
        total = part_small[:, columns]
        total = jnp.where(row == 0, grad_gain[:, columns], total)
        total = jnp.where(row == 1, grad_bias[:, columns], total)
        total = jnp.where(row == 2, sums_query[block], total)
        total = jnp.where(row == 3, value_row, total)
        for inside in range(4):
            owner = block * 4 + inside
            moved = pltpu.roll(total, 128 - inside * 32, 1) if inside else total
            grads[slots[0], owner, 192:208, :] = bfloat(moved)
            grads[slots[1], owner, 192:208, :] = jnp.zeros((16, 128), jnp.bfloat16)
    for owner in range(16):
        grads_own[owner] = grads[0, owner]
        grads_away[owner] = grads[1, owner]
    for copy in stores:
        copy.wait()


def combine_kernel(late_own, late_other, early_in, early_other, sums, early, done):
    copy = pltpu.make_async_copy(early_in.at[0], early, done)
    copy.start()
    for owner in range(16):
        sums[owner, 0:EARLY, :] = bfloat(f32(late_own[owner]) + f32(late_other[owner]))
    copy.wait()
    for owner in range(16):
        sums[owner, EARLY:BLOCK, :] = bfloat(f32(early[owner]) + f32(early_other[owner]))


def reduce_kernel(pieces, sums):
    total = bfloat(sum(f32(pieces[owner]) for owner in range(16)))
    for group in range(4):
        sums[group] = total


def adam_update(weight, grad_sum, mean_old, square_old, step_rate, decay_on):
    mean_new = beta_first * mean_old + (1.0 - beta_first) * grad_sum
    square_new = beta_second * square_old + (1.0 - beta_second) * grad_sum * grad_sum
    mean_hat = mean_new / (1.0 - beta_first**STEP)
    square_hat = square_new / (1.0 - beta_second**STEP)
    weight_new = weight - step_rate * (
        mean_hat / (jnp.sqrt(square_hat) + adam_epsilon) + decay_on * weight_decay * weight
    )
    return (weight_new, mean_new, square_new)


rates = ((0.04, 1.0), (1.0, 1.0), (0.04, 1.0), (0.02, 1.0), (2.0, 0.0))


def adam_kernel(scalars, grads_own, grads_other, *refs):
    core = scalars[0]
    for index in range(2):
        own, other = refs[15 + 2 * index], refs[16 + 2 * index]
        whole = refs[19 + index]
        whole[pl.ds(pl.multiple_of(core * HALF, HALF), HALF), :] = own[...]
        whole[pl.ds(pl.multiple_of((1 - core) * HALF, HALF), HALF), :] = other[...]
    first_core = scalars[0] == 0
    olds, news = refs[:15], refs[21:36]

    def picked(half, rows, part=None):
        own, other = (
            jnp.concatenate([f32(ref[lanes, rows, :]) for lanes in range(4)], axis=1)
            if part is None
            else sum(f32(ref[group, part * 48 + rows.start : part * 48 + rows.stop, :]) for group in range(4))
            for ref in (grads_own, grads_other)
        )
        return jnp.where(first_core, own, other) if half == 0 else jnp.where(first_core, other, own)

    def late(half, rows):
        return jnp.concatenate([picked(half, rows, part) for part in range(4)], axis=1)

    grad_qkv = jnp.concatenate([late(0, slice(0, 48)), late(1, slice(0, 48))], axis=0)
    grad_small = picked(0, slice(192, 208), 0)[0:12, 0:32]
    grad_up = picked(0, slice(208, 336)).T
    grad_down = picked(1, slice(208, 336))
    grad_proj = jnp.concatenate([picked(0, slice(336, 352)), picked(1, slice(336, 352))], axis=0)
    for index, grad in enumerate((grad_qkv, grad_proj, grad_up, grad_down, grad_small)):
        results = adam_update(
            olds[index][...], grad, olds[5 + index][...], olds[10 + index][...], *rates[index]
        )
        for group, result in enumerate(results):
            news[group * 5 + index][...] = result


def call(
    kernel, shapes, scratch=(), scalars=1, hbm_in=(), hbm_out=(), flops=0, moved=0, vmem_mib=20
):
    vmem = pl.BlockSpec(memory_space=pltpu.VMEM)
    hbm = pl.BlockSpec(memory_space=pltpu.HBM)
    smem = pl.BlockSpec(memory_space=pltpu.SMEM)

    def run(*args):
        specs = [
            smem if index < scalars else hbm if index in hbm_in else vmem
            for index in range(len(args))
        ]
        args = [
            pltpu.with_memory_space_constraint(arg, pltpu.HBM) if index in hbm_in else arg
            for index, arg in enumerate(args)
        ]
        return pl.pallas_call(
            kernel,
            out_shape=[
                pltpu.HBM(shape, kind) if index in hbm_out else jax.ShapeDtypeStruct(shape, kind)
                for index, (shape, kind) in enumerate(shapes)
            ],
            in_specs=specs,
            out_specs=[hbm if index in hbm_out else vmem for index in range(len(shapes))],
            scratch_shapes=list(scratch),
            compiler_params=pltpu.CompilerParams(vmem_limit_bytes=vmem_mib * 1024 * 1024),
            cost_estimate=pl.CostEstimate(flops=flops, bytes_accessed=moved, transcendentals=0),
        )(*args)

    return run


def exchange(values):
    return lax.all_to_all(values, CTX, 0, 0, tiled=True)


def swap_cores(values):
    return lax.ppermute(values, "c", [(0, 1), (1, 0)])


def on_device(
    tokens, cotangent, lengths,
    w_qkv, w_proj, w_up, w_down, w_small,
    mean_qkv, mean_proj, mean_up, mean_down, mean_small,
    square_qkv, square_proj, square_up, square_down, square_small,
):
    kind = jnp.bfloat16
    core = lax.axis_index("c")
    place = lax.axis_index("z") * 4 + lax.axis_index("y")
    scalars = jnp.stack([core, lax.axis_index("x"), place]).astype(jnp.int32)
    lens_other = swap_cores(lengths)
    turned_olds = (
        w_qkv.T, w_proj.T, w_up, w_down, w_small,
        mean_qkv.T, mean_proj.T, mean_up, mean_down, mean_small,
        square_qkv.T, square_proj.T, square_up, square_down, square_small,
    )
    single = jnp.float32
    rows_kind = pltpu.VMEM((ROWS, WIDTH), kind)
    pair_kind = pltpu.VMEM((2, HALF, WIDTH), kind)
    small_kind = pltpu.VMEM((16, WIDTH), single)

    send, rows_away = call(
        gather_kernel,
        [((16, BLOCK, 128), kind), ((2, HALF, WIDTH), kind)],
        [
            pair_kind,
            pltpu.VMEM((48, WIDTH), single),
            pltpu.VMEM((16, 128), single),
            pltpu.VMEM((128, 128), single),
            pltpu.VMEM((128, 128), single),
            pltpu.VMEM((12, 32), single),
            pltpu.VMEM((BLOCK, 128), kind),
            pltpu.VMEM((16, 128), single),
            pltpu.SemaphoreType.DMA((7,)),
        ],
        hbm_in=range(1, 8), moved=3 << 20,
    )(scalars, tokens, cotangent, *turned_olds[0:5])
    rows_other = swap_cores(rows_away)
    first_own = exchange(send)
    first_other = swap_cores(first_own[:, 0:EARLY])
    later_own = lax.all_gather(first_own[:, EARLY:BLOCK], "x", axis=0, tiled=False)
    first_other, lens_other = lax.optimization_barrier((first_other, lens_other))

    send, weights, small = call(
        qkv_kernel,
        [((16, 192, 128), kind), ((1536, WIDTH), kind), ((16, WIDTH), single)],
        [
            rows_kind, small_kind,
            pltpu.SemaphoreType.DMA((1,)), pltpu.SemaphoreType.DMA((1,)),
        ],
        hbm_in=(1,), hbm_out=(2,), flops=2 * 256 * 512 * 1536, moved=6 << 20,
    )(scalars, tokens, rows_other, first_own, first_other)
    pieces = exchange(send)
    kept = [
        ((4096, 128), kind), ((4096, 128), kind), ((128, 4096), kind),
        ((8, HEAD_DIM, ROWS), single), ((8, 8, ROWS), single),
    ]
    kept_scratch = [pltpu.VMEM(*item) for item in kept]
    send, *kept_values = call(
        attend_kernel,
        [((16, 64, 128), kind)] + kept,
        kept_scratch
        + [
            pltpu.VMEM((128, 4096), kind), pltpu.VMEM((CHUNK, ROWS), single),
            pltpu.SemaphoreType.DMA((5,)),
        ],
        scalars=3, hbm_out=(1, 2, 3, 4, 5), vmem_mib=28, flops=36 * 512 * 256 * 2 * 256 * 2, moved=4 << 20,
    )(scalars, lengths, lens_other, pieces, swap_cores(pieces))
    send, later_own = lax.optimization_barrier((send, later_own))
    later_other = swap_cores(later_own)
    attended = exchange(send)
    out_own, out_away, send, grad_resid, part_small, early = call(
        middle_kernel,
        [
            ((HALF, WIDTH), kind),
            ((HALF, WIDTH), kind),
            ((16, 64, 128), kind),
            ((ROWS, WIDTH), single),
            ((16, WIDTH), single),
            ((4, 2, 16, 144, 128), kind),
        ],
        [
            pltpu.VMEM((WIDTH, WIDTH), kind),
            pltpu.VMEM((4, 2, 16, 144, 128), kind),
            pltpu.VMEM((HALF, WIDTH), kind), pltpu.VMEM((HALF, WIDTH), kind),
            rows_kind, rows_kind, pair_kind,
            pltpu.VMEM((4, 16, 144, 128), kind),
            small_kind,
            small_kind,
            pltpu.SemaphoreType.DMA((8,)),
            pltpu.SemaphoreType.DMA((6,)),
        ],
        scalars=3, hbm_in=(4, 5, 6, 7, 9), hbm_out=(0, 1, 4, 5),
        flops=2 * 256 * 512 * (3 * 512 + 6 * 2048), moved=12 << 20, vmem_mib=32,
    )(
        scalars, lengths, lens_other, attended, tokens, cotangent, rows_other,
        later_own, later_other, small,
    )
    early = lax.psum_scatter(
        early.reshape(4 * 2 * 16 * 144, 128), "x", scatter_dimension=0, tiled=True
    ).reshape(2, 16, 144, 128)
    grads = exchange(send)
    send, send_core = call(
        attend_back_kernel,
        [((16, 192, 128), kind), ((16, HALF, 128), kind)],
        kept_scratch
        + [
            pltpu.VMEM((4096, 128), single), pltpu.VMEM((CHUNK, ROWS), single),
            pltpu.SemaphoreType.DMA((4, 3)), pltpu.SemaphoreType.DMA((2,)),
        ],
        scalars=3, hbm_in=(4, 5, 6, 7, 8), vmem_mib=32, flops=36 * 512 * 256 * 2 * 256 * 5, moved=5 << 20,
    )(scalars, lengths, lens_other, pieces, *kept_values, grads)
    whole = f32(send[:, 0:HALF]) + f32(swap_cores(send_core))
    pieces = exchange(jnp.concatenate([bfloat(whole), send[:, HALF:]], axis=1))
    grad_in_own, grad_in_away, late_own, late_away = call(
        last_kernel,
        [((HALF, WIDTH), kind), ((HALF, WIDTH), kind)] + [((16, EARLY, 128), kind)] * 2,
        [
            pltpu.VMEM((HALF, WIDTH), kind), pltpu.VMEM((HALF, WIDTH), kind),
            rows_kind, pair_kind, small_kind, small_kind,
            pltpu.VMEM((2, 16, EARLY, 128), kind), pltpu.SemaphoreType.DMA((6,)),
        ],
        hbm_in=(2, 3, 5, 7), hbm_out=(0, 1), flops=4 * 256 * 512 * 1536, moved=8 << 20,
    )(scalars, pieces, tokens, rows_other, weights, small, grad_resid, part_small)

    late_other, out_other, grad_in_other = lax.optimization_barrier(
        (swap_cores(late_away), swap_cores(out_away), swap_cores(grad_in_away))
    )
    (sums,) = call(
        combine_kernel, [((16, BLOCK, 128), kind)],
        [pltpu.VMEM((16, 144, 128), kind), pltpu.SemaphoreType.DMA],
        scalars=0, hbm_in=(2,), moved=4 << 20,
    )(
        late_own, late_other, early, swap_cores(early[1])
    )
    (sums,) = call(reduce_kernel, [((4, BLOCK, 128), kind)], scalars=0, moved=2 << 20)(
        exchange(sums)
    )
    grads_own = lax.all_to_all(sums, "x", 0, 0, tiled=True)
    out, grad_in, *news = call(
        adam_kernel,
        [((ROWS, WIDTH), kind)] * 2 + [(old.shape, single) for old in turned_olds],
        moved=8 << 20,
    )(
        scalars, grads_own, swap_cores(grads_own), *turned_olds,
        out_own, out_other, grad_in_own, grad_in_other,
    )
    news = [new.T if index % 5 < 2 else new for index, new in enumerate(news)]
    return (out, grad_in, *news)


def solution(mesh):
    fine = Mesh(mesh.devices.reshape(4, 2, 4, 4), ("x", "c", "z", "y"))
    rows = P(("x", "c", "z", "y"), None)
    columns = P(None, CTX)
    shards = (columns, columns, columns, P(CTX, None), columns)
    return jax.shard_map(
        on_device,
        mesh=fine,
        in_specs=(rows, rows, P(("x", "c"), None)) + shards * 3,
        out_specs=(rows, rows) + shards * 3,
        check_vma=False,
    )
```

```python
import functools
import jax
import jax.numpy as jnp
from jax import lax
from jax.experimental import pallas as pl
from jax.experimental.pallas import tpu as pltpu
from jax.sharding import Mesh, PartitionSpec as P

HEADS = 8
HEAD_DIM = 64
STEP = 10
WIDTH = 512
HIDDEN = 2048
ROWS = 256
HALF = 128
CHUNK = 512
TILE = 512
WIDE = 1024
EARLY = 208
BLOCK = 352

epsilon = 1e-05
negative_big = -1e30
beta_first = 0.9
beta_second = 0.95
adam_epsilon = 1e-08
weight_decay = 0.1
gelu_scale = 0.7978845608028654
gelu_cubic = 0.044715
log2_e = 1.4426950408889634

NN = (((1,), (0,)), ((), ()))
NT = (((1,), (1,)), ((), ()))
TN = (((0,), (0,)), ((), ()))
CTX = ("z", "y")


def dot(left, right, dims):
    return lax.dot_general(left, right, dims, preferred_element_type=jnp.float32)


def bfloat(values):
    return values.astype(jnp.bfloat16)


def f32(values):
    return values.astype(jnp.float32)


def normed(values):
    center = values - jnp.mean(values, axis=-1, keepdims=True)
    spread = jnp.mean(center * center, axis=-1, keepdims=True)
    scale = lax.rsqrt(spread + epsilon)
    return center * scale, scale


def norm_back(unit, scale, gain, grad):
    scaled = grad * gain
    first = jnp.mean(scaled, axis=-1, keepdims=True)
    second = jnp.mean(scaled * unit, axis=-1, keepdims=True)
    grad_values = (scaled - first - unit * second) * scale
    grad_gain = jnp.sum(grad * unit, axis=0, keepdims=True)
    grad_bias = jnp.sum(grad, axis=0, keepdims=True)
    return grad_values, grad_gain, grad_bias


def low_lanes(shape):
    return lax.broadcasted_iota(jnp.int32, shape, 1) < HEAD_DIM


def fetch(pairs, done):
    copies = [
        pltpu.make_async_copy(source, target, done.at[index])
        for index, (source, target) in enumerate(pairs)
    ]
    for copy in copies:
        copy.start()
    return copies


def mixed_rows(core, own, other):
    keep = own[pl.ds(pl.multiple_of(core * HALF, HALF), HALF), :]
    first = jnp.where(core == 0, keep, other)
    second = jnp.where(core == 0, other, keep)
    return jnp.concatenate([first, second], axis=0)


def pair_pack(top, bottom):
    low = low_lanes(top.shape)
    first = jnp.where(low, top, pltpu.roll(bottom, HEAD_DIM, 1))
    second = jnp.where(low, pltpu.roll(top, HEAD_DIM, 1), bottom)
    return first, second


def gather_kernel(
    scalars, tokens_in, cotangent_in, qkv_in, proj_in, up_in, down_in, small_in, send, rows_out,
    rows, qkv, proj, up, down, small, block, small_block, done,
):
    core = scalars[0]
    lanes = pl.ds(pl.multiple_of(scalars[1] * 128, 128), 128)
    away = pl.ds(pl.multiple_of((1 - core) * HALF, HALF), HALF)
    pairs = (
        (qkv_in.at[pl.ds(pl.multiple_of(core * 48, 16), 48)], qkv),
        (up_in.at[lanes], up),
        (down_in.at[:, lanes], down),
        (proj_in.at[pl.ds(pl.multiple_of(core * 16, 16), 16), lanes], proj),
        (small_in, small),
        (tokens_in.at[away], rows.at[0]), (cotangent_in.at[away], rows.at[1]),
    )
    for copy in fetch(pairs, done):
        copy.wait()
    first_core = core == 0
    rows_out[...] = rows[...]
    small_block[...] = jnp.zeros((16, 128), jnp.float32)
    small_block[0:12, 0:32] = small[...]
    for part in range(4):
        columns = slice(part * 128, part * 128 + 128)
        block[part * 48 : part * 48 + 48, :] = bfloat(qkv[:, columns])
    block[192:208, :] = bfloat(small_block[...])
    half = jnp.where(first_core, up[...].T, down[...])
    block[208:336, :] = bfloat(half)
    block[336:352, :] = bfloat(proj[...])
    for owner in range(16):
        send[owner] = block[...]


def qkv_kernel(
    scalars, tokens_in, rows_other, wide_own, wide_other, send, weights, small_out,
    tokens, small, done, stored,
):
    copies = fetch(((tokens_in, tokens),), done)
    first_core = scalars[0] == 0

    def wide(half, owner, part, first):
        rows = slice(part * 48 + first, part * 48 + first + 16)
        own, other = wide_own[owner, rows, :], wide_other[owner, rows, :]
        return jnp.where(first_core, own, other) if half == 0 else jnp.where(first_core, other, own)

    for owner in range(16):
        for piece in range(6):
            first = owner * 96 + piece * 16
            part, offset = divmod(first, 512)
            if part == 0:
                target = first
            else:
                head, inside = divmod(offset, HEAD_DIM)
                target = 512 + head * 128 + (part - 1) * HEAD_DIM + inside
            half, row = divmod(piece * 16, 48)
            for lanes in range(4):
                weights[target : target + 16, lanes * 128 : lanes * 128 + 128] = wide(
                    half, owner, lanes, row
                )
    lane = lax.broadcasted_iota(jnp.int32, (16, 128), 1)
    for block in range(4):
        total = jnp.zeros((16, 128), jnp.float32)
        for inside in range(4):
            piece = f32(wide_own[block * 4 + inside, 192:208, :])
            moved = pltpu.roll(piece, inside * 32, 1) if inside else piece
            keep = (lane >= inside * 32) & (lane < inside * 32 + 32)
            total = jnp.where(keep, moved, total)
        small[:, block * 128 : block * 128 + 128] = total
    stores = fetch(((small, small_out),), stored)
    for copy in copies:
        copy.wait()
    unit, _ = normed(f32(mixed_rows(scalars[0], tokens, rows_other[0])))
    hidden = bfloat(unit * small[0:1, :] + small[1:2, :])
    for pair in range(4):
        columns = slice(pair * 128, pair * 128 + 128)
        query = dot(hidden, weights[columns, :], NT) + small[2:3, columns]
        query = f32(bfloat(query)) * HEAD_DIM**-0.5
        for group in range(2):
            rows = group * HALF
            blocks = pair_pack(query[rows : rows + 64], query[rows + 64 : rows + 128])
            for offset, block in enumerate(blocks):
                send[group * 8 + pair * 2 + offset, HALF : HALF + 64, :] = bfloat(block)
    for head in range(HEADS):
        rows = slice(512 + head * 128, 512 + head * 128 + 128)
        bias = small[3:4, (head // 2) * 128 : (head // 2) * 128 + 128]
        if head % 2 == 0:
            bias = pltpu.roll(jnp.broadcast_to(bias, (8, 128)), HEAD_DIM, 1)[0:1]
        bias = jnp.where(low_lanes((1, 128)), 0.0, bias)
        both = bfloat(dot(hidden, weights[rows, :], NT) + bias)
        send[head, 0:HALF, :] = both[0:HALF]
        send[8 + head, 0:HALF, :] = both[HALF:ROWS]
    for copy in stores:
        copy.wait()


def query_rows(core):
    lane = lax.broadcasted_iota(jnp.int32, (1, ROWS), 1)
    return ((lane & 64) << 2) + core * HALF + (lane & 63) + ((lane & 128) >> 1)


def doc_of(position, first_end, second_end):
    return (position >= first_end).astype(jnp.int32) + (position >= second_end).astype(jnp.int32)


def doc_start(position, first_end, second_end):
    return jnp.where(
        position >= second_end, second_end, jnp.where(position >= first_end, first_end, 0)
    )


def packed_t(block):
    turned = block.T
    return jnp.concatenate([turned[0:HEAD_DIM], turned[HEAD_DIM:128]], axis=1)


def causal_bias(bias, core):
    key = lax.broadcasted_iota(jnp.int32, (CHUNK, ROWS), 0)
    bias[...] = jnp.where(key <= query_rows(core), 0.0, negative_big)


def keyed_rows(rows, first, first_end, second_end):
    lane = lax.broadcasted_iota(jnp.int32, (ROWS, 128), 1)
    row = lax.broadcasted_iota(jnp.int32, (ROWS, 128), 0) + first
    mark = lane - HEAD_DIM == doc_of(row, first_end, second_end)
    return bfloat(jnp.where(lane < HEAD_DIM, rows, jnp.where(mark, 1.0, 0.0)))


def keyed_queries(query_t, step, core, first_end, second_end):
    position = query_rows(core) + step * CHUNK
    line = lax.broadcasted_iota(jnp.int32, (HEAD_DIM, ROWS), 0)
    other = (line < 3) & (line != doc_of(position, first_end, second_end))
    penalty = jnp.where(other, negative_big, 0.0)
    return bfloat(jnp.concatenate([query_t, penalty], axis=0))


def packed_block(pieces, step):
    return jnp.concatenate(
        [f32(pieces[2 * step, HALF : HALF + 64, :]), f32(pieces[2 * step + 1, HALF : HALF + 64, :])],
        axis=0,
    )


def doc_ends(scalars, lens_own, lens_other, group):
    own = scalars[0] == group
    first = jnp.where(own, lens_own[0, 0], lens_other[0, 0])
    return first, first + jnp.where(own, lens_own[0, 1], lens_other[0, 1])


def attend_kernel(
    scalars, lens_own, lens_other, pieces, others,
    send, keyed_hbm, keys_hbm, turned_hbm, out_hbm, stats_hbm,
    keyed, keys_out, turned_out, out_t, stats, ones_t, bias, done,
):
    core = scalars[0]
    first_end, second_end = doc_ends(scalars, lens_own, lens_other, scalars[2] // HEADS)
    causal_bias(bias, core)

    def turn(source, _):
        columns = pl.ds(pl.multiple_of(source * ROWS, ROWS), ROWS)
        own, other = pieces[source, 0:HALF, :], others[source, 0:HALF, :]
        first, second = jnp.where(core == 0, own, other), jnp.where(core == 0, other, own)
        keys = jnp.concatenate([first, second], axis=0)
        keys_out[columns, :] = keys
        keys = f32(keys)
        keyed[columns, :] = keyed_rows(keys, source * ROWS, first_end, second_end)
        turned = keys.T
        turned_out[:, columns] = bfloat(turned)
        row = lax.broadcasted_iota(jnp.int32, (128, ROWS), 0)
        ones_t[:, columns] = bfloat(jnp.where(row < HEAD_DIM, 1.0, turned))
        return 0

    lax.fori_loop(0, 16, turn, 0, unroll=4)
    stores = fetch(((keyed, keyed_hbm), (keys_out, keys_hbm), (turned_out, turned_hbm)), done)

    def one_pair(pair, _):
        step = 2 * pair
        queries = tuple(
            keyed_queries(
                packed_t(packed_block(pieces, step + index)), step + index, core, first_end, second_end
            )
            for index in range(2)
        )

        def advance(scores, values, state):
            run_max, total = state
            new_max = jnp.maximum(run_max, jnp.max(scores, axis=0, keepdims=True))
            weights = bfloat(jnp.exp2((scores - new_max) * log2_e))
            scale = jnp.exp2((run_max - new_max) * log2_e)
            return new_max, total * scale + dot(values, weights, NN)

        def body(wide, state):
            rows = pl.ds(pl.multiple_of(wide * WIDE, WIDE), WIDE)
            keys, values = keyed[rows, :], ones_t[:, rows]
            scores = [dot(keys, query, NN) for query in queries]
            return tuple(advance(scores[index], values, state[index]) for index in range(2))

        start = (
            jnp.full((1, ROWS), negative_big, jnp.float32),
            jnp.zeros((128, ROWS), jnp.float32),
        )
        low = doc_start(step * CHUNK, first_end, second_end) // WIDE
        first, second = lax.fori_loop(low, pair, body, (start, start))
        rows = pl.ds(pl.multiple_of(pair * WIDE, WIDE), WIDE)
        keys, values = keyed[rows, :], ones_t[:, rows]
        scores = dot(keys, queries[1], NN)
        scores = jnp.concatenate([scores[0:CHUNK], scores[CHUNK:WIDE] + bias[...]], axis=0)
        first = advance(dot(keys[0:CHUNK], queries[0], NN) + bias[...], values[:, 0:CHUNK], first)
        second = advance(scores, values, second)
        for index, (run_max, total) in enumerate((first, second)):
            row_sum = total[0:1]
            result = total[HEAD_DIM:128] / row_sum
            out_t[step + index] = result
            stats[step + index] = jnp.broadcast_to(run_max + jnp.log(row_sum), (8, ROWS))
            packed = jnp.concatenate([result[:, 0:128], result[:, 128:256]], axis=0).T
            send[2 * (step + index)] = bfloat(packed[0:64])
            send[2 * (step + index) + 1] = bfloat(packed[64:128])
        return 0

    lax.fori_loop(0, 4, one_pair, 0)
    stores += fetch(((out_t, out_hbm), (stats, stats_hbm)), done.at[pl.ds(3, 2)])
    for copy in stores:
        copy.wait()


def attend_back_kernel(
    scalars, lens_own, lens_other, pieces, keyed_hbm, keys_hbm, turned_hbm, out_hbm, stats_hbm, grads,
    send, send_core, keyed, key_rows, turned, out_t, stats, total, bias, done, done_small,
):
    small_copies = fetch(((out_hbm, out_t), (stats_hbm, stats)), done_small)

    def wide_copies(pair):
        rows = pl.ds(pl.multiple_of(pair * WIDE, WIDE), WIDE)
        places = (
            (keyed_hbm.at[rows, :], keyed.at[rows, :]),
            (keys_hbm.at[rows, :], key_rows.at[rows, :]),
            (turned_hbm.at[:, rows], turned.at[:, rows]),
        )
        return [
            pltpu.make_async_copy(source, target, done.at[pair, index])
            for index, (source, target) in enumerate(places)
        ]

    for pair in range(4):
        for copy in wide_copies(pair):
            copy.start()
    core = scalars[0]
    first_end, second_end = doc_ends(scalars, lens_own, lens_other, scalars[2] // HEADS)
    causal_bias(bias, core)

    def clear(source, _):
        rows = pl.ds(pl.multiple_of(source * ROWS, ROWS), ROWS)
        total[rows, :] = jnp.zeros((ROWS, 128), jnp.float32)
        return 0

    lax.fori_loop(0, 16, clear, 0)
    for copy in small_copies:
        copy.wait()
    low_half = low_lanes((128, 128))

    def load_block(step):
        query = packed_block(pieces, step)
        query_t = keyed_queries(packed_t(query), step, core, first_end, second_end)
        top = jnp.where(low_half, query, 0.0)
        bottom = jnp.where(low_half, pltpu.roll(query, HEAD_DIM, 1), 0.0)
        query = bfloat(jnp.concatenate([top, bottom], axis=0))
        grad = jnp.concatenate([f32(grads[2 * step]), f32(grads[2 * step + 1])], axis=0)
        grad_t = packed_t(grad)
        dots = jnp.sum(grad_t * out_t[step], axis=0, keepdims=True)
        grad_t = bfloat(jnp.concatenate([jnp.zeros_like(grad_t), grad_t], axis=0))
        top = jnp.where(low_half, 0.0, pltpu.roll(grad, HEAD_DIM, 1))
        bottom = jnp.where(low_half, 0.0, grad)
        grad = bfloat(jnp.concatenate([top, bottom], axis=0))
        return query_t, grad_t, query, grad, dots, stats[step][0:1]

    def one_pair(pair, _):
        step = 2 * pair
        for copy in wide_copies(pair):
            copy.wait()
        loaded = tuple(load_block(step + index) for index in range(2))

        def score_grads(index, scores, grad_weights):
            weights = jnp.exp2((scores - loaded[index][5]) * log2_e)
            return bfloat(weights * (grad_weights - loaded[index][4])), bfloat(weights)

        both = jnp.concatenate([loaded[0][2], loaded[0][3], loaded[1][2], loaded[1][3]], axis=0)

        def body(wide, state):
            rows = pl.ds(pl.multiple_of(wide * WIDE, WIDE), WIDE)
            marked, keys, keys_t = keyed[rows, :], key_rows[rows, :], turned[:, rows]
            scores = [dot(marked, item[0], NN) for item in loaded]
            grad_weights = [dot(keys, item[1], NN) for item in loaded]
            parts = [score_grads(index, scores[index], grad_weights[index]) for index in range(2)]
            total[rows, :] += dot(jnp.concatenate(parts[0] + parts[1], axis=1), both, NN)
            return tuple(state[index] + dot(keys_t, parts[index][0], NN) for index in range(2))

        start = jnp.zeros((128, ROWS), jnp.float32)
        low = doc_start(step * CHUNK, first_end, second_end) // WIDE
        first, second = lax.fori_loop(low, pair, body, (start, start))
        rows = pl.ds(pl.multiple_of(pair * WIDE, WIDE), CHUNK)
        rows_next = pl.ds(pl.multiple_of(pair * WIDE + CHUNK, CHUNK), CHUNK)
        marked, keys, keys_t = keyed[rows, :], key_rows[rows, :], turned[:, rows]
        marked_next, keys_next = keyed[rows_next, :], key_rows[rows_next, :]
        parts = (
            score_grads(
                0, dot(marked, loaded[0][0], NN) + bias[...], dot(keys, loaded[0][1], NN)
            ),
            score_grads(1, dot(marked, loaded[1][0], NN), dot(keys, loaded[1][1], NN)),
            score_grads(
                1, dot(marked_next, loaded[1][0], NN) + bias[...], dot(keys_next, loaded[1][1], NN)
            ),
        )
        total[rows, :] += dot(jnp.concatenate(parts[0] + parts[1], axis=1), both, NN)
        total[rows_next, :] += dot(jnp.concatenate(parts[2], axis=1), both[2 * ROWS : 4 * ROWS], NN)
        first = first + dot(keys_t, parts[0][0], NN)
        second = second + dot(keys_t, parts[1][0], NN)
        second = second + dot(turned[:, rows_next], parts[2][0], NN)
        for index, grad_query_t in enumerate((first, second)):
            turn = grad_query_t[0:HEAD_DIM] * HEAD_DIM**-0.5
            packed = jnp.concatenate([turn[:, 0:128], turn[:, 128:256]], axis=0).T
            send[2 * (step + index), HALF : HALF + 64, :] = bfloat(packed[0:64])
            send[2 * (step + index) + 1, HALF : HALF + 64, :] = bfloat(packed[64:128])
        return 0

    lax.fori_loop(0, 4, one_pair, 0)

    def emit(source, _):
        mine = pl.ds(pl.multiple_of(source * ROWS + core * HALF, HALF), HALF)
        away = pl.ds(pl.multiple_of(source * ROWS + (1 - core) * HALF, HALF), HALF)
        send[source, 0:HALF, :] = bfloat(total[mine, :])
        send_core[source] = bfloat(total[away, :])
        return 0

    lax.fori_loop(0, 16, emit, 0)


def middle_kernel(
    scalars, lens_own, lens_other, attended_in, tokens_in, cotangent_in, rows_in, later_in,
    later_other, small_in,
    out_own_hbm, out_away_hbm, send, grad_resid_out, small_hbm, grads_out,
    w_proj, grads, out_own, out_away, tokens, cotangent, rows_other, later_own, small, grad_small,
    done, fetched,
):
    pairs = (
        (later_in.at[:, :, 128:144, :], later_own.at[:, :, 128:144, :]),
        (tokens_in, tokens), (rows_in, rows_other), (small_in, small), (cotangent_in, cotangent),
        (later_in.at[:, :, 0:128, :], later_own.at[:, :, 0:128, :]),
    )
    copies = fetch(pairs, fetched)
    core = scalars[0]
    first_core = core == 0
    slots = (core, 1 - core)
    for copy in copies[0:5]:
        copy.wait()
    for owner in range(16):
        for lanes in range(4):
            columns = slice(lanes * 128, lanes * 128 + 128)
            own = later_own[lanes, owner, 128:144, :]
            other = later_other[lanes, owner, 128:144, :]
            first = owner * 32
            w_proj[first : first + 16, columns] = jnp.where(first_core, own, other)
            w_proj[first + 16 : first + 32, columns] = jnp.where(first_core, other, own)
    blocks = []
    for pair in range(4):
        parts = []
        for group in range(2):
            head = group * 8 + pair * 2
            parts += pair_pack(f32(attended_in[head]), f32(attended_in[head + 1]))
        blocks.append(jnp.concatenate(parts, axis=0))
    attended = bfloat(jnp.concatenate(blocks, axis=1))
    residual = f32(mixed_rows(core, tokens, rows_other[0])) + dot(attended, w_proj[...], NT) + small[4:5, :]
    unit, scale = normed(residual)
    hidden_in = bfloat(unit * small[5:6, :] + small[6:7, :])
    row = lax.broadcasted_iota(jnp.int32, (ROWS, 1), 0)
    position = (row & (HALF - 1)) + scalars[2] * ROWS + core * HALF
    _, first_live = doc_ends(scalars, lens_own, lens_other, 0)
    _, second_live = doc_ends(scalars, lens_own, lens_other, 1)
    live = position < jnp.where(row < HALF, first_live, second_live)
    grad_out = jnp.where(live, f32(mixed_rows(core, cotangent, rows_other[1])), 0.0)
    grad_out_b = bfloat(grad_out)

    copies[5].wait()

    def one_tile(tile, state):
        branch, grad_hidden_in = state
        owners = pl.ds(tile * 4, 4)
        own, other = (
            jnp.concatenate(
                [part[lanes, owners, 0:128, :].reshape(TILE, 128) for lanes in range(4)], axis=1
            )
            for part in (later_own, later_other)
        )
        up_rows = jnp.where(first_core, own, other)
        down_rows = jnp.where(first_core, other, own)
        hidden = dot(hidden_in, up_rows, NT) + small[pl.ds(8 + tile, 1), :]
        square = hidden * hidden
        bend = jnp.tanh(gelu_scale * hidden * (1.0 + gelu_cubic * square))
        half_open = 0.5 * (1.0 + bend)
        activated = bfloat(hidden * half_open)
        slope = half_open + 0.5 * hidden * (1.0 - bend * bend) * gelu_scale * (
            1.0 + 3.0 * gelu_cubic * square
        )
        branch = branch + dot(activated, down_rows, NN)
        grad_hidden = dot(grad_out_b, down_rows, NT) * slope
        grad_hidden_b = bfloat(grad_hidden)
        grad_hidden_in = grad_hidden_in + dot(grad_hidden_b, up_rows, NN)
        grad_small[pl.ds(8 + tile, 1), :] = jnp.sum(grad_hidden, axis=0, keepdims=True)
        grad_up = bfloat(dot(grad_hidden_b, hidden_in, TN))
        grad_down = bfloat(dot(activated, grad_out_b, TN))
        for lanes in range(4):
            columns = slice(lanes * 128, lanes * 128 + 128)
            grads[lanes, slots[0], owners, 0:128, :] = grad_up[:, columns].reshape(4, 128, 128)
            grads[lanes, slots[1], owners, 0:128, :] = grad_down[:, columns].reshape(4, 128, 128)
        here = grads.at[:, :, owners, 0:128, :]
        pltpu.make_async_copy(here, grads_out.at[:, :, owners, 0:128, :], done.at[tile]).start()
        return branch, grad_hidden_in

    zeros = jnp.zeros((ROWS, WIDTH), jnp.float32)
    branch, grad_hidden_in = lax.fori_loop(0, HIDDEN // TILE, one_tile, (zeros, zeros))
    out = bfloat(residual + branch + small[7:8, :])
    out_own[...] = jnp.where(first_core, out[0:HALF], out[HALF:ROWS])
    out_away[...] = jnp.where(first_core, out[HALF:ROWS], out[0:HALF])
    grad_norm, grad_gain, grad_bias = norm_back(unit, scale, small[5:6, :], grad_hidden_in)
    grad_resid = grad_out + grad_norm
    grad_resid_out[...] = grad_resid
    grad_resid_b = bfloat(grad_resid)
    grad_proj = bfloat(dot(grad_resid_b, attended, TN)).reshape(16, 32, WIDTH)
    for lanes in range(4):
        columns = slice(lanes * 128, lanes * 128 + 128)
        grads[lanes, slots[0], :, 128:144, :] = grad_proj[:, 0:16, columns]
        grads[lanes, slots[1], :, 128:144, :] = grad_proj[:, 16:32, columns]
    tail = pltpu.make_async_copy(
        grads.at[:, :, :, 128:144, :], grads_out.at[:, :, :, 128:144, :], done.at[4]
    )
    tail.start()
    grad_small[0:4, :] = jnp.zeros((4, WIDTH), jnp.float32)
    grad_small[12:16, :] = jnp.zeros((4, WIDTH), jnp.float32)
    grad_small[4:5, :] = jnp.sum(grad_resid, axis=0, keepdims=True)
    grad_small[5:6, :] = grad_gain
    grad_small[6:7, :] = grad_bias
    grad_small[7:8, :] = jnp.sum(grad_out, axis=0, keepdims=True)
    pairs = (
        (grad_small, small_hbm), (out_own, out_own_hbm), (out_away, out_away_hbm),
    )
    stores = fetch(pairs, done.at[pl.ds(5, 3)])
    grad_attended = f32(bfloat(dot(grad_resid_b, w_proj[...], NN)))
    for pair in range(4):
        columns = slice(pair * 128, pair * 128 + 128)
        for group in range(2):
            first = group * HALF
            halves = grad_attended[first : first + 64, columns], grad_attended[
                first + 64 : first + 128, columns
            ]
            for offset, block in enumerate(pair_pack(*halves)):
                send[group * 8 + pair * 2 + offset] = bfloat(block)
    for tile in range(HIDDEN // TILE):
        owners = pl.ds(tile * 4, 4)
        pltpu.make_async_copy(
            grads.at[:, :, owners, 0:128, :], grads_out.at[:, :, owners, 0:128, :], done.at[tile]
        ).wait()
    tail.wait()
    for copy in stores:
        copy.wait()


def last_kernel(
    scalars, pieces, tokens_in, rows_in, weights, small_in, grad_resid, part_in,
    grad_in_own, grad_in_away, grads_own, grads_away,
    tokens, rows_other, small, part_small, grads, done,
):
    pairs = (
        (tokens_in, tokens), (rows_in, rows_other), (small_in, small), (part_in, part_small)
    )
    copies = fetch(pairs, done)
    core = scalars[0]
    slots = (core, 1 - core)
    for copy in copies:
        copy.wait()
    unit, scale = normed(f32(mixed_rows(core, tokens, rows_other[0])))
    hidden = bfloat(unit * small[0:1, :] + small[1:2, :])
    grad_hidden = jnp.zeros((ROWS, WIDTH), jnp.float32)
    parts_all = []
    sums_query = []
    sums_value = []

    def store(weight_grad, first_rows):
        for index in range(8):
            owner, row = divmod(first_rows[index // 4] + index % 4 * 16, 96)
            for lanes in range(4):
                place = slice(lanes * 48 + row % 48, lanes * 48 + row % 48 + 16)
                grads[slots[row // 48], owner, place, :] = weight_grad[
                    index * 16 : index * 16 + 16, lanes * 128 : lanes * 128 + 128
                ]

    for pair in range(4):
        parts = []
        for group in range(2):
            head = group * 8 + pair * 2
            blocks = (f32(pieces[head + offset, HALF : HALF + 64, :]) for offset in range(2))
            parts += pair_pack(*blocks)
        grad_query = jnp.concatenate(parts, axis=0)
        sums_query.append(jnp.sum(grad_query, axis=0, keepdims=True))
        grad_query = bfloat(grad_query)
        rows = slice(pair * 128, pair * 128 + 128)
        store(bfloat(dot(grad_query, hidden, TN)), (pair * 128, pair * 128 + HEAD_DIM))
        parts_all.append((grad_query, rows))
    for head in range(HEADS):
        both = jnp.concatenate([pieces[head, 0:HALF, :], pieces[8 + head, 0:HALF, :]], axis=0)
        sums_value.append(jnp.sum(f32(both), axis=0, keepdims=True))
        rows = slice(512 + head * 128, 512 + head * 128 + 128)
        first = 512 + head * HEAD_DIM
        store(bfloat(dot(both, hidden, TN)), (first, first + 512))
        parts_all.append((both, rows))
    for part, rows in parts_all:
        grad_hidden = grad_hidden + dot(part, weights[rows, :], NN)
    grad_norm, grad_gain, grad_bias = norm_back(unit, scale, small[0:1, :], grad_hidden)
    grad_in = bfloat(grad_resid[...] + grad_norm)
    grad_in_own[...] = jnp.where(core == 0, grad_in[0:HALF], grad_in[HALF:ROWS])
    grad_in_away[...] = jnp.where(core == 0, grad_in[HALF:ROWS], grad_in[0:HALF])
    row = lax.broadcasted_iota(jnp.int32, (16, 128), 0)
    lane = lax.broadcasted_iota(jnp.int32, (16, 128), 1)
    for block in range(4):
        columns = slice(block * 128, block * 128 + 128)
        first = pltpu.roll(jnp.broadcast_to(sums_value[2 * block], (16, 128)), HEAD_DIM, 1)
        second = jnp.broadcast_to(sums_value[2 * block + 1], (16, 128))
        value_row = jnp.where(lane < HEAD_DIM, first, second)
        total = part_small[:, columns]
        total = jnp.where(row == 0, grad_gain[:, columns], total)
        total = jnp.where(row == 1, grad_bias[:, columns], total)
        total = jnp.where(row == 2, sums_query[block], total)
        total = jnp.where(row == 3, value_row, total)
        for inside in range(4):
            owner = block * 4 + inside
            moved = pltpu.roll(total, 128 - inside * 32, 1) if inside else total
            grads[slots[0], owner, 192:208, :] = bfloat(moved)
            grads[slots[1], owner, 192:208, :] = jnp.zeros((16, 128), jnp.bfloat16)
    for owner in range(16):
        grads_own[owner] = grads[0, owner]
        grads_away[owner] = grads[1, owner]


def combine_kernel(late_own, late_other, early_in, early_other, sums, early, done):
    copy = pltpu.make_async_copy(early_in.at[0], early, done)
    copy.start()
    for owner in range(16):
        sums[owner, 0:EARLY, :] = bfloat(f32(late_own[owner]) + f32(late_other[owner]))
    copy.wait()
    for owner in range(16):
        sums[owner, EARLY:BLOCK, :] = bfloat(f32(early[owner]) + f32(early_other[owner]))


def reduce_kernel(pieces, sums):
    total = bfloat(sum(f32(pieces[owner]) for owner in range(16)))
    for group in range(4):
        sums[group] = total


def adam_update(weight, grad_sum, mean_old, square_old, step_rate, decay_on):
    mean_new = beta_first * mean_old + (1.0 - beta_first) * grad_sum
    square_new = beta_second * square_old + (1.0 - beta_second) * grad_sum * grad_sum
    mean_hat = mean_new / (1.0 - beta_first**STEP)
    square_hat = square_new / (1.0 - beta_second**STEP)
    weight_new = weight - step_rate * (
        mean_hat / (jnp.sqrt(square_hat) + adam_epsilon) + decay_on * weight_decay * weight
    )
    return (weight_new, mean_new, square_new)


rates = ((0.04, 1.0), (1.0, 1.0), (0.04, 1.0), (0.02, 1.0), (2.0, 0.0))


def adam_kernel(scalars, grads_own, grads_other, *refs):
    core = scalars[0]
    for index in range(2):
        own, other = refs[15 + 2 * index], refs[16 + 2 * index]
        whole = refs[19 + index]
        whole[pl.ds(pl.multiple_of(core * HALF, HALF), HALF), :] = own[...]
        whole[pl.ds(pl.multiple_of((1 - core) * HALF, HALF), HALF), :] = other[...]
    first_core = scalars[0] == 0
    olds, news = refs[:15], refs[21:36]

    def picked(half, rows, part=None):
        own, other = (
            jnp.concatenate([f32(ref[lanes, rows, :]) for lanes in range(4)], axis=1)
            if part is None
            else sum(f32(ref[group, part * 48 + rows.start : part * 48 + rows.stop, :]) for group in range(4))
            for ref in (grads_own, grads_other)
        )
        return jnp.where(first_core, own, other) if half == 0 else jnp.where(first_core, other, own)

    def late(half, rows):
        return jnp.concatenate([picked(half, rows, part) for part in range(4)], axis=1)

    grad_qkv = jnp.concatenate([late(0, slice(0, 48)), late(1, slice(0, 48))], axis=0)
    grad_small = picked(0, slice(192, 208), 0)[0:12, 0:32]
    grad_up = picked(0, slice(208, 336)).T
    grad_down = picked(1, slice(208, 336))
    grad_proj = jnp.concatenate([picked(0, slice(336, 352)), picked(1, slice(336, 352))], axis=0)
    for index, grad in enumerate((grad_qkv, grad_proj, grad_up, grad_down, grad_small)):
        results = adam_update(
            olds[index][...], grad, olds[5 + index][...], olds[10 + index][...], *rates[index]
        )
        for group, result in enumerate(results):
            news[group * 5 + index][...] = result


def call(
    kernel, shapes, scratch=(), scalars=1, hbm_in=(), hbm_out=(), flops=0, moved=0, vmem_mib=20
):
    vmem = pl.BlockSpec(memory_space=pltpu.VMEM)
    hbm = pl.BlockSpec(memory_space=pltpu.HBM)
    smem = pl.BlockSpec(memory_space=pltpu.SMEM)

    def run(*args):
        specs = [
            smem if index < scalars else hbm if index in hbm_in else vmem
            for index in range(len(args))
        ]
        args = [
            pltpu.with_memory_space_constraint(arg, pltpu.HBM) if index in hbm_in else arg
            for index, arg in enumerate(args)
        ]
        return pl.pallas_call(
            kernel,
            out_shape=[
                pltpu.HBM(shape, kind) if index in hbm_out else jax.ShapeDtypeStruct(shape, kind)
                for index, (shape, kind) in enumerate(shapes)
            ],
            in_specs=specs,
            out_specs=[hbm if index in hbm_out else vmem for index in range(len(shapes))],
            scratch_shapes=list(scratch),
            compiler_params=pltpu.CompilerParams(vmem_limit_bytes=vmem_mib * 1024 * 1024),
            cost_estimate=pl.CostEstimate(flops=flops, bytes_accessed=moved, transcendentals=0),
        )(*args)

    return run


def exchange(values):
    return lax.all_to_all(values, CTX, 0, 0, tiled=True)


def swap_cores(values):
    return lax.ppermute(values, "c", [(0, 1), (1, 0)])


def on_device(
    tokens, cotangent, lengths,
    w_qkv, w_proj, w_up, w_down, w_small,
    mean_qkv, mean_proj, mean_up, mean_down, mean_small,
    square_qkv, square_proj, square_up, square_down, square_small,
):
    kind = jnp.bfloat16
    core = lax.axis_index("c")
    place = lax.axis_index("z") * 4 + lax.axis_index("y")
    scalars = jnp.stack([core, lax.axis_index("x"), place]).astype(jnp.int32)
    lens_other = swap_cores(lengths)
    turned_olds = (
        w_qkv.T, w_proj.T, w_up, w_down, w_small,
        mean_qkv.T, mean_proj.T, mean_up, mean_down, mean_small,
        square_qkv.T, square_proj.T, square_up, square_down, square_small,
    )
    single = jnp.float32
    rows_kind = pltpu.VMEM((ROWS, WIDTH), kind)
    pair_kind = pltpu.VMEM((2, HALF, WIDTH), kind)
    small_kind = pltpu.VMEM((16, WIDTH), single)

    send, rows_away = call(
        gather_kernel,
        [((16, BLOCK, 128), kind), ((2, HALF, WIDTH), kind)],
        [
            pair_kind,
            pltpu.VMEM((48, WIDTH), single),
            pltpu.VMEM((16, 128), single),
            pltpu.VMEM((128, 128), single),
            pltpu.VMEM((128, 128), single),
            pltpu.VMEM((12, 32), single),
            pltpu.VMEM((BLOCK, 128), kind),
            pltpu.VMEM((16, 128), single),
            pltpu.SemaphoreType.DMA((7,)),
        ],
        hbm_in=range(1, 8), moved=3 << 20,
    )(scalars, tokens, cotangent, *turned_olds[0:5])
    rows_other = swap_cores(rows_away)
    first_own = exchange(send)
    first_other = swap_cores(first_own[:, 0:EARLY])
    later_own = lax.all_gather(first_own[:, EARLY:BLOCK], "x", axis=0, tiled=False)
    first_other, lens_other = lax.optimization_barrier((first_other, lens_other))

    send, weights, small = call(
        qkv_kernel,
        [((16, 192, 128), kind), ((1536, WIDTH), kind), ((16, WIDTH), single)],
        [
            rows_kind, small_kind,
            pltpu.SemaphoreType.DMA((1,)), pltpu.SemaphoreType.DMA((1,)),
        ],
        hbm_in=(1,), hbm_out=(2,), flops=2 * 256 * 512 * 1536, moved=6 << 20,
    )(scalars, tokens, rows_other, first_own, first_other)
    pieces = exchange(send)
    kept = [
        ((4096, 128), kind), ((4096, 128), kind), ((128, 4096), kind),
        ((8, HEAD_DIM, ROWS), single), ((8, 8, ROWS), single),
    ]
    kept_scratch = [pltpu.VMEM(*item) for item in kept]
    send, *kept_values = call(
        attend_kernel,
        [((16, 64, 128), kind)] + kept,
        kept_scratch
        + [
            pltpu.VMEM((128, 4096), kind), pltpu.VMEM((CHUNK, ROWS), single),
            pltpu.SemaphoreType.DMA((5,)),
        ],
        scalars=3, hbm_out=(1, 2, 3, 4, 5), vmem_mib=28, flops=36 * 512 * 256 * 2 * 256 * 2, moved=4 << 20,
    )(scalars, lengths, lens_other, pieces, swap_cores(pieces))
    send, later_own = lax.optimization_barrier((send, later_own))
    later_other = swap_cores(later_own)
    attended = exchange(send)
    out_own, out_away, send, grad_resid, part_small, early = call(
        middle_kernel,
        [
            ((HALF, WIDTH), kind),
            ((HALF, WIDTH), kind),
            ((16, 64, 128), kind),
            ((ROWS, WIDTH), single),
            ((16, WIDTH), single),
            ((4, 2, 16, 144, 128), kind),
        ],
        [
            pltpu.VMEM((WIDTH, WIDTH), kind),
            pltpu.VMEM((4, 2, 16, 144, 128), kind),
            pltpu.VMEM((HALF, WIDTH), kind), pltpu.VMEM((HALF, WIDTH), kind),
            rows_kind, rows_kind, pair_kind,
            pltpu.VMEM((4, 16, 144, 128), kind),
            small_kind,
            small_kind,
            pltpu.SemaphoreType.DMA((8,)),
            pltpu.SemaphoreType.DMA((6,)),
        ],
        scalars=3, hbm_in=(4, 5, 6, 7, 9), hbm_out=(0, 1, 4, 5),
        flops=2 * 256 * 512 * (3 * 512 + 6 * 2048), moved=12 << 20, vmem_mib=32,
    )(
        scalars, lengths, lens_other, attended, tokens, cotangent, rows_other,
        later_own, later_other, small,
    )
    early = lax.psum_scatter(
        early.reshape(4 * 2 * 16 * 144, 128), "x", scatter_dimension=0, tiled=True
    ).reshape(2, 16, 144, 128)
    grads = exchange(send)
    send, send_core = call(
        attend_back_kernel,
        [((16, 192, 128), kind), ((16, HALF, 128), kind)],
        kept_scratch
        + [
            pltpu.VMEM((4096, 128), single), pltpu.VMEM((CHUNK, ROWS), single),
            pltpu.SemaphoreType.DMA((4, 3)), pltpu.SemaphoreType.DMA((2,)),
        ],
        scalars=3, hbm_in=(4, 5, 6, 7, 8), vmem_mib=32, flops=36 * 512 * 256 * 2 * 256 * 5, moved=5 << 20,
    )(scalars, lengths, lens_other, pieces, *kept_values, grads)
    whole = f32(send[:, 0:HALF]) + f32(swap_cores(send_core))
    pieces = exchange(jnp.concatenate([bfloat(whole), send[:, HALF:]], axis=1))
    grad_in_own, grad_in_away, late_own, late_away = call(
        last_kernel,
        [((HALF, WIDTH), kind), ((HALF, WIDTH), kind)] + [((16, EARLY, 128), kind)] * 2,
        [
            rows_kind, pair_kind, small_kind, small_kind,
            pltpu.VMEM((2, 16, EARLY, 128), kind), pltpu.SemaphoreType.DMA((4,)),
        ],
        hbm_in=(2, 3, 5, 7), flops=4 * 256 * 512 * 1536, moved=8 << 20,
    )(scalars, pieces, tokens, rows_other, weights, small, grad_resid, part_small)

    late_other, out_other, grad_in_other = lax.optimization_barrier(
        (swap_cores(late_away), swap_cores(out_away), swap_cores(grad_in_away))
    )
    (sums,) = call(
        combine_kernel, [((16, BLOCK, 128), kind)],
        [pltpu.VMEM((16, 144, 128), kind), pltpu.SemaphoreType.DMA],
        scalars=0, hbm_in=(2,), moved=4 << 20,
    )(
        late_own, late_other, early, swap_cores(early[1])
    )
    (sums,) = call(reduce_kernel, [((4, BLOCK, 128), kind)], scalars=0, moved=2 << 20)(
        exchange(sums)
    )
    grads_own = lax.all_to_all(sums, "x", 0, 0, tiled=True)
    out, grad_in, *news = call(
        adam_kernel,
        [((ROWS, WIDTH), kind)] * 2 + [(old.shape, single) for old in turned_olds],
        moved=8 << 20,
    )(
        scalars, grads_own, swap_cores(grads_own), *turned_olds,
        out_own, out_other, grad_in_own, grad_in_other,
    )
    news = [new.T if index % 5 < 2 else new for index, new in enumerate(news)]
    return (out, grad_in, *news)


def solution(mesh):
    fine = Mesh(mesh.devices.reshape(4, 2, 4, 4), ("x", "c", "z", "y"))
    rows = P(("x", "c", "z", "y"), None)
    columns = P(None, CTX)
    shards = (columns, columns, columns, P(CTX, None), columns)
    return jax.shard_map(
        on_device,
        mesh=fine,
        in_specs=(rows, rows, P(("x", "c"), None)) + shards * 3,
        out_specs=(rows, rows) + shards * 3,
        check_vma=False,
    )
```
